32 devices in a mesh: dp: 8 (over z, x), narrow: 4 (over y, core).
Axes of the slice: x: 2, y: 2, z: 4, core: 2. Of those that a mesh axis runs over, the one named last changes fastest.
Arguments:
- inputs: bfloat16 [32768, 768], P(('dp', 'narrow')), may hold values from -6 to 6
- segments: int32 [128, 256], P('dp'), may hold values from 0 to 3, as said below
- row_kind: int32 [128, 256], P('dp'), may hold values from 0 to 1, as said below
- query_weight: bfloat16 [768, 768], P('dp', 'narrow'), may hold values from -0.21875 to 0.21875
- query_bias: bfloat16 [768], P('dp'), may hold values from -1.75 to 1.75
- key_weight: bfloat16 [768, 768], P('dp', 'narrow'), may hold values from -0.21875 to 0.21875
- value_weight: bfloat16 [768, 768], P('dp', 'narrow'), may hold values from -0.21875 to 0.21875
- value_bias: bfloat16 [768], P('dp'), may hold values from -1.75 to 1.75
- output_weight: bfloat16 [768, 768], P('dp', 'narrow'), may hold values from -1.75 to 1.75
- output_bias: bfloat16 [768], P('dp'), may hold values from -1.75 to 1.75
- first_gain: bfloat16 [768], P('dp'), may hold values from 0.5 to 1.5
- first_shift: bfloat16 [768], P('dp'), may hold values from -1.75 to 1.75
- up_weight: bfloat16 [768, 3072], P('dp', 'narrow'), may hold values from -0.21875 to 0.21875
- up_bias: bfloat16 [3072], P('dp'), may hold values from -1.75 to 1.75
- down_weight: bfloat16 [3072, 768], P('dp', 'narrow'), may hold values from -0.21875 to 0.21875
- down_bias: bfloat16 [768], P('dp'), may hold values from -1.75 to 1.75
- second_gain: bfloat16 [768], P('dp'), may hold values from 0.5 to 1.5
- second_shift: bfloat16 [768], P('dp'), may hold values from -1.75 to 1.75
- out_cotangent: bfloat16 [32768, 768], P(('dp', 'narrow')), may hold values from -6 to 6
- loss_cotangent: float32 [128], P('dp'), may hold values from -131072 to 131072
Outputs:
- mixed: bfloat16 [32768, 768], P('dp')
- transport: float32 [128], P('dp')
- grad_inputs: float32 [32768, 768], P(('dp', 'narrow'))
- grad_query_weight: float32 [768, 768], P('dp', 'narrow')
- grad_query_bias: float32 [768], P('dp')
- grad_key_weight: float32 [768, 768], P('dp', 'narrow')
- grad_value_weight: float32 [768, 768], P('dp', 'narrow')
- grad_value_bias: float32 [768], P('dp')
- grad_output_weight: float32 [768, 768], P('dp', 'narrow')
- grad_output_bias: float32 [768], P('dp')
- grad_first_gain: float32 [768], P('dp')
- grad_first_shift: float32 [768], P('dp')
- grad_up_weight: float32 [768, 3072], P('dp', 'narrow')
- grad_up_bias: float32 [3072], P('dp')
- grad_down_weight: float32 [3072, 768], P('dp', 'narrow')
- grad_down_bias: float32 [768], P('dp')
- grad_second_gain: float32 [768], P('dp')
- grad_second_shift: float32 [768], P('dp')
The draws below stay inside these ranges and needn't reach their ends.
Inputs may be any that keep to these rules, and one draw needn't show every extreme that they name: `segments`: along each packed sequence the segment number never falls; each segment is a run of a multiple of 16 rows; in every aligned group of 4 packed sequences one, drawn from the seed, is a single segment. `row_kind`: the first row of every segment is a word and its last row a region.
All inputs are finite; a program needn't handle non-finite values.
Results may differ from the reference program's by a relative error of at most 0.018.
The reference program's roundings to bfloat16 on the way count: a program that leaves them out, or rounds other values in their place, can miss the bound.
Values may be sent and summed in bfloat16 or wider, within the bound.
A program may use at most 192 MiB of HBM per device.

```python
import jax
import jax.numpy as jnp
from jax import lax

D = 768
HEADS = 12
HEAD_DIM = 64
FF = 3072
LEN = 256
ITERS = 20
PACKS = 128
TOKENS = 32768


def layout(key):
    cut_key, bit_key, pick_key = jax.random.split(key, 3)
    cuts = jax.random.randint(cut_key, (PACKS, 3, 1), 1, LEN // 16 + 1) * 16
    chosen = jax.random.randint(pick_key, (), 0, 4)
    whole = jnp.arange(PACKS) % 4 == chosen
    cuts = jnp.where(whole[:, None, None], LEN, cuts)
    position = jnp.arange(LEN)[None, None, :]
    segment = jnp.sum((position >= cuts).astype(jnp.int32), axis=1).astype(jnp.int32)
    coins = jax.random.randint(bit_key, (PACKS, LEN), 0, 2)
    before = jnp.concatenate([segment[:, :1] - 1, segment[:, :-1]], axis=1)
    after = jnp.concatenate([segment[:, 1:], segment[:, -1:] + 1], axis=1)
    opening = segment != before
    closing = segment != after
    kinds = jnp.where(opening, 0, jnp.where(closing, 1, coins)).astype(jnp.int32)
    return (segment, kinds)


def draw_segments(key, part):
    segment, kinds = layout(key)
    return segment


def draw_row_kind(key, part):
    segment, kinds = layout(key)
    return kinds


def block_levels(stream_key, dims, shards, least, largest):
    def one(dim, blocks):
        steps = jax.random.uniform(jax.random.fold_in(jax.random.fold_in(stream_key, 6), dim), (blocks,), jnp.float32, least / len(shards), largest / len(shards))
        return jnp.repeat(jnp.exp(steps), dims[dim] // blocks).reshape((-1,) + (1,) * (len(dims) - dim - 1))

    level = one(*shards[0])
    for cut in shards[1:]:
        level = level * one(*cut)
    return level


def scatter_about(rng, extent, scale, bound, cuts=(), kind=jnp.bfloat16):
    result = jax.random.normal(rng, extent, jnp.float32) * scale
    if len(cuts) > 0:
        result = block_levels(rng, extent, cuts, -0.22, 0.18) * result
    return jnp.clip(result, min=-bound, max=bound).astype(kind)


def setup_inputs(seed: int = 0) -> dict:
    streams_of = jax.random.split(jax.random.key(seed), 21)
    inputs = scatter_about(streams_of[0], (TOKENS, D), 1.0, 6.0, ((0, 32),))
    segments = draw_segments(jax.random.fold_in(streams_of[20], 71), 0)
    row_kind = draw_row_kind(jax.random.fold_in(streams_of[20], 71), 0)
    query_weight = scatter_about(streams_of[3], (D, D), D ** -0.5, 0.21875, ((0, 8), (1, 4)))
    query_bias = scatter_about(streams_of[4], (D,), 0.3, 1.75, ((0, 8),))
    key_weight = scatter_about(streams_of[5], (D, D), D ** -0.5, 0.21875, ((0, 8), (1, 4)))
    value_weight = scatter_about(streams_of[6], (D, D), D ** -0.5, 0.21875, ((0, 8), (1, 4)))
    value_bias = scatter_about(streams_of[7], (D,), 0.3, 1.75, ((0, 8),))
    output_weight = scatter_about(streams_of[8], (D, D), (D // 64) ** -0.5, 1.75, ((0, 8), (1, 4)))
    output_bias = scatter_about(streams_of[9], (D,), 0.3, 1.75, ((0, 8),))
    first_gain = jnp.clip(1.0 + 0.1 * jax.random.normal(streams_of[10], (D,), jnp.float32), 0.5, 1.5).astype(jnp.bfloat16)
    first_shift = scatter_about(streams_of[11], (D,), 0.3, 1.75, ((0, 8),))
    up_weight = scatter_about(streams_of[12], (D, FF), D ** -0.5, 0.21875, ((0, 8), (1, 4)))
    up_bias = scatter_about(streams_of[13], (FF,), 0.3, 1.75, ((0, 8),))
    down_weight = scatter_about(streams_of[14], (FF, D), (FF // 4) ** -0.5, 0.21875, ((0, 8), (1, 4)))
    down_bias = scatter_about(streams_of[15], (D,), 0.3, 1.75, ((0, 8),))
    second_gain = jnp.clip(1.0 + 0.1 * jax.random.normal(streams_of[16], (D,), jnp.float32), 0.5, 1.5).astype(jnp.bfloat16)
    second_shift = scatter_about(streams_of[17], (D,), 0.3, 1.75, ((0, 8),))
    out_cotangent = scatter_about(streams_of[18], (TOKENS, D), 1.0, 6.0, ((0, 32),))
    loss_cotangent = scatter_about(streams_of[19], (PACKS,), (LEN * D // 8), 131072.0, ((0, 8),), jnp.float32)
    return dict(inputs=inputs, segments=segments, row_kind=row_kind, query_weight=query_weight, query_bias=query_bias, key_weight=key_weight, value_weight=value_weight, value_bias=value_bias, output_weight=output_weight, output_bias=output_bias, first_gain=first_gain, first_shift=first_shift, up_weight=up_weight, up_bias=up_bias, down_weight=down_weight, down_bias=down_bias, second_gain=second_gain, second_shift=second_shift, out_cotangent=out_cotangent, loss_cotangent=loss_cotangent)


HIGH = lax.Precision.HIGHEST
EPS_NORM = 1e-06
BETA = 0.5
MASKED = -1e+30

@jax.custom_vjp
def low(v):
    return lax.optimization_barrier(v.astype(jnp.bfloat16)).astype(jnp.float32)

@jax.custom_vjp
def low_back(v):
    return v

def low_keep(v):
    return (low(v), None)

def low_pass(kept, grad):
    return (grad,)

def back_keep(v):
    return (v, None)

def back_low(kept, grad):
    return (low(grad),)
low.defvjp(low_keep, low_pass)
low_back.defvjp(back_keep, back_low)

def layer_norm(values, gain, shift):
    centre = values - lax.optimization_barrier(jnp.mean(values, axis=-1, keepdims=True))
    spread = lax.optimization_barrier(jnp.mean(centre * centre, axis=-1, keepdims=True))
    return centre * lax.rsqrt(spread + EPS_NORM) * gain + shift

def block(rows_in, seg_rows, kind_rows, params):
    w_query, b_query, w_key, w_value, b_value, w_output, b_output, g_first, s_first, w_up, b_up, w_down, b_down, g_second, s_second = params
    count = seg_rows.shape[0]
    shape_heads = (count, LEN, HEADS, HEAD_DIM)
    query = low(low_back(jnp.dot(rows_in, w_query, precision=HIGH) + b_query)).reshape(shape_heads)
    keys = low(low_back(jnp.dot(rows_in, w_key, precision=HIGH))).reshape(shape_heads)
    values = low(low_back(jnp.dot(rows_in, w_value, precision=HIGH) + b_value)).reshape(shape_heads)
    scores = low_back(jnp.einsum('plhe,pmhe->phlm', query, keys, precision=HIGH) * HEAD_DIM ** (-0.5))
    paired = seg_rows[:, :, None] == seg_rows[:, None, :]
    scores = jnp.where(paired[:, None], scores, MASKED)
    probability = jax.nn.softmax(scores, axis=-1)
    context = low(low_back(jnp.einsum('phlm,pmhe->plhe', low(probability), values, precision=HIGH)))
    context = context.reshape(count * LEN, D)
    attended = low_back(jnp.dot(context, w_output, precision=HIGH) + b_output)
    first = layer_norm(rows_in + attended, g_first, s_first)
    inner = low_back(jnp.dot(low(first), w_up, precision=HIGH) + b_up)
    branch = low_back(jnp.dot(low(jax.nn.gelu(inner, approximate=False)), w_down, precision=HIGH) + b_down)
    output = low(layer_norm(first + branch, g_second, s_second))
    feats = output.reshape(count, LEN, D)
    unit_rows = low(feats * lax.rsqrt(lax.optimization_barrier(jnp.sum(feats * feats, axis=-1, keepdims=True)) + EPS_NORM))
    cosine = low_back(jnp.einsum('pid,pjd->pij', unit_rows, unit_rows, precision=HIGH))
    costs = 1.0 - cosine
    word_rows = (kind_rows == 0).astype(jnp.float32)
    region_rows = 1.0 - word_rows
    same_segment = paired.astype(jnp.float32)
    word_count = lax.optimization_barrier(jnp.sum(same_segment * word_rows[:, None, :], axis=2))
    region_count = lax.optimization_barrier(jnp.sum(same_segment * region_rows[:, :, None], axis=1))
    kernel = jnp.exp(-costs / BETA) * same_segment * word_rows[:, :, None] * region_rows[:, None, :]
    sigma_cols = region_rows / region_count
    coupling = jnp.ones_like(kernel)
    for iterate in range(ITERS):
        weighted = kernel * coupling
        row_sum = lax.optimization_barrier(jnp.sum(weighted * sigma_cols[:, None, :], axis=2))
        delta_rows = word_rows / (word_count * row_sum + 1.0 - word_rows)
        col_sum = lax.optimization_barrier(jnp.sum(weighted * delta_rows[:, :, None], axis=1))
        sigma_cols = region_rows / (region_count * col_sum + 1.0 - region_rows)
        coupling = delta_rows[:, :, None] * weighted * sigma_cols[:, None, :]
    return (output, lax.optimization_barrier(jnp.sum(coupling * costs, axis=(1, 2))))

def reference(inputs, segments, row_kind, query_weight, query_bias, key_weight, value_weight, value_bias, output_weight, output_bias, first_gain, first_shift, up_weight, up_bias, down_weight, down_bias, second_gain, second_shift, out_cotangent, loss_cotangent):
    weights = tuple((item.astype(jnp.float32) for item in (query_weight, query_bias, key_weight, value_weight, value_bias, output_weight, output_bias, first_gain, first_shift, up_weight, up_bias, down_weight, down_bias, second_gain, second_shift)))
    group_packs = 16

    def forward(rows_all, *params):
        grouped = rows_all.reshape(PACKS // group_packs, group_packs * LEN, D)
        seg_groups = segments.reshape(PACKS // group_packs, group_packs, LEN)
        kind_groups = row_kind.reshape(PACKS // group_packs, group_packs, LEN)

        def apply(item):
            return block(item[0], item[1], item[2], params)
        outputs, losses = lax.map(jax.checkpoint(apply), (grouped, seg_groups, kind_groups))
        return (outputs.reshape(TOKENS, D), losses.reshape(PACKS))
    (output, losses), pullback = jax.vjp(forward, inputs.astype(jnp.float32), *weights)
    grads = pullback((out_cotangent.astype(jnp.float32), loss_cotangent))
    return (output.astype(jnp.bfloat16), losses, grads[0], grads[1], grads[2], grads[3], grads[4], grads[5], grads[6], grads[7], grads[8], grads[9], grads[10], grads[11], grads[12], grads[13], grads[14], grads[15])
```

```python
import functools

import jax
import jax.numpy as jnp
from jax import lax
from jax.experimental import pallas as pl
from jax.experimental.pallas import tpu as pltpu
from jax.sharding import PartitionSpec as P

D = 768
HEADS = 12
HEAD_DIM = 64
LEN = 256
ITERS = 20
ROWS = 32
VMEM_LIMIT = 60 * 1024 * 1024


EPS_NORM = 1e-06
BETA = 0.5
MASKED = -1e30


def product(left, right):
    return jnp.dot(left, right, preferred_element_type=jnp.float32)


def product_left(left, right):
    return lax.dot_general(
        left, right, (((0,), (0,)), ((), ())), preferred_element_type=jnp.float32
    )


def product_right(left, right):
    return lax.dot_general(
        left, right, (((1,), (1,)), ((), ())), preferred_element_type=jnp.float32
    )


def layer_norm(values, gain, shift):
    centre = values - jnp.mean(values, axis=-1, keepdims=True)
    spread = jnp.mean(centre * centre, axis=-1, keepdims=True)
    recip = lax.rsqrt(spread + EPS_NORM)
    normed = centre * recip
    return (normed * gain + shift, normed, recip)


def norm_back(grad_out, normed, recip, gain):
    scaled = grad_out * gain
    inner_mean = jnp.mean(scaled, axis=-1, keepdims=True)
    cross_mean = jnp.mean(scaled * normed, axis=-1, keepdims=True)
    grad_in = recip * (scaled - inner_mean - normed * cross_mean)
    return (grad_in, jnp.sum(grad_out * normed, axis=0), jnp.sum(grad_out, axis=0))


def gelu_slope(values):
    normal_cdf = 0.5 * (1.0 + lax.erf(values * 0.7071067811865476))
    density = jnp.exp(-0.5 * values * values) * 0.3989422804014327
    return normal_cdf + values * density


def fetch_weights(matrices, vectors):
    wide = [lax.all_gather(item, "narrow", axis=1, tiled=True) for item in matrices]
    return (
        [lax.all_gather(item, "dp", axis=0, tiled=True) for item in wide],
        [lax.all_gather(item, "dp", axis=0, tiled=True).astype(jnp.float32) for item in vectors],
    )


def reduce_grads(matrices, vectors):
    reduced = [lax.psum_scatter(item, "dp", scatter_dimension=0, tiled=True) for item in matrices]
    sums = [lax.psum_scatter(item, "dp", scatter_dimension=0, tiled=True) for item in vectors]
    return (
        [
            lax.psum_scatter(
                item.astype(jnp.bfloat16), "narrow", scatter_dimension=1, tiled=True
            ).astype(jnp.float32)
            for item in reduced
        ],
        lax.psum(sums, "narrow"),
    )


MESH = pl.DeviceIdType.MESH


def hops():
    dp, narrow = lax.axis_index("dp"), lax.axis_index("narrow")
    return (dp // 2, lax.rem(dp, 2), narrow // 2, lax.rem(narrow, 2))


def place(me, depth, item, order):
    s, a, b, c = item
    z, x, y, core = me
    dx, dy = (a, b) if order == "x" else (b, a)
    z = z if isinstance(s, int) and s == 0 else lax.rem(z + s + depth, depth)
    x = 1 - x if dx else x
    y = 1 - y if dy else y
    core = 1 - core if c else core
    return (2 * z + x, 2 * y + core)


def greet(me, depth):
    peers = [place(me, depth, (s, 0, 0, 0), "x") for s in range(1, depth)]
    peers += [place(me, depth, (0, *bits), "x") for bits in ((1, 0, 0), (0, 1, 0), (0, 0, 1))]
    barrier = pltpu.get_barrier_semaphore()
    for peer in peers:
        pl.semaphore_signal(barrier, inc=1, device_id=peer, device_id_type=MESH)
    pl.semaphore_wait(barrier, len(peers))


def number(item):
    s, a, b, c = item
    return ((s * 2 + a) * 2 + b) * 2 + c


class Gather:
    def __init__(self, land, send_sem, recv_sem, chunks):
        self.land, self.send_sem, self.recv_sem, self.chunks = land, send_sem, recv_sem, chunks
        self.me = hops()
        self.depth = land.shape[0] // 2
        self.sent = []

    def copy(self, k, item, target):
        first, rows, order = self.chunks[k]
        s, a, b, c = item
        source = place(self.me, self.depth, (-s, a, b, c), order)
        block = self.land.at[source[0], source[1], pl.ds(first, rows), :]
        kind, amount = target
        there = {"z": (amount, 0, 0, 0), "p": (0, 1, 0, 0), "q": (0, 0, 1, 0), "c": (0, 0, 0, 1)}[kind]
        at = {"z": (amount, a, b, c), "p": (s, 1, b, c), "q": (s, a, 1, c), "c": (s, a, b, 1)}[kind]
        mark = number(at)
        return pltpu.make_async_remote_copy(
            src_ref=block,
            dst_ref=block,
            send_sem=self.send_sem.at[k, mark],
            recv_sem=self.recv_sem.at[k, mark],
            device_id=place(self.me, self.depth, there, order),
            device_id_type=MESH,
        )

    def send(self, k, item, kinds):
        for kind in kinds:
            for amount in range(1, self.depth) if kind == "z" else (1,):
                copy = self.copy(k, item, (kind, amount))
                copy.start()
                self.sent.append(copy)

    def wait(self, k, item):
        first, rows, order = self.chunks[k]
        s, a, b, c = item
        source = place(self.me, self.depth, (-s, a, b, c), order)
        block = self.land.at[source[0], source[1], pl.ds(first, rows), :]
        mark = number(item)
        pltpu.make_async_remote_copy(
            src_ref=block,
            dst_ref=block,
            send_sem=self.send_sem.at[k, mark],
            recv_sem=self.recv_sem.at[k, mark],
            device_id=place(self.me, self.depth, (0, 0, 0, 1), order),
            device_id_type=MESH,
        ).wait_recv()

    def start(self, k):
        self.send(k, (0, 0, 0, 0), "zpqc")

    def after_z(self, k):
        for s in range(1, self.depth):
            self.wait(k, (s, 0, 0, 0))
            self.send(k, (s, 0, 0, 0), "pqc")

    def after_p(self, k):
        for s in range(self.depth):
            self.wait(k, (s, 1, 0, 0))
            self.send(k, (s, 1, 0, 0), "qc")

    def after_q(self, k):
        for s in range(self.depth):
            for a in range(2):
                self.wait(k, (s, a, 1, 0))
                self.send(k, (s, a, 1, 0), "c")

    def after_c(self, k):
        for s in range(self.depth):
            for a in range(2):
                for b in range(2):
                    self.wait(k, (s, a, b, 1))

    def drain(self):
        for copy in self.sent:
            copy.wait_send()
        self.sent = []


def swap(half):
    return pltpu.roll(half, 64, 1)


def left_half(shape):
    return lax.broadcasted_iota(jnp.int32, shape, 1) < 64


def pack_block(block, odd):
    rows = block.shape[0]
    wide = jnp.concatenate([block, jnp.zeros((rows, 64), jnp.float32)], axis=1)
    turned = pltpu.roll(wide, 192, 1)
    main = jnp.where(odd, turned[:, :128], wide[:, :128])
    rest = jnp.where(left_half((rows, 128)), jnp.where(odd, wide[:, :128], wide[:, 128:]), 0.0)
    top, low = rest[: rows // 2], rest[rows // 2 :]
    return main, jnp.where(odd, swap(top) + low, top + swap(low))


def middle_of(even, odd):
    left = left_half(even.shape)
    return jnp.where(left, even, odd), swap(jnp.where(left, odd, even))


def fold_middle(top, low):
    left = left_half(top.shape)
    return jnp.where(left, top, swap(low)), jnp.where(left, swap(low), top)


VEC, SQUARE, UP, DOWN, TOTAL = 0, 16, 592, 1168, 1744


def gather_chunks():
    return (
        (0, 160, "x"), (160, 144, "y"),
        (304, 144, "x"), (448, 144, "y"),
        (592, 144, "x"), (736, 144, "y"), (880, 144, "x"), (1024, 144, "y"),
        (1168, 144, "x"), (1312, 144, "y"), (1456, 144, "x"), (1600, 144, "y"),
    )


def gather_kernel(
    q_ref, k_ref, v_ref, o_ref, up_ref, down_ref, vec_ref,
    fq_ref, fk_ref, fv_ref, fo_ref, fup_ref, fdown_ref, fvec_ref,
    land, send_sem, recv_sem,
):
    me = hops()
    depth = land.shape[0] // 2
    dp, narrow = lax.axis_index("dp"), lax.axis_index("narrow")
    odd = lax.rem(narrow, 2) == 1
    own = land.at[dp, narrow]
    half = q_ref.shape[0]
    own[0:16, :] = vec_ref[...]
    for i, ref in enumerate((q_ref, k_ref, v_ref, o_ref)):
        main, rest = pack_block(ref[...].astype(jnp.float32), odd)
        at = SQUARE + 144 * i
        own[at : at + 96, :] = main.astype(jnp.bfloat16)
        own[at + 96 : at + 144, :] = rest.astype(jnp.bfloat16)
    greet(me, depth)
    g = Gather(land, send_sem, recv_sem, gather_chunks())
    for k in range(4):
        g.start(k)
    for t in range(6):
        own[UP + 96 * t : UP + 96 * (t + 1), :] = up_ref[:, 128 * t : 128 * (t + 1)]
    main, rest = pack_block(down_ref[...].astype(jnp.float32), odd)
    own[DOWN : DOWN + 384, :] = main.astype(jnp.bfloat16)
    own[DOWN + 384 : DOWN + 576, :] = rest.astype(jnp.bfloat16)

    def put_square(ref, at, rows):
        for d in range(2 * depth):
            for pair in range(land.shape[1] // 2):
                even, other = land.at[d, 2 * pair], land.at[d, 2 * pair + 1]
                here = pl.ds(d * rows, rows)
                ref[here, pl.ds(384 * pair, 128)] = even[at : at + rows, :]
                ref[here, pl.ds(384 * pair + 256, 128)] = other[at : at + rows, :]
                top, low = middle_of(
                    even[at + rows : at + rows * 3 // 2, :].astype(jnp.float32),
                    other[at + rows : at + rows * 3 // 2, :].astype(jnp.float32),
                )
                ref[pl.ds(d * rows, rows // 2), pl.ds(384 * pair + 128, 128)] = top.astype(jnp.bfloat16)
                ref[pl.ds(d * rows + rows // 2, rows // 2), pl.ds(384 * pair + 128, 128)] = low.astype(jnp.bfloat16)

    steps = len(g.chunks) // 2
    for j in range(steps + 4):
        for stage, lag in ((g.after_z, 0), (g.after_p, 1), (g.after_q, 2), (g.after_c, 3)):
            if 0 <= j - lag < steps:
                stage(2 * (j - lag))
                stage(2 * (j - lag) + 1)
            if lag == 0 and j + 2 < steps:
                g.start(2 * j + 4)
                g.start(2 * j + 5)
        if j == 4:
            for i, ref in enumerate((fq_ref, fk_ref, fv_ref, fo_ref)):
                put_square(ref, SQUARE + 144 * i, 96)
    for d in range(2 * depth):
        for n in range(land.shape[1]):
            for t in range(6):
                fup_ref[pl.ds(96 * d, 96), pl.ds(768 * n + 128 * t, 128)] = land[d, n, UP + 96 * t : UP + 96 * (t + 1), :]
    put_square(fdown_ref, DOWN, 384)
    for d in range(2 * depth):
        fvec_ref[d] = land[d, 0, 0:16, :].astype(jnp.float32)
    g.drain()


def gather_weights(matrices, vectors, dp, narrow):
    packed = jnp.stack([jnp.pad(item, (0, 32)) for item in vectors[:8]])
    packed = jnp.concatenate([packed, vectors[8].reshape(3, 128), jnp.zeros((5, 128), jnp.bfloat16)])
    vmem = pl.BlockSpec(memory_space=pltpu.VMEM)
    square = jax.ShapeDtypeStruct((D, D), jnp.bfloat16)
    count = len(gather_chunks())
    out = pl.pallas_call(
        gather_kernel,
        name="gather",
        out_shape=(
            square, square, square, square,
            jax.ShapeDtypeStruct((D, 4 * D), jnp.bfloat16),
            jax.ShapeDtypeStruct((4 * D, D), jnp.bfloat16),
            jax.ShapeDtypeStruct((dp, 16, 128), jnp.float32),
        ),
        in_specs=[vmem] * 7,
        out_specs=(vmem,) * 7,
        scratch_shapes=[
            pltpu.VMEM((dp, narrow, TOTAL, 128), jnp.bfloat16),
            pltpu.SemaphoreType.DMA((count, dp * narrow)),
            pltpu.SemaphoreType.DMA((count, dp * narrow)),
        ],
        compiler_params=pltpu.CompilerParams(
            collective_id=0, has_side_effects=True, vmem_limit_bytes=VMEM_LIMIT
        ),
    )(*matrices, packed)
    vec = out[6]
    flat = [vec[:, i, :96].reshape(D) for i in range(8)] + [vec[:, 8:11, :].reshape(4 * D)]
    return out[:6], flat


class Scatter:
    def __init__(self, part, lands, send_sem, recv_sem, chunks):
        self.part, self.lands, self.send_sem, self.recv_sem, self.chunks = part, lands, send_sem, recv_sem, chunks
        self.me = hops()
        self.depth = part.shape[0] // 2
        self.sent = []

    def block(self, k, item):
        first, rows, order = self.chunks[k]
        owner = place(self.me, self.depth, item, order)
        return self.part.at[owner[0], owner[1], pl.ds(first, rows), :]

    def landing(self, k, item):
        first, rows, order = self.chunks[k]
        s, a, b, c = item
        rows = pl.ds(first, rows)
        if c:
            return self.lands[0].at[(s * 2 + a) * 2 + b, rows, :]
        if b:
            return self.lands[1].at[s * 2 + a, rows, :]
        if a:
            return self.lands[2].at[s, rows, :]
        return self.lands[3].at[s - 1, rows, :]

    def copy(self, k, item):
        s, a, b, c = item
        hop = (0, 0, 0, 1) if c else (0, 0, 1, 0) if b else (0, 1, 0, 0) if a else (s, 0, 0, 0)
        mark = number(item)
        return pltpu.make_async_remote_copy(
            src_ref=self.block(k, item),
            dst_ref=self.landing(k, item),
            send_sem=self.send_sem.at[k, mark],
            recv_sem=self.recv_sem.at[k, mark],
            device_id=place(self.me, self.depth, hop, self.chunks[k][2]),
            device_id_type=MESH,
        )

    def send(self, k, item):
        copy = self.copy(k, item)
        copy.start()
        self.sent.append(copy)

    def take(self, k, item, into):
        self.copy(k, item).wait_recv()
        ref = self.block(k, into)
        ref[...] = (ref[...].astype(jnp.float32) + self.landing(k, item)[...].astype(jnp.float32)).astype(jnp.bfloat16)

    def start(self, k):
        for s in range(self.depth):
            for a in range(2):
                for b in range(2):
                    self.send(k, (s, a, b, 1))

    def after_c(self, k):
        for b in (1, 0):
            for s in range(self.depth):
                for a in range(2):
                    self.take(k, (s, a, b, 1), (s, a, b, 0))
                    if b:
                        self.send(k, (s, a, 1, 0))

    def after_q(self, k):
        for a in (1, 0):
            for s in range(self.depth):
                self.take(k, (s, a, 1, 0), (s, a, 0, 0))
                if a:
                    self.send(k, (s, 1, 0, 0))

    def after_p(self, k):
        for s in [*range(1, self.depth), 0]:
            self.take(k, (s, 1, 0, 0), (s, 0, 0, 0))
            if s:
                self.send(k, (s, 0, 0, 0))

    def total(self, k):
        for s in range(1, self.depth):
            self.copy(k, (s, 0, 0, 0)).wait_recv()
        first, rows, order = self.chunks[k]
        value = self.block(k, (0, 0, 0, 0))[...].astype(jnp.float32)
        for s in range(1, self.depth):
            value = value + self.landing(k, (s, 0, 0, 0))[...].astype(jnp.float32)
        return value

    def drain(self):
        for copy in self.sent:
            copy.wait_send()
        self.sent = []


def scatter_lands(depth):
    shape = lambda count: pltpu.VMEM((count, TOTAL, 128), jnp.bfloat16)
    return [shape(depth * 4), shape(depth * 2), shape(depth), shape(max(depth - 1, 1))]


def scatter_kernel(
    q_ref, k_ref, v_ref, o_ref, up_ref, down_ref, vec_ref,
    gq_ref, gk_ref, gv_ref, go_ref, gup_ref, gdown_ref, gvec_ref,
    part, land_c, land_q, land_p, land_z, total, send_sem, recv_sem,
):
    me = hops()
    depth = part.shape[0] // 2
    narrow = lax.axis_index("narrow")
    odd = lax.rem(narrow, 2) == 1
    greet(me, depth)
    g = Scatter(part, (land_c, land_q, land_p, land_z), send_sem, recv_sem, scatter_chunks())

    def take_square(ref, at, rows):
        for d in range(2 * depth):
            for pair in range(part.shape[1] // 2):
                even, other = part.at[d, 2 * pair], part.at[d, 2 * pair + 1]
                here = pl.ds(d * rows, rows)
                even[at : at + rows, :] = ref[here, pl.ds(384 * pair, 128)]
                other[at : at + rows, :] = ref[here, pl.ds(384 * pair + 256, 128)]
                middle = ref[here, pl.ds(384 * pair + 128, 128)].astype(jnp.float32)
                one, two = fold_middle(middle[: rows // 2], middle[rows // 2 :])
                even[at + rows : at + rows * 3 // 2, :] = one.astype(jnp.bfloat16)
                other[at + rows : at + rows * 3 // 2, :] = two.astype(jnp.bfloat16)

    take_square(down_ref, DOWN, 384)
    for d in range(2 * depth):
        for n in range(part.shape[1]):
            for t in range(6):
                part[d, n, UP + 96 * t : UP + 96 * (t + 1), :] = up_ref[pl.ds(96 * d, 96), pl.ds(768 * n + 128 * t, 128)]
    for i, ref in enumerate((q_ref, k_ref, v_ref, o_ref)):
        take_square(ref, SQUARE + 144 * i, 96)
    for d in range(2 * depth):
        for n in range(part.shape[1]):
            part[d, n, 0:16, :] = vec_ref[d]
    count = len(g.chunks)
    for j in range(count + 4):
        if j < count:
            g.start(j)
        if 0 <= j - 1 < count:
            g.after_c(j - 1)
        if 0 <= j - 2 < count:
            g.after_q(j - 2)
        if 0 <= j - 3 < count:
            g.after_p(j - 3)
        if 0 <= j - 4 < count:
            first, rows, order = g.chunks[j - 4]
            total[pl.ds(first, rows), :] = g.total(j - 4)
    gvec_ref[...] = total[0:16, :]
    for t in range(6):
        gup_ref[:, 128 * t : 128 * (t + 1)] = total[UP + 96 * t : UP + 96 * (t + 1), :]
    for ref, at in ((gq_ref, SQUARE), (gk_ref, SQUARE + 144), (gv_ref, SQUARE + 288), (go_ref, SQUARE + 432), (gdown_ref, DOWN)):
        rows = ref.shape[0]
        ref[...] = unpack_block(total[at : at + rows, :], total[at + rows : at + rows * 3 // 2, :], odd)
    g.drain()


def unpack_block(main, rest, odd):
    left = left_half(rest.shape)
    other = swap(rest)
    top, low = jnp.where(odd, other, rest), jnp.where(odd, rest, other)
    piece = jnp.concatenate([top, low], axis=0)
    piece = jnp.where(left_half(piece.shape), piece, 0.0)
    swapped = swap(main)
    first = jnp.where(odd, jnp.where(left_half(piece.shape), piece, swapped), main)
    second = jnp.where(odd, swapped, piece)
    return jnp.concatenate([first, second[:, :64]], axis=1)


def scatter_chunks():
    return (
        (1168, 144, "x"), (1312, 144, "y"), (1456, 144, "x"), (1600, 144, "y"),
        (592, 144, "x"), (736, 144, "y"), (880, 144, "x"), (1024, 144, "y"),
        (448, 144, "x"), (304, 144, "y"), (160, 144, "x"), (0, 160, "y"),
    )


def scatter_grads(matrices, packed, dp, narrow):
    vmem = pl.BlockSpec(memory_space=pltpu.VMEM)
    square = jax.ShapeDtypeStruct((D // dp, D // narrow), jnp.float32)
    count = len(scatter_chunks())
    return pl.pallas_call(
        scatter_kernel,
        name="scatter",
        out_shape=(
            square, square, square, square,
            jax.ShapeDtypeStruct((D // dp, 4 * D // narrow), jnp.float32),
            jax.ShapeDtypeStruct((4 * D // dp, D // narrow), jnp.float32),
            jax.ShapeDtypeStruct((16, 128), jnp.float32),
        ),
        in_specs=[vmem] * 7,
        out_specs=(vmem,) * 7,
        scratch_shapes=[
            pltpu.VMEM((dp, narrow, TOTAL, 128), jnp.bfloat16),
            *scatter_lands(dp // 2),
            pltpu.VMEM((TOTAL, 128), jnp.float32),
            pltpu.SemaphoreType.DMA((count, dp * narrow)),
            pltpu.SemaphoreType.DMA((count, dp * narrow)),
        ],
        compiler_params=pltpu.CompilerParams(
            collective_id=1, has_side_effects=True, vmem_limit_bytes=VMEM_LIMIT
        ),
    )(*matrices, packed)


def transport_kernel(
    mixed_ref, seg_ref, kind_ref, weight_ref, cot_ref, normed_ref, recip_ref, gain_ref,
    value_ref, second_ref, branch_ref, sums_ref,
    kern_ref, prod_ref, flow_ref, acc_ref, left_ref, sigma_ref,
):
    packs = mixed_ref.shape[0] // LEN
    base = lax.axis_index("narrow") * packs
    blocks = LEN // ROWS
    lanes = lambda col: jnp.concatenate([col, col], axis=1)
    fold = lambda wide: wide[:, :128] + wide[:, 128:]
    eight = lambda wide: jnp.sum(wide.reshape(ROWS // 8, 8, LEN), axis=0)
    replicate = lambda col: jnp.broadcast_to(col, (ROWS, 128))

    def turned(row):
        return jnp.transpose(jnp.broadcast_to(row, (128, LEN)))

    for p in range(packs):
        rows = pl.ds(p * LEN, LEN)
        feats = mixed_ref[rows, :].astype(jnp.float32)
        recip = lax.rsqrt(jnp.sum(feats * feats, axis=1, keepdims=True) + EPS_NORM)
        unit = (feats * recip).astype(jnp.bfloat16)
        cosine = product_right(unit, unit)
        seg_row = seg_ref[pl.ds(base + p, 1), :].astype(jnp.float32)
        region_row = jnp.where(kind_ref[pl.ds(base + p, 1), :] == 0, 0.0, 1.0)
        seg_col = turned(seg_row)
        word_col = 1.0 - turned(region_row)
        same = jnp.where(lanes(seg_col) == seg_row, 1.0, 0.0)
        word_count = jnp.sum(same * (1.0 - region_row), axis=1, keepdims=True)
        region_count = jnp.sum(same * lanes(1.0 - word_col), axis=0, keepdims=True)
        kern_ref[p] = jnp.exp((cosine - 1.0) * (1.0 / BETA)) * same * lanes(word_col) * region_row
        left_ref[p, 0] = word_col
        left_ref[p, 1] = jnp.broadcast_to(word_count, (LEN, 128))
        prod_ref[0, p] = jnp.ones((LEN, LEN), jnp.float32)
        sigma_ref[0, p, 0:1] = region_row / region_count
        sigma_ref[0, p, 1:2] = region_row
        sigma_ref[0, p, 2:3] = region_count

    def advance(t, carry):
        for p in range(packs):
            sigma = sigma_ref[t, p, 0:1]
            scale = jnp.where(t == 0, 1.0, sigma)
            region = sigma_ref[0, p, 1:2]
            count = sigma_ref[0, p, 2:3]
            total = jnp.zeros((8, LEN), jnp.float32)
            for b in range(blocks):
                rows = pl.ds(b * ROWS, ROWS)
                weighted = kern_ref[p, rows, :] * (prod_ref[t, p, rows, :] * scale)
                row_sum = jnp.sum(fold(weighted * sigma), axis=1, keepdims=True)
                word = left_ref[p, 0, rows, :]
                delta = word / (left_ref[p, 1, rows, :] * replicate(row_sum) + 1.0 - word)
                scaled = weighted * lanes(delta)
                prod_ref[t + 1, p, rows, :] = scaled
                total = total + eight(scaled)
            col_sum = jnp.sum(total, axis=0, keepdims=True)
            sigma_ref[t + 1, p, 0:1] = region / (count * col_sum + 1.0 - region)
        return carry

    lax.fori_loop(0, ITERS, advance, 0)

    starts = []
    for p in range(packs):
        rows = pl.ds(p * LEN, LEN)
        weight = weight_ref[base + p]
        feats = mixed_ref[rows, :].astype(jnp.float32)
        recip = lax.rsqrt(jnp.sum(feats * feats, axis=1, keepdims=True) + EPS_NORM)
        unit = (feats * recip).astype(jnp.bfloat16)
        cosine = product_right(unit, unit)
        moved = (prod_ref[ITERS, p] * sigma_ref[ITERS, p, 0:1]) * (1.0 - cosine)
        value_ref[p : p + 1, :] = jnp.broadcast_to(jnp.sum(moved), (1, 128))
        moved = moved * weight
        flow_ref[p] = moved
        acc_ref[p] = jnp.zeros((LEN, LEN), jnp.float32)
        starts += [jnp.sum(moved, axis=0, keepdims=True), jnp.zeros((1, LEN), jnp.float32)]

    def retreat(step, carry):
        t = ITERS - 1 - step
        out = []
        for p in range(packs):
            flow_sum, spread = carry[2 * p : 2 * p + 2]
            before = sigma_ref[t, p, 0:1]
            d_col = -sigma_ref[0, p, 2:3] * sigma_ref[t + 1, p, 0:1] * (spread + flow_sum)
            total = jnp.zeros((8, LEN), jnp.float32)
            shift = jnp.zeros((8, LEN), jnp.float32)
            for b in range(blocks):
                rows = pl.ds(b * ROWS, ROWS)
                scaled = prod_ref[t + 1, p, rows, :]
                flow = flow_ref[p, rows, :] + scaled * d_col
                d_row = replicate(jnp.sum(fold(flow), axis=1, keepdims=True))
                d_row = -left_ref[p, 1, rows, :] * d_row
                moved = scaled * lanes(d_row)
                flow = flow + moved * before
                flow_ref[p, rows, :] = flow
                acc_ref[p, rows, :] = acc_ref[p, rows, :] + flow
                total = total + eight(flow)
                shift = shift + eight(moved)
            out += [
                jnp.sum(total, axis=0, keepdims=True),
                before * jnp.sum(shift, axis=0, keepdims=True),
            ]
        return tuple(out)

    lax.fori_loop(0, ITERS, retreat, tuple(starts))

    sums = [jnp.zeros((1, D), jnp.float32)] * 3
    for p in range(packs):
        rows = pl.ds(p * LEN, LEN)
        coupling = prod_ref[ITERS, p] * sigma_ref[ITERS, p, 0:1]
        d_cost = weight_ref[base + p] * coupling - acc_ref[p] * (1.0 / BETA)
        d_cosine = (-d_cost).astype(jnp.bfloat16)
        feats = mixed_ref[rows, :].astype(jnp.float32)
        recip = lax.rsqrt(jnp.sum(feats * feats, axis=1, keepdims=True) + EPS_NORM)
        unit = feats * recip
        unit_low = unit.astype(jnp.bfloat16)
        d_unit = product(d_cosine, unit_low) + product_left(d_cosine, unit_low)
        d_mixed = cot_ref[rows, :].astype(jnp.float32) + recip * (
            d_unit - unit * jnp.sum(d_unit * unit, axis=1, keepdims=True)
        )
        normed = normed_ref[rows, :]
        scaled = d_mixed * gain_ref[...]
        inner_mean = jnp.mean(scaled, axis=1, keepdims=True)
        cross_mean = jnp.mean(scaled * normed, axis=1, keepdims=True)
        d_second = recip_ref[rows, 0:1] * (scaled - inner_mean - normed * cross_mean)
        d_branch = d_second.astype(jnp.bfloat16)
        second_ref[rows, :] = d_second
        branch_ref[rows, :] = d_branch
        sums[0] = sums[0] + jnp.sum(d_mixed * normed, axis=0, keepdims=True)
        sums[1] = sums[1] + jnp.sum(d_mixed, axis=0, keepdims=True)
        sums[2] = sums[2] + jnp.sum(d_branch.astype(jnp.float32), axis=0, keepdims=True)
    for k in range(3):
        sums_ref[k : k + 1, :] = sums[k]


def transport_step(mixed, segments, row_kind, weight, cotangent, normed, recip, gain):
    rows = mixed.shape[0]
    packs = rows // LEN
    vmem = pl.BlockSpec(memory_space=pltpu.VMEM)
    square = (packs, LEN, LEN)
    return pl.pallas_call(
        transport_kernel,
        name="transport",
        out_shape=(
            jax.ShapeDtypeStruct((packs, 128), jnp.float32),
            jax.ShapeDtypeStruct((rows, D), jnp.float32),
            jax.ShapeDtypeStruct((rows, D), jnp.bfloat16),
            jax.ShapeDtypeStruct((8, D), jnp.float32),
        ),
        in_specs=[vmem, vmem, vmem, pl.BlockSpec(memory_space=pltpu.SMEM), vmem, vmem, vmem, vmem],
        out_specs=(vmem, vmem, vmem, vmem),
        scratch_shapes=[
            pltpu.VMEM(square, jnp.float32),
            pltpu.VMEM((ITERS + 1, *square), jnp.float32),
            pltpu.VMEM(square, jnp.float32),
            pltpu.VMEM(square, jnp.float32),
            pltpu.VMEM((packs, 2, LEN, 128), jnp.float32),
            pltpu.VMEM((ITERS + 1, packs, 8, LEN), jnp.float32),
        ],
        compiler_params=pltpu.CompilerParams(vmem_limit_bytes=VMEM_LIMIT),
    )(mixed, segments, row_kind, weight, cotangent, normed, recip, gain)


def per_device(
    inputs,
    segments,
    row_kind,
    query_weight,
    query_bias,
    key_weight,
    value_weight,
    value_bias,
    output_weight,
    output_bias,
    first_gain,
    first_shift,
    up_weight,
    up_bias,
    down_weight,
    down_bias,
    second_gain,
    second_shift,
    out_cotangent,
    loss_cotangent,
):
    pack_count = inputs.shape[0] // LEN
    row_count = inputs.shape[0]
    position = lax.axis_index("narrow")
    own_seg = lax.dynamic_slice_in_dim(segments, position * pack_count, pack_count, 0)
    matrices = (query_weight, key_weight, value_weight, output_weight, up_weight, down_weight)
    vectors = (
        query_bias,
        value_bias,
        output_bias,
        first_gain,
        first_shift,
        down_bias,
        second_gain,
        second_shift,
        up_bias,
    )
    dp, narrow = lax.axis_size("dp"), lax.axis_size("narrow")
    direct = D // dp == 96 and D // narrow == 192
    fetch = functools.partial(gather_weights, dp=dp, narrow=narrow) if direct else fetch_weights
    (w_query, w_key, w_value, w_output, w_up, w_down), gathered = fetch(matrices, vectors)
    b_query, b_value, b_output, g_first, s_first, b_down, g_second, s_second, b_up = gathered
    shape_heads = (pack_count, LEN, HEADS, HEAD_DIM)
    scale = HEAD_DIM ** (-0.5)
    query_low = (product(inputs, w_query) + b_query).astype(jnp.bfloat16)
    key_low = product(inputs, w_key).astype(jnp.bfloat16)
    value_low = (product(inputs, w_value) + b_value).astype(jnp.bfloat16)
    query_heads = query_low.reshape(shape_heads)
    key_heads = key_low.reshape(shape_heads)
    value_heads = value_low.reshape(shape_heads)
    paired = own_seg[:, None, :, None] == own_seg[:, None, None, :]

    def attention_scores():
        raw = jnp.einsum(
            "plhe,pmhe->phlm", query_heads, key_heads, preferred_element_type=jnp.float32
        )
        return jnp.where(paired, raw * scale, MASKED)

    scores = attention_scores()
    highest = jnp.max(scores, axis=-1, keepdims=True)
    shifted = jnp.exp(scores - highest)
    denominator = jnp.sum(shifted, axis=-1, keepdims=True)
    probability_low = (shifted / denominator).astype(jnp.bfloat16)
    log_total = highest + jnp.log(denominator)
    context_low = (
        jnp.einsum(
            "phlm,pmhe->plhe", probability_low, value_heads, preferred_element_type=jnp.float32
        )
        .reshape(row_count, D)
        .astype(jnp.bfloat16)
    )
    rows_float = inputs.astype(jnp.float32)
    attended = product(context_low, w_output) + b_output
    first, normed_first, recip_first = layer_norm(rows_float + attended, g_first, s_first)
    first_low = first.astype(jnp.bfloat16)
    inner = product(first_low, w_up) + b_up
    active_low = jax.nn.gelu(inner, approximate=False).astype(jnp.bfloat16)
    branch = product(active_low, w_down) + b_down
    output, normed_second, recip_second = layer_norm(first + branch, g_second, s_second)
    output_low = output.astype(jnp.bfloat16)
    group_out = lax.all_gather(output_low, "narrow", axis=0, tiled=True)
    partial_value, d_second, d_branch, sums_second = transport_step(
        output_low,
        segments,
        row_kind,
        loss_cotangent,
        out_cotangent,
        normed_second,
        jnp.broadcast_to(recip_second, (row_count, 128)),
        g_second.reshape(1, D),
    )
    transport_loss = lax.all_gather(partial_value[:, 0], "narrow", axis=0, tiled=True)
    grad_second_gain, grad_second_shift, grad_down_bias = sums_second[0], sums_second[1], sums_second[2]
    grad_down_weight = product_left(active_low, d_branch)
    d_inner = (product_right(d_branch, w_down) * gelu_slope(inner)).astype(jnp.bfloat16)
    grad_up_bias = jnp.sum(d_inner.astype(jnp.float32), axis=0)
    grad_up_weight = product_left(first_low, d_inner)
    d_first = d_second + product_right(d_inner, w_up)
    d_sum_first, grad_first_gain, grad_first_shift = norm_back(
        d_first, normed_first, recip_first, g_first
    )
    d_attended = d_sum_first.astype(jnp.bfloat16)
    grad_output_bias = jnp.sum(d_attended.astype(jnp.float32), axis=0)
    grad_output_weight = product_left(context_low, d_attended)
    d_context = product_right(d_attended, w_output).astype(jnp.bfloat16).reshape(shape_heads)
    probability = jnp.exp(attention_scores() - log_total)
    prob_again = probability.astype(jnp.bfloat16)
    d_values = (
        jnp.einsum("phlm,plhe->pmhe", prob_again, d_context, preferred_element_type=jnp.float32)
        .astype(jnp.bfloat16)
        .reshape(row_count, D)
    )
    d_probability = jnp.einsum(
        "plhe,pmhe->phlm", d_context, value_heads, preferred_element_type=jnp.float32
    )
    d_scores = (
        probability * (d_probability - jnp.sum(probability * d_probability, axis=-1, keepdims=True))
    ).astype(jnp.bfloat16)
    d_query = (
        (
            jnp.einsum("phlm,pmhe->plhe", d_scores, key_heads, preferred_element_type=jnp.float32)
            * scale
        )
        .astype(jnp.bfloat16)
        .reshape(row_count, D)
    )
    d_keys = (
        (
            jnp.einsum("phlm,plhe->pmhe", d_scores, query_heads, preferred_element_type=jnp.float32)
            * scale
        )
        .astype(jnp.bfloat16)
        .reshape(row_count, D)
    )
    grad_query_weight = product_left(inputs, d_query)
    grad_query_bias = jnp.sum(d_query.astype(jnp.float32), axis=0)
    grad_key_weight = product_left(inputs, d_keys)
    grad_value_weight = product_left(inputs, d_values)
    grad_value_bias = jnp.sum(d_values.astype(jnp.float32), axis=0)
    grad_inputs = (
        d_sum_first
        + product_right(d_query, w_query)
        + product_right(d_keys, w_key)
        + product_right(d_values, w_value)
    )
    grads = (grad_query_weight, grad_key_weight, grad_value_weight, grad_output_weight, grad_up_weight, grad_down_weight)
    sums = (
        grad_query_bias,
        grad_value_bias,
        grad_output_bias,
        grad_first_gain,
        grad_first_shift,
        grad_down_bias,
        grad_second_gain,
        grad_second_shift,
        grad_up_bias,
    )
    if direct:
        small = jnp.stack([jnp.pad(item.reshape(dp, D // dp), ((0, 0), (0, 128 - D // dp))) for item in sums[:8]], axis=1)
        packed = jnp.concatenate([small, sums[8].reshape(dp, 3, 128), jnp.zeros((dp, 5, 128), jnp.float32)], axis=1)
        out = scatter_grads([item.astype(jnp.bfloat16) for item in grads], packed.astype(jnp.bfloat16), dp, narrow)
        mats, vec = out[:6], out[6]
        vecs = [vec[i, : D // dp] for i in range(8)] + [vec[8:11].reshape(4 * D // dp)]
    else:
        mats, vecs = reduce_grads(grads, sums)
    return (
        group_out,
        transport_loss,
        grad_inputs,
        mats[0],
        vecs[0],
        mats[1],
        mats[2],
        vecs[1],
        mats[3],
        vecs[2],
        vecs[3],
        vecs[4],
        mats[4],
        vecs[8],
        mats[5],
        vecs[5],
        vecs[6],
        vecs[7],
    )


def solution(mesh):
    return jax.shard_map(
        per_device,
        mesh=mesh,
        in_specs=(
            P(("dp", "narrow"), None),
            P("dp", None),
            P("dp", None),
            P("dp", "narrow"),
            P("dp"),
            P("dp", "narrow"),
            P("dp", "narrow"),
            P("dp"),
            P("dp", "narrow"),
            P("dp"),
            P("dp"),
            P("dp"),
            P("dp", "narrow"),
            P("dp"),
            P("dp", "narrow"),
            P("dp"),
            P("dp"),
            P("dp"),
            P(("dp", "narrow"), None),
            P("dp"),
        ),
        out_specs=(
            P("dp", None),
            P("dp"),
            P(("dp", "narrow"), None),
            P("dp", "narrow"),
            P("dp"),
            P("dp", "narrow"),
            P("dp", "narrow"),
            P("dp"),
            P("dp", "narrow"),
            P("dp"),
            P("dp"),
            P("dp"),
            P("dp", "narrow"),
            P("dp"),
            P("dp", "narrow"),
            P("dp"),
            P("dp"),
            P("dp"),
        ),
        check_vma=False,
    )
```

```python
import functools

import jax
import jax.numpy as jnp
from jax import lax
from jax.experimental import pallas as pl
from jax.experimental.pallas import tpu as pltpu
from jax.sharding import PartitionSpec as P

D = 768
HEADS = 12
HEAD_DIM = 64
LEN = 256
ITERS = 20
ROWS = 32
VMEM_LIMIT = 62 * 1024 * 1024

EPS_NORM = 1e-06
BETA = 0.5
MASKED = -1e30


def product(left, right):
    return jnp.dot(left, right, preferred_element_type=jnp.float32)


def product_left(left, right):
    return lax.dot_general(
        left, right, (((0,), (0,)), ((), ())), preferred_element_type=jnp.float32
    )


def product_right(left, right):
    return lax.dot_general(
        left, right, (((1,), (1,)), ((), ())), preferred_element_type=jnp.float32
    )


def fetch_weights(matrices, vectors):
    wide = [lax.all_gather(item, "narrow", axis=1, tiled=True) for item in matrices]
    query, keys, values, output, up, down = [lax.all_gather(item, "dp", axis=0, tiled=True) for item in wide]
    vecs = [lax.all_gather(item, "dp", axis=0, tiled=True).astype(jnp.float32) for item in vectors]
    up = up.reshape(GRID[0], BLOCK, GRID[1], 6, 128).transpose(0, 2, 3, 1, 4).reshape(*GRID, 6 * BLOCK, 128)
    small = jnp.pad(jnp.stack(vecs[:8]), ((0, 8), (0, 128)))
    tiles = jnp.pad(vecs[8].reshape(24, 128), ((0, 8), (0, 0)))
    return (jnp.concatenate([query, keys, values, output]), up, down, small, tiles)


def reduce_grads(matrices, vectors):
    reduced = [lax.psum_scatter(item, "dp", scatter_dimension=0, tiled=True) for item in matrices]
    sums = [lax.psum_scatter(item, "dp", scatter_dimension=0, tiled=True) for item in vectors]
    return (
        [
            lax.psum_scatter(
                item.astype(jnp.bfloat16), "narrow", scatter_dimension=1, tiled=True
            ).astype(jnp.float32)
            for item in reduced
        ],
        lax.psum(sums, "narrow"),
    )


MESH = pl.DeviceIdType.MESH
FF = 4 * D
VEC, SQUARE, UP, DOWN, TOTAL = 0, 16, 592, 1168, 1744
STEP, PART, STEPS = 288, 144, 6
GRID = (8, 4)
BLOCK = D // GRID[0]


def hops():
    dp, narrow = lax.axis_index("dp"), lax.axis_index("narrow")
    return (dp // 2, lax.rem(dp, 2), narrow // 2, lax.rem(narrow, 2))


def place(me, depth, item, order):
    s, a, b, c = item
    z, x, y, core = me
    dx, dy = (a, b) if order == "x" else (b, a)
    z = z if s == 0 else lax.rem(z + s + depth, depth)
    x = 1 - x if dx else x
    y = 1 - y if dy else y
    core = 1 - core if c else core
    return (2 * z + x, 2 * y + core)


def greet(me, depth):
    peers = [place(me, depth, (s, 0, 0, 0), "x") for s in range(1, depth)]
    peers += [place(me, depth, (0, *bits), "x") for bits in ((1, 0, 0), (0, 1, 0), (0, 0, 1))]
    barrier = pltpu.get_barrier_semaphore()
    for peer in peers:
        pl.semaphore_signal(barrier, inc=1, device_id=peer, device_id_type=MESH)
    pl.semaphore_wait(barrier, len(peers))


def number(item):
    s, a, b, c = item
    return ((s * 2 + a) * 2 + b) * 2 + c


def chunks_of(step):
    first = SQUARE + step * STEP
    return ((2 * step, first, PART, "x"), (2 * step + 1, first + PART, STEP - PART, "y"))


VEC_CHUNK = (2 * STEPS, 0, SQUARE, "x")


class Gather:
    def __init__(self, land, send_sem, recv_sem):
        self.land, self.send_sem, self.recv_sem = land, send_sem, recv_sem
        self.me = hops()
        self.depth = land.shape[0] // 2

    def copy(self, chunk, item, hop, at):
        row, first, rows, order = chunk
        s, a, b, c = item
        source = place(self.me, self.depth, (-s, a, b, c), order)
        block = self.land.at[source[0], source[1], pl.ds(first, rows), :]
        return pltpu.make_async_remote_copy(
            src_ref=block,
            dst_ref=block,
            send_sem=self.send_sem.at[row, number(at)],
            recv_sem=self.recv_sem.at[row, number(at)],
            device_id=place(self.me, self.depth, hop, order),
            device_id_type=MESH,
        )

    def send(self, chunk, item, kinds):
        s, a, b, c = item
        if "z" in kinds:
            for far in range(1, self.depth):
                self.copy(chunk, item, (far, 0, 0, 0), (far, 0, 0, 0)).start()
        if "p" in kinds:
            self.copy(chunk, item, (0, 1, 0, 0), (s, 1, b, c)).start()
        if "q" in kinds:
            self.copy(chunk, item, (0, 0, 1, 0), (s, a, 1, c)).start()
        if "c" in kinds:
            self.copy(chunk, item, (0, 0, 0, 1), (s, a, b, 1)).start()

    def take(self, chunk, item, kinds):
        self.copy(chunk, item, (0, 0, 0, 1), item).wait_recv()
        self.send(chunk, item, kinds)

    def start(self, chunk):
        self.send(chunk, (0, 0, 0, 0), "zpqc")

    def after_z(self, chunk):
        for s in range(1, self.depth):
            self.take(chunk, (s, 0, 0, 0), "pqc")

    def after_p(self, chunk):
        for s in range(self.depth):
            self.take(chunk, (s, 1, 0, 0), "qc")

    def after_q(self, chunk):
        for s in range(self.depth):
            for a in range(2):
                self.take(chunk, (s, a, 1, 0), "c")

    def after_c(self, chunk):
        for s in range(self.depth):
            for a in range(2):
                for b in range(2):
                    self.take(chunk, (s, a, b, 1), "")

    def drain(self, chunk):
        for s in range(self.depth):
            for a in range(2):
                for b in range(2):
                    for c in range(2):
                        if s + a + b + c:
                            self.copy(chunk, (0, 0, 0, 0), (0, 0, 0, 1), (s, a, b, c)).wait_send()

    def each(self, stage, step):
        if 0 <= step < STEPS:
            for chunk in chunks_of(step):
                getattr(self, stage)(chunk)

    def slot(self, i):
        for stage, step in (("after_z", i), ("start", i + 2), ("after_p", i - 1), ("after_q", i - 2), ("after_c", i - 3)):
            self.each(stage, step)


def swap(half):
    return pltpu.roll(half, 64, 1)


def left_half(shape):
    return lax.broadcasted_iota(jnp.int32, shape, 1) < 64


def pack_block(block, odd):
    rows = block.shape[0]
    wide = jnp.concatenate([block, jnp.zeros((rows, 64), jnp.float32)], axis=1)
    turned = pltpu.roll(wide, 192, 1)
    main = jnp.where(odd, turned[:, :128], wide[:, :128])
    rest = jnp.where(left_half((rows, 128)), jnp.where(odd, wide[:, :128], wide[:, 128:]), 0.0)
    top, low = rest[: rows // 2], rest[rows // 2 :]
    return main, jnp.where(odd, swap(top) + low, top + swap(low))


def middle_of(even, odd):
    left = left_half(even.shape)
    return jnp.where(left, even, odd), swap(jnp.where(left, odd, even))


def put_block(land, d, at, rows, ref, row):
    half = rows // 2
    for pair in range(GRID[1] // 2):
        even, other = land.at[d, 2 * pair], land.at[d, 2 * pair + 1]
        left = 384 * pair
        ref[pl.ds(row, rows), left : left + 128] = even[at : at + rows, :]
        ref[pl.ds(row, rows), left + 256 : left + 384] = other[at : at + rows, :]
        top, low = middle_of(
            even[at + rows : at + rows + half, :].astype(jnp.float32),
            other[at + rows : at + rows + half, :].astype(jnp.float32),
        )
        ref[pl.ds(row, half), left + 128 : left + 256] = top.astype(jnp.bfloat16)
        ref[pl.ds(row + half, half), left + 128 : left + 256] = low.astype(jnp.bfloat16)


def norm_parts(values):
    centre = values - jnp.mean(values, axis=1, keepdims=True)
    spread = jnp.mean(centre * centre, axis=1, keepdims=True)
    recip = lax.rsqrt(spread + EPS_NORM)
    return centre * recip, recip


def gelu_parts(z):
    size = jnp.abs(z)
    base = 1.0 + 0.2316419 * size
    t = pl.reciprocal(base, approx=True)
    t = t * (2.0 - base * t)
    density = jnp.exp(z * z * -0.5) * 0.3989422804014327
    poly = t * (0.319381530 + t * (-0.356563782 + t * (1.781477937 + t * (-1.821255978 + t * 1.330274429))))
    tail = poly * density
    cdf = jnp.where(z < 0.0, tail, 1.0 - tail)
    return z * cdf, cdf + z * density


def forward_kernel(direct, *refs):
    if direct:
        q_ref, k_ref, v_ref, o_ref, upw_ref, downw_ref, small_ref = refs[:7]
        refs = refs[7:]
    else:
        square_in, up_in, down_in, vec_in, bup_in = refs[:5]
        refs = refs[5:]
    in_ref, seg_ref = refs[:2]
    (square_out, up_out, down_out, vec_ref, qkv_out, prob_out, turned_out, norm1_out, recip1_out,
     act_out, slope_out, mixed_out, norm2_out, recip2_out) = refs[2:16]
    (land, square, down, bup, qkv, prob, turned, ctx, first, flow, norm, recip, act, slope, act_turned, mixed,
     out_sem, pack_sem, tile_sem) = refs[16:35]
    packs = in_ref.shape[0] // LEN
    base = lax.axis_index("narrow") * packs
    pending = {}

    def save(name, src, dst):
        pending[name] = pltpu.make_async_copy(src, dst, out_sem.at[len(pending)])
        pending[name].start()

    if direct:
        send_sem, recv_sem = refs[35:37]
        dp, narrow = lax.axis_index("dp"), lax.axis_index("narrow")
        odd = lax.rem(narrow, 2) == 1
        own = land.at[dp, narrow]
        own[0:16, :] = small_ref[...]
        for i, ref in enumerate((q_ref, k_ref, v_ref, o_ref)):
            main, rest = pack_block(ref[...].astype(jnp.float32), odd)
            at = SQUARE + PART * i
            own[at : at + BLOCK, :] = main.astype(jnp.bfloat16)
            own[at + BLOCK : at + PART, :] = rest.astype(jnp.bfloat16)
        g = Gather(land, send_sem, recv_sem)
        greet(g.me, g.depth)
        g.start(VEC_CHUNK)
        g.each("start", 0)
        g.each("start", 1)
        for t in range(6):
            own[UP + BLOCK * t : UP + BLOCK * (t + 1), :] = upw_ref[:, 128 * t : 128 * (t + 1)]
        main, rest = pack_block(downw_ref[...].astype(jnp.float32), odd)
        own[DOWN : DOWN + 384, :] = main.astype(jnp.bfloat16)
        own[DOWN + 384 : DOWN + 576, :] = rest.astype(jnp.bfloat16)
        g.after_z(VEC_CHUNK)
        g.slot(0)
        g.after_p(VEC_CHUNK)
        g.slot(1)
        g.after_q(VEC_CHUNK)
        g.slot(2)
        g.after_c(VEC_CHUNK)
        g.slot(3)
        vec_ref[...] = jnp.zeros_like(vec_ref)
        for d in range(GRID[0]):
            tile = land[d, 0, 0:16, :].astype(jnp.float32)
            wide = jnp.concatenate([tile, jnp.zeros((16, 128), jnp.float32)], axis=1)
            at, shift = divmod(BLOCK * d, 128)
            wide = pltpu.roll(wide, shift, 1) if shift else wide
            vec_ref[:, 128 * at : 128 * at + 256] += wide
            bup[3 * d : 3 * d + 3, :] = tile[8:11]
            for i in range(2):
                put_block(land, d, SQUARE + PART * i, BLOCK, square, D * i + BLOCK * d)
        g.slot(4)
        for d in range(GRID[0]):
            for i in range(2, 4):
                put_block(land, d, SQUARE + PART * i, BLOCK, square, D * i + BLOCK * d)

        def tick(loop, index, pieces):
            for when, stage, step in pieces:
                pl.when(index == when)(lambda: g.each(stage, step))
    else:
        fills = [
            pltpu.make_async_copy(src, dst, out_sem.at[i])
            for i, (src, dst) in enumerate(
                ((square_in, square), (down_in, down), (up_in, land.at[:, :, pl.ds(UP, DOWN - UP), :]))
            )
        ]
        for copy in fills:
            copy.start()
        vec_ref[...] = vec_in[...]
        bup[...] = bup_in[...]
        for copy in fills:
            copy.wait()
        tick = lambda loop, index, pieces: None
    save("square", square, square_out)

    def pack_copies(p):
        k = p % 2
        at = pl.ds(pl.multiple_of(p * LEN, LEN), LEN)
        return [
            pltpu.make_async_copy(prob.at[k], prob_out.at[p], pack_sem.at[0, k]),
            pltpu.make_async_copy(qkv.at[k], qkv_out.at[at, :], pack_sem.at[1, k]),
            pltpu.make_async_copy(turned.at[k], turned_out.at[:, :, at], pack_sem.at[2, k]),
        ]

    def attend(p, carry):
        rows = pl.ds(pl.multiple_of(p * LEN, LEN), LEN)
        k = p % 2

        @pl.when(p >= 2)
        def _():
            for copy in pack_copies(p - 2):
                copy.wait()

        x = in_ref[rows, :]
        turned[k, 0] = jnp.transpose(x)
        for i in range(3):
            part = product(x, square[D * i : D * (i + 1), :])
            if i != 1:
                part = part + vec_ref[i // 2 : i // 2 + 1, :D]
            qkv[k, :, D * i : D * (i + 1)] = part.astype(jnp.bfloat16)
        tick("attend", p, ((0, "after_z", 5), (1, "after_q", 3), (2, "after_p", 5)))
        seg_row = seg_ref[pl.ds(base + p, 1), :].astype(jnp.float32)
        seg_col = jnp.transpose(jnp.broadcast_to(seg_row, (128, LEN)))
        same = jnp.concatenate([seg_col, seg_col], axis=1) == seg_row
        left = left_half((LEN, 128))
        for h in range(HEADS // 2):
            columns = slice(128 * h, 128 * (h + 1))
            query = qkv[k, :, columns] * jnp.asarray(HEAD_DIM**-0.5, jnp.bfloat16)
            keys = qkv[k, :, D + 128 * h : D + 128 * (h + 1)]
            values = qkv[k, :, 2 * D + 128 * h : 2 * D + 128 * (h + 1)]
            mixes = []
            for side in range(2):
                mine = left if side == 0 else jnp.logical_not(left)
                scores = product_right(jnp.where(mine, query, jnp.zeros_like(query)), keys)
                scores = jnp.where(same, scores, MASKED)
                shifted = jnp.exp(scores - jnp.max(scores, axis=1, keepdims=True))
                total = jnp.sum(shifted, axis=1, keepdims=True)
                low = (shifted * (1.0 / total)).astype(jnp.bfloat16)
                prob[k, 2 * h + side] = low
                mixes.append(product(low, values))
            ctx[:, columns] = jnp.where(left, mixes[0], mixes[1]).astype(jnp.bfloat16)
            if h == 3:
                tick("attend", p, ((0, "after_p", 4), (1, "after_c", 2), (2, "after_q", 4), (3, "after_c", 3)))
        turned[k, 1] = jnp.transpose(ctx[...])
        total = x.astype(jnp.float32) + (product(ctx[...], square[3 * D :, :]) + vec_ref[2:3, :D])
        normed, scale = norm_parts(total)
        value = normed * vec_ref[3:4, :D] + vec_ref[4:5, :D]
        first[rows, :] = value
        low = value.astype(jnp.bfloat16)
        flow[rows, :] = low
        turned[k, 2] = jnp.transpose(low)
        norm[rows, :] = normed
        recip[0, rows, :] = jnp.broadcast_to(scale, (LEN, 128))
        for copy in pack_copies(p):
            copy.start()
        return carry

    lax.fori_loop(0, packs, attend, 0)
    save("norm", norm, norm1_out)
    save("recip", recip.at[0], recip1_out)
    for p in (packs - 2, packs - 1):
        for copy in pack_copies(p):
            copy.wait()

    def tile_copies(t):
        k = t % 2
        copies = []
        for n in range(GRID[1]):
            columns = pl.ds(pl.multiple_of(D * n + 128 * t, 128), 128)
            first_row = pl.multiple_of(UP + BLOCK * t, 16)
            copies += [
                pltpu.make_async_copy(slope.at[k, n], slope_out.at[:, columns], tile_sem.at[0, k, n]),
                pltpu.make_async_copy(act_turned.at[k, n], act_out.at[columns, :], tile_sem.at[1, k, n]),
                pltpu.make_async_copy(
                    land.at[:, n, pl.ds(first_row, BLOCK), :], up_out.at[:, :, columns], tile_sem.at[2, k, n]
                ),
            ]
        return copies

    def widen(t, carry):
        k = t % 2

        @pl.when(t >= 2)
        def _():
            for copy in tile_copies(t - 2):
                copy.wait()

        first_row = pl.multiple_of(UP + BLOCK * t, 16)
        for pair in range(2):
            weight = jnp.concatenate(
                [land[:, 2 * pair + i, pl.ds(first_row, BLOCK), :].reshape(D, 128) for i in range(2)], axis=1
            )
            bias = jnp.concatenate([bup[pl.ds(6 * (2 * pair + i) + t, 1), :] for i in range(2)], axis=1)
            for r in range(packs):
                rows = slice(LEN * r, LEN * (r + 1))
                value, turn = gelu_parts(product(flow[rows, :], weight) + bias)
                value, turn = value.astype(jnp.bfloat16), turn.astype(jnp.bfloat16)
                back = jnp.transpose(value)
                for i in range(2):
                    n = 2 * pair + i
                    columns = pl.ds(pl.multiple_of(D * n + 128 * t, 128), 128)
                    act[rows, columns] = value[:, 128 * i : 128 * (i + 1)]
                    act_turned[k, n, :, rows] = back[128 * i : 128 * (i + 1), :]
                    slope[k, n, rows, :] = turn[:, 128 * i : 128 * (i + 1)]
        tick("widen", t, ((0, "after_q", 5), (1, "after_c", 4)))
        for copy in tile_copies(t):
            copy.start()
        return carry

    lax.fori_loop(0, 6, widen, 0)
    if direct:
        g.each("after_c", 5)
        for d in range(GRID[0]):
            put_block(land, d, DOWN, 384, down, 384 * d)
    save("down", down, down_out)
    pending["norm"].wait()

    def finish(p, carry):
        rows = pl.ds(pl.multiple_of(p * LEN, LEN), LEN)
        total = first[rows, :] + (product(act[rows, :], down[...]) + vec_ref[5:6, :D])
        normed, scale = norm_parts(total)
        norm[rows, :] = normed
        recip[1, rows, :] = jnp.broadcast_to(scale, (LEN, 128))
        mixed[rows, :] = (normed * vec_ref[6:7, :D] + vec_ref[7:8, :D]).astype(jnp.bfloat16)
        return carry

    lax.fori_loop(0, packs, finish, 0)
    save("mixed", mixed, mixed_out)
    save("norm2", norm, norm2_out)
    save("recip2", recip.at[1], recip2_out)
    for t in (4, 5):
        for copy in tile_copies(t):
            copy.wait()
    if direct:
        for chunk in [VEC_CHUNK] + [chunk for step in range(STEPS) for chunk in chunks_of(step)]:
            g.drain(chunk)
    for name, copy in pending.items():
        if name != "norm":
            copy.wait()


def forward_step(direct, weights, inputs, segments, dp, narrow):
    rows = inputs.shape[0]
    packs = rows // LEN
    vmem = pl.BlockSpec(memory_space=pltpu.VMEM)
    anywhere = pl.BlockSpec(memory_space=pl.ANY)
    low = lambda *shape: jax.ShapeDtypeStruct(shape, jnp.bfloat16)
    full = lambda *shape: jax.ShapeDtypeStruct(shape, jnp.float32)
    room = lambda *shape: pltpu.VMEM(shape, jnp.bfloat16)
    wide = lambda *shape: pltpu.VMEM(shape, jnp.float32)
    sems = [pltpu.SemaphoreType.DMA((2 * STEPS + 1, 32))] * 2 if direct else []
    return pl.pallas_call(
        functools.partial(forward_kernel, direct),
        name="forward",
        out_shape=(
            low(FF, D), low(GRID[0], BLOCK, FF), low(FF, D), full(16, 896),
            low(rows, 3 * D), low(packs, HEADS, LEN, LEN), low(3, D, rows), full(rows, D), full(rows, 128),
            low(FF, rows), low(rows, FF), low(rows, D), full(rows, D), full(rows, 128),
        ),
        in_specs=([vmem] * 7 if direct else [anywhere] * 3 + [vmem] * 2) + [vmem] * 2,
        out_specs=(anywhere,) * 3 + (vmem,) + (anywhere,) * 10,
        scratch_shapes=[
            room(*GRID, TOTAL, 128), room(FF, D), room(FF, D), wide(32, 128),
            room(2, LEN, 3 * D), room(2, HEADS, LEN, LEN), room(2, 3, D, LEN), room(LEN, D), wide(rows, D), room(rows, D),
            wide(rows, D), wide(2, rows, 128), room(rows, FF), room(2, 4, rows, 128), room(2, 4, 128, rows), room(rows, D),
            pltpu.SemaphoreType.DMA((12,)), pltpu.SemaphoreType.DMA((3, 2)), pltpu.SemaphoreType.DMA((3, 2, 4)),
            *sems,
        ],
        compiler_params=pltpu.CompilerParams(
            vmem_limit_bytes=VMEM_LIMIT, **(dict(collective_id=0, has_side_effects=True) if direct else {})
        ),
    )(*weights, inputs, segments)


def transport_kernel(
    mixed_ref, seg_ref, kind_ref, weight_ref, cot_ref, normed_ref, recip_ref, gain_ref,
    value_ref, second_ref, branch_ref, sums_ref,
    kern_ref, prod_ref, flow_ref, acc_ref, left_ref, sigma_ref,
):
    packs = mixed_ref.shape[0] // LEN
    base = lax.axis_index("narrow") * packs
    blocks = LEN // ROWS
    lanes = lambda col: jnp.concatenate([col, col], axis=1)
    fold = lambda wide: wide[:, :128] + wide[:, 128:]
    eight = lambda wide: jnp.sum(wide.reshape(ROWS // 8, 8, LEN), axis=0)
    replicate = lambda col: jnp.broadcast_to(col, (ROWS, 128))

    def turned(row):
        return jnp.transpose(jnp.broadcast_to(row, (128, LEN)))

    for p in range(packs):
        rows = pl.ds(p * LEN, LEN)
        feats = mixed_ref[rows, :].astype(jnp.float32)
        recip = lax.rsqrt(jnp.sum(feats * feats, axis=1, keepdims=True) + EPS_NORM)
        unit = (feats * recip).astype(jnp.bfloat16)
        cosine = product_right(unit, unit)
        seg_row = seg_ref[pl.ds(base + p, 1), :].astype(jnp.float32)
        region_row = jnp.where(kind_ref[pl.ds(base + p, 1), :] == 0, 0.0, 1.0)
        seg_col = turned(seg_row)
        word_col = 1.0 - turned(region_row)
        same = jnp.where(lanes(seg_col) == seg_row, 1.0, 0.0)
        word_count = jnp.sum(same * (1.0 - region_row), axis=1, keepdims=True)
        region_count = jnp.sum(same * lanes(1.0 - word_col), axis=0, keepdims=True)
        kern_ref[p] = jnp.exp((cosine - 1.0) * (1.0 / BETA)) * same * lanes(word_col) * region_row
        left_ref[p, 0] = word_col
        left_ref[p, 1] = jnp.broadcast_to(word_count, (LEN, 128))
        prod_ref[0, p] = jnp.ones((LEN, LEN), jnp.float32)
        sigma_ref[0, p, 0:1] = region_row / region_count
        sigma_ref[0, p, 1:2] = region_row
        sigma_ref[0, p, 2:3] = region_count

    def advance(t, carry):
        for p in range(packs):
            sigma = sigma_ref[t, p, 0:1]
            scale = jnp.where(t == 0, 1.0, sigma)
            region = sigma_ref[0, p, 1:2]
            count = sigma_ref[0, p, 2:3]
            total = jnp.zeros((8, LEN), jnp.float32)
            for b in range(blocks):
                rows = pl.ds(b * ROWS, ROWS)
                weighted = kern_ref[p, rows, :] * (prod_ref[t, p, rows, :] * scale)
                row_sum = jnp.sum(fold(weighted * sigma), axis=1, keepdims=True)
                word = left_ref[p, 0, rows, :]
                delta = word / (left_ref[p, 1, rows, :] * replicate(row_sum) + 1.0 - word)
                scaled = weighted * lanes(delta)
                prod_ref[t + 1, p, rows, :] = scaled
                total = total + eight(scaled)
            col_sum = jnp.sum(total, axis=0, keepdims=True)
            sigma_ref[t + 1, p, 0:1] = region / (count * col_sum + 1.0 - region)
        return carry

    lax.fori_loop(0, ITERS, advance, 0)

    starts = []
    for p in range(packs):
        rows = pl.ds(p * LEN, LEN)
        weight = weight_ref[base + p]
        feats = mixed_ref[rows, :].astype(jnp.float32)
        recip = lax.rsqrt(jnp.sum(feats * feats, axis=1, keepdims=True) + EPS_NORM)
        unit = (feats * recip).astype(jnp.bfloat16)
        cosine = product_right(unit, unit)
        moved = (prod_ref[ITERS, p] * sigma_ref[ITERS, p, 0:1]) * (1.0 - cosine)
        value_ref[p : p + 1, :] = jnp.broadcast_to(jnp.sum(moved), (1, 128))
        moved = moved * weight
        flow_ref[p] = moved
        acc_ref[p] = jnp.zeros((LEN, LEN), jnp.float32)
        starts += [jnp.sum(moved, axis=0, keepdims=True), jnp.zeros((1, LEN), jnp.float32)]

    def retreat(step, carry):
        t = ITERS - 1 - step
        out = []
        for p in range(packs):
            flow_sum, spread = carry[2 * p : 2 * p + 2]
            before = sigma_ref[t, p, 0:1]
            d_col = -sigma_ref[0, p, 2:3] * sigma_ref[t + 1, p, 0:1] * (spread + flow_sum)
            total = jnp.zeros((8, LEN), jnp.float32)
            shift = jnp.zeros((8, LEN), jnp.float32)
            for b in range(blocks):
                rows = pl.ds(b * ROWS, ROWS)
                scaled = prod_ref[t + 1, p, rows, :]
                flow = flow_ref[p, rows, :] + scaled * d_col
                d_row = replicate(jnp.sum(fold(flow), axis=1, keepdims=True))
                d_row = -left_ref[p, 1, rows, :] * d_row
                moved = scaled * lanes(d_row)
                flow = flow + moved * before
                flow_ref[p, rows, :] = flow
                acc_ref[p, rows, :] = acc_ref[p, rows, :] + flow
                total = total + eight(flow)
                shift = shift + eight(moved)
            out += [
                jnp.sum(total, axis=0, keepdims=True),
                before * jnp.sum(shift, axis=0, keepdims=True),
            ]
        return tuple(out)

    lax.fori_loop(0, ITERS, retreat, tuple(starts))

    sums = [jnp.zeros((1, D), jnp.float32)] * 3
    for p in range(packs):
        rows = pl.ds(p * LEN, LEN)
        coupling = prod_ref[ITERS, p] * sigma_ref[ITERS, p, 0:1]
        d_cost = weight_ref[base + p] * coupling - acc_ref[p] * (1.0 / BETA)
        d_cosine = (-d_cost).astype(jnp.bfloat16)
        feats = mixed_ref[rows, :].astype(jnp.float32)
        recip = lax.rsqrt(jnp.sum(feats * feats, axis=1, keepdims=True) + EPS_NORM)
        unit = feats * recip
        unit_low = unit.astype(jnp.bfloat16)
        d_unit = product(d_cosine, unit_low) + product_left(d_cosine, unit_low)
        d_mixed = cot_ref[rows, :].astype(jnp.float32) + recip * (
            d_unit - unit * jnp.sum(d_unit * unit, axis=1, keepdims=True)
        )
        normed = normed_ref[rows, :]
        scaled = d_mixed * gain_ref[...]
        inner_mean = jnp.mean(scaled, axis=1, keepdims=True)
        cross_mean = jnp.mean(scaled * normed, axis=1, keepdims=True)
        d_second = recip_ref[rows, 0:1] * (scaled - inner_mean - normed * cross_mean)
        d_branch = d_second.astype(jnp.bfloat16)
        second_ref[rows, :] = d_second
        branch_ref[rows, :] = d_branch
        sums[0] = sums[0] + jnp.sum(d_mixed * normed, axis=0, keepdims=True)
        sums[1] = sums[1] + jnp.sum(d_mixed, axis=0, keepdims=True)
        sums[2] = sums[2] + jnp.sum(d_branch.astype(jnp.float32), axis=0, keepdims=True)
    for k in range(3):
        sums_ref[k : k + 1, :] = sums[k]


def transport_step(mixed, segments, row_kind, weight, cotangent, normed, recip, gain):
    rows = mixed.shape[0]
    packs = rows // LEN
    vmem = pl.BlockSpec(memory_space=pltpu.VMEM)
    square = (packs, LEN, LEN)
    return pl.pallas_call(
        transport_kernel,
        name="transport",
        out_shape=(
            jax.ShapeDtypeStruct((packs, 128), jnp.float32),
            jax.ShapeDtypeStruct((rows, D), jnp.float32),
            jax.ShapeDtypeStruct((rows, D), jnp.bfloat16),
            jax.ShapeDtypeStruct((8, D), jnp.float32),
        ),
        in_specs=[vmem, vmem, vmem, pl.BlockSpec(memory_space=pltpu.SMEM), vmem, vmem, vmem, vmem],
        out_specs=(vmem, vmem, vmem, vmem),
        scratch_shapes=[
            pltpu.VMEM(square, jnp.float32),
            pltpu.VMEM((ITERS + 1, *square), jnp.float32),
            pltpu.VMEM(square, jnp.float32),
            pltpu.VMEM(square, jnp.float32),
            pltpu.VMEM((packs, 2, LEN, 128), jnp.float32),
            pltpu.VMEM((ITERS + 1, packs, 8, LEN), jnp.float32),
        ],
        compiler_params=pltpu.CompilerParams(vmem_limit_bytes=VMEM_LIMIT),
    )(mixed, segments, row_kind, weight, cotangent, normed, recip, gain)


class Scatter:
    def __init__(self, part, lands, send_sem, recv_sem, credit):
        self.part, self.lands, self.send_sem, self.recv_sem, self.credit = part, lands, send_sem, recv_sem, credit
        self.me = hops()
        self.depth = part.shape[0] // 2

    def block(self, chunk, item):
        row, first, rows, order = chunk
        owner = place(self.me, self.depth, item, order)
        return self.part.at[owner[0], owner[1], pl.ds(first, rows), :]

    def landing(self, chunk, item):
        row, first, rows, order = chunk
        s, a, b, c = item
        span = pl.ds(first, rows)
        if c:
            step, at = divmod(first - SQUARE, STEP) if first else (2, 0)
            slot = (step % 2) * STEP + at if first else 2 * STEP
            return self.lands[0].at[(s * 2 + a) * 2 + b, pl.ds(slot, rows), :]
        if b:
            return self.lands[1].at[s * 2 + a, span, :]
        if a:
            return self.lands[2].at[s, span, :]
        return self.lands[3].at[s - 1, span, :]

    def copy(self, chunk, item):
        s, a, b, c = item
        hop = (0, 0, 0, 1) if c else (0, 0, 1, 0) if b else (0, 1, 0, 0) if a else (s, 0, 0, 0)
        return pltpu.make_async_remote_copy(
            src_ref=self.block(chunk, item),
            dst_ref=self.landing(chunk, item),
            send_sem=self.send_sem.at[chunk[0], number(item)],
            recv_sem=self.recv_sem.at[chunk[0], number(item)],
            device_id=place(self.me, self.depth, hop, chunk[3]),
            device_id_type=MESH,
        )

    def take(self, chunk, item, into):
        self.copy(chunk, item).wait_recv()
        ref = self.block(chunk, into)
        ref[...] = (
            ref[...].astype(jnp.float32) + self.landing(chunk, item)[...].astype(jnp.float32)
        ).astype(jnp.bfloat16)

    def start(self, chunk):
        for s in range(self.depth):
            for a in range(2):
                for b in (1, 0):
                    self.copy(chunk, (s, a, b, 1)).start()

    def after_c(self, chunk):
        for b in (1, 0):
            for s in range(self.depth):
                for a in range(2):
                    self.take(chunk, (s, a, b, 1), (s, a, b, 0))
                    if b:
                        self.copy(chunk, (s, a, 1, 0)).start()

    def after_q(self, chunk):
        for a in (1, 0):
            for s in range(self.depth):
                self.take(chunk, (s, a, 1, 0), (s, a, 0, 0))
                if a:
                    self.copy(chunk, (s, 1, 0, 0)).start()

    def after_p(self, chunk):
        for s in [*range(1, self.depth), 0]:
            self.take(chunk, (s, 1, 0, 0), (s, 0, 0, 0))
            if s:
                self.copy(chunk, (s, 0, 0, 0)).start()

    def finish(self, chunk, total):
        for s in range(1, self.depth):
            self.copy(chunk, (s, 0, 0, 0)).wait_recv()
        value = self.block(chunk, (0, 0, 0, 0))[...].astype(jnp.float32)
        for s in range(1, self.depth):
            value = value + self.landing(chunk, (s, 0, 0, 0))[...].astype(jnp.float32)
        total[pl.ds(chunk[1], chunk[2]), :] = value

    def drain(self, chunk):
        for s in range(self.depth):
            for a in range(2):
                for b in range(2):
                    for c in range(2):
                        if s + a + b + c:
                            self.copy(chunk, (s, a, b, c)).wait_send()

    def tick(self, stage, step, total):
        if stage == "start" and step < STEPS - 2:
            pl.semaphore_wait(self.credit, 1)
        for chunk in chunks_of(step):
            if stage == "finish":
                self.finish(chunk, total)
            else:
                getattr(self, stage)(chunk)
        if stage == "after_c" and step >= 2:
            other = place(self.me, self.depth, (0, 0, 0, 1), "x")
            pl.semaphore_signal(self.credit, inc=1, device_id=other, device_id_type=MESH)


def fold_middle(top, low):
    left = left_half(top.shape)
    return jnp.where(left, top, swap(low)), jnp.where(left, swap(low), top)


def take_block(part, d, at, rows, block, pair):
    even, other = part.at[d, 2 * pair], part.at[d, 2 * pair + 1]
    half = rows // 2
    even[at : at + rows, :] = block[:, :128].astype(jnp.bfloat16)
    other[at : at + rows, :] = block[:, 256:].astype(jnp.bfloat16)
    one, two = fold_middle(block[:half, 128:256], block[half:, 128:256])
    even[at + rows : at + rows + half, :] = one.astype(jnp.bfloat16)
    other[at + rows : at + rows + half, :] = two.astype(jnp.bfloat16)


def unpack_block(main, rest, odd):
    other = swap(rest)
    top, low = jnp.where(odd, other, rest), jnp.where(odd, rest, other)
    piece = jnp.concatenate([top, low], axis=0)
    left = left_half(piece.shape)
    swapped = swap(main)
    first = jnp.where(odd, jnp.where(left, piece, swapped), main)
    second = jnp.where(odd, swapped, piece)
    return jnp.concatenate([first, second[:, :64]], axis=1)


def backward_kernel(direct, *refs):
    (act_in, slope_in, branch_in, second_in, sums_in, turned_in, norm_in, recip_in, qkv_in, prob_in,
     square_in, up_in, down_in, vec_ref) = refs[:14]
    refs = refs[14:]
    if direct:
        grad_in_out, gq_ref, gk_ref, gv_ref, go_ref, gup_ref, gdown_ref, gvec_ref = refs[:8]
        refs = refs[8:]
    else:
        grad_in_out, gsquare_ref, gup_ref, gdown_ref, gvec_ref, gbup_ref = refs[:6]
        refs = refs[6:]
    turned, slope, square, up, flow, norm, recip, branch, prob, sums, bup, load_sem, prob_sem, out_sem = refs[:14]
    rows_all = slope.shape[0]
    packs = rows_all // LEN
    if direct:
        part, land_c, land_q, land_p, land_z, total, send_sem, recv_sem, credit = refs[14:23]
        g = Scatter(part, (land_c, land_q, land_p, land_z), send_sem, recv_sem, credit)
        odd = lax.rem(lax.axis_index("narrow"), 2) == 1
    else:
        (stage,) = refs[14:15]

    loads = {}

    def load(name, src, dst):
        loads[name] = pltpu.make_async_copy(src, dst, load_sem.at[len(loads)])
        loads[name].start()

    load("branch", branch_in, branch)
    load("act", act_in, turned)
    load("down", down_in, square)
    load("slope", slope_in, slope)
    load("up", up_in, up)
    load("flow", second_in, flow)
    load("norm", norm_in, norm)
    load("recip", recip_in, recip)
    if direct:
        greet(g.me, g.depth)

    def tick(index, pieces):
        if direct:
            for when, name, step in pieces:
                if isinstance(index, int):
                    if index == when:
                        g.tick(name, step, total)
                else:
                    pl.when(index == when)(lambda: g.tick(name, step, total))

    sums[...] = jnp.zeros_like(sums)
    bup[...] = jnp.zeros_like(bup)
    sums[5:6, :D] = sums_in[2:3, :]
    sums[6:7, :D] = sums_in[0:1, :]
    sums[7:8, :D] = sums_in[1:2, :]
    loads["branch"].wait()
    loads["act"].wait()

    def put_down(d, carry):
        at = pl.multiple_of(384 * d, 128)
        grad = product(turned[pl.ds(at, 384), :], branch[...])
        if direct:
            for pair in range(2):
                take_block(part, d, DOWN, 384, grad[:, 384 * pair : 384 * (pair + 1)], pair)
        else:
            stage[0, 0:384, :] = grad
            copy = pltpu.make_async_copy(stage.at[0, pl.ds(0, 384), :], gdown_ref.at[pl.ds(at, 384), :], out_sem.at[0])
            copy.start()
            copy.wait()
        return carry

    lax.fori_loop(0, 8, put_down, 0)
    tick(0, ((0, "start", 5), (0, "start", 4)))
    load("turned", turned_in, turned.at[pl.ds(0, 3 * D), :])
    loads["down"].wait()
    loads["slope"].wait()

    def narrow_down(c, carry):
        at = pl.multiple_of(256 * c, 128)
        columns = pl.ds(at, 256)
        weight = square[pl.ds(at, 256), :]
        column_sum = jnp.zeros((1, 256), jnp.float32)
        for r in range(packs):
            rows = slice(LEN * r, LEN * (r + 1))
            value = product_right(branch[rows, :], weight) * slope[rows, columns].astype(jnp.float32)
            low = value.astype(jnp.bfloat16)
            slope[rows, columns] = low
            column_sum = column_sum + jnp.sum(low.astype(jnp.float32), axis=0, keepdims=True)
        bup[pl.ds(2 * c, 1), :] = column_sum[:, :128]
        bup[pl.ds(2 * c + 1, 1), :] = column_sum[:, 128:]
        tick(c, ((3, "after_c", 5), (6, "after_c", 4)))
        return carry

    lax.fori_loop(0, 12, narrow_down, 0)
    load("square", square_in, square)
    loads["turned"].wait()

    def put_up(i, carry):
        t, pair = i // 2, i % 2
        first_row = pl.multiple_of(UP + BLOCK * t, 16)
        at = [pl.multiple_of(D * (2 * pair + j) + 128 * t, 128) for j in range(2)]
        columns = jnp.concatenate([slope[:, pl.ds(at[j], 128)] for j in range(2)], axis=1)
        grad = product(turned[2 * D : 3 * D, :], columns)
        for j in range(2):
            block = grad[:, 128 * j : 128 * (j + 1)]
            if direct:
                part[:, 2 * pair + j, pl.ds(first_row, BLOCK), :] = block.astype(jnp.bfloat16).reshape(GRID[0], BLOCK, 128)
            else:
                stage[j, :, :128] = block
                copy = pltpu.make_async_copy(stage.at[j, :, pl.ds(0, 128)], gup_ref.at[:, pl.ds(at[j], 128)], out_sem.at[j])
                copy.start()
                copy.wait()
        tick(i, ((6, "after_q", 5),))
        return carry

    lax.fori_loop(0, 12, put_up, 0)
    tick(0, ((0, "start", 3), (0, "start", 2)))
    for name in ("up", "flow", "norm", "recip"):
        loads[name].wait()

    def norm_back(r, carry):
        rows = pl.ds(pl.multiple_of(r * LEN, LEN), LEN)
        d_first = flow[rows, :] + product_right(slope[rows, :], up[...])
        normed = norm[rows, :]
        scaled = d_first * vec_ref[3:4, :D]
        inner_mean = jnp.mean(scaled, axis=1, keepdims=True)
        cross_mean = jnp.mean(scaled * normed, axis=1, keepdims=True)
        d_sum = recip[rows, 0:1] * (scaled - inner_mean - normed * cross_mean)
        flow[rows, :] = d_sum
        low = d_sum.astype(jnp.bfloat16)
        branch[rows, :] = low
        sums[3:4, :D] += jnp.sum(d_first * normed, axis=0, keepdims=True)
        sums[4:5, :D] += jnp.sum(d_first, axis=0, keepdims=True)
        sums[2:3, :D] += jnp.sum(low.astype(jnp.float32), axis=0, keepdims=True)
        tick(r, ((0, "after_c", 3), (2, "after_c", 2), (3, "after_q", 4)))
        return carry

    lax.fori_loop(0, packs, norm_back, 0)
    load("qkv", qkv_in, slope.at[:, pl.ds(0, 3 * D)])

    def put_square(i, left, right):
        for pair in range(2):
            grad = product(left, right[:, 384 * pair : 384 * (pair + 1)])
            if direct:
                for d in range(GRID[0]):
                    take_block(part, d, SQUARE + PART * i, BLOCK, grad[BLOCK * d : BLOCK * (d + 1)], pair)
            else:
                stage[0, :, :384] = grad
                copy = pltpu.make_async_copy(
                    stage.at[0, :, pl.ds(0, 384)], gsquare_ref.at[pl.ds(D * i, D), pl.ds(384 * pair, 384)], out_sem.at[0]
                )
                copy.start()
                copy.wait()

    put_square(3, turned[D : 2 * D, :], branch)
    loads["square"].wait()
    loads["qkv"].wait()
    for r in range(packs):
        rows = slice(LEN * r, LEN * (r + 1))
        slope[rows, 3 * D :] = product_right(branch[rows, :], square[3 * D :, :]).astype(jnp.bfloat16)
    tick(0, ((0, "after_q", 3),))

    def prob_copy(p):
        return pltpu.make_async_copy(prob_in.at[p], prob.at[p % 2], prob_sem.at[p % 2])

    prob_copy(0).start()

    def attend(p, carry):
        rows = pl.ds(pl.multiple_of(p * LEN, LEN), LEN)
        k = p % 2
        pl.when(p + 1 < packs)(lambda: prob_copy(p + 1).start())
        prob_copy(p).wait()
        left = left_half((LEN, 128))
        for h in range(HEADS // 2):
            columns = slice(128 * h, 128 * (h + 1))
            key_columns = slice(D + 128 * h, D + 128 * (h + 1))
            value_columns = slice(2 * D + 128 * h, 2 * D + 128 * (h + 1))
            query, keys, values = slope[rows, columns], slope[rows, key_columns], slope[rows, value_columns]
            d_context = slope[rows, 3 * D + 128 * h : 3 * D + 128 * (h + 1)]
            d_values, d_query, d_keys = [], [], []
            for side in range(2):
                mine = left if side == 0 else jnp.logical_not(left)
                low = prob[k, 2 * h + side]
                d_values.append(product_left(low, d_context))
                d_prob = product_right(jnp.where(mine, d_context, jnp.zeros_like(d_context)), values)
                share = low.astype(jnp.float32)
                moved = share * d_prob
                d_scores = (moved - share * jnp.sum(moved, axis=1, keepdims=True)).astype(jnp.bfloat16)
                d_query.append(product(d_scores, keys))
                d_keys.append(product_left(d_scores, query))
            scale = HEAD_DIM**-0.5
            low_query = (jnp.where(left, *d_query) * scale).astype(jnp.bfloat16)
            low_values = jnp.where(left, *d_values).astype(jnp.bfloat16)
            slope[rows, columns] = low_query
            slope[rows, key_columns] = (jnp.where(left, *d_keys) * scale).astype(jnp.bfloat16)
            slope[rows, value_columns] = low_values
            sums[0:1, columns] += jnp.sum(low_query.astype(jnp.float32), axis=0, keepdims=True)
            sums[1:2, columns] += jnp.sum(low_values.astype(jnp.float32), axis=0, keepdims=True)
        tick(p, ((0, "after_p", 5), (1, "after_q", 2), (2, "after_p", 4)))
        return carry

    lax.fori_loop(0, packs, attend, 0)
    for i in range(3):
        put_square(i, turned[0:D, :], slope[:, D * i : D * (i + 1)])
    if direct:
        for d in range(GRID[0]):
            at, shift = divmod(BLOCK * d, 128)
            wide = sums[:, 128 * at : 128 * at + 256]
            wide = pltpu.roll(wide, 256 - shift, 1) if shift else wide
            mine = lax.broadcasted_iota(jnp.int32, (8, 128), 1) < BLOCK
            tile = jnp.concatenate([jnp.where(mine, wide[:8, :128], 0.0), bup[3 * d : 3 * d + 8, :]], axis=0)
            for n in range(GRID[1]):
                part[d, n, 0:16, :] = tile.astype(jnp.bfloat16)
        tick(0, ((0, "start", 1), (0, "start", 0)))
        g.start(VEC_CHUNK)
    tick(0, ((0, "after_p", 3), (0, "after_c", 1), (0, "after_c", 0)))
    if direct:
        g.after_c(VEC_CHUNK)

    def widen_back(r, carry):
        rows = pl.ds(pl.multiple_of(r * LEN, LEN), LEN)
        value = flow[rows, :]
        for i in range(3):
            value = value + product_right(slope[rows, D * i : D * (i + 1)], square[D * i : D * (i + 1), :])
        norm[rows, :] = value
        tick(r, ((1, "after_p", 2),))
        return carry

    lax.fori_loop(0, packs, widen_back, 0)
    result = pltpu.make_async_copy(norm, grad_in_out, out_sem.at[0])
    result.start()
    if direct:
        tick(0, ((0, "finish", 5), (0, "finish", 4), (0, "after_q", 1), (0, "after_q", 0)))
        g.after_q(VEC_CHUNK)
        tick(0, ((0, "finish", 3), (0, "finish", 2), (0, "after_p", 1), (0, "after_p", 0)))
        g.after_p(VEC_CHUNK)
        for t in range(6):
            gup_ref[:, 128 * t : 128 * (t + 1)] = total[UP + BLOCK * t : UP + BLOCK * (t + 1), :]
        gdown_ref[...] = unpack_block(total[DOWN : DOWN + 384, :], total[DOWN + 384 : DOWN + 576, :], odd)
        tick(0, ((0, "finish", 1), (0, "finish", 0)))
        g.finish(VEC_CHUNK, total)
        gvec_ref[...] = total[0:16, :]
        for i, ref in enumerate((gq_ref, gk_ref, gv_ref, go_ref)):
            at = SQUARE + PART * i
            ref[...] = unpack_block(total[at : at + BLOCK, :], total[at + BLOCK : at + PART, :], odd)
        for chunk in [VEC_CHUNK] + [chunk for step in range(STEPS) for chunk in chunks_of(step)]:
            g.drain(chunk)
    else:
        gvec_ref[...] = sums[...]
        gbup_ref[...] = bup[...]
    result.wait()


def backward_step(direct, operands, dp, narrow):
    rows = operands[1].shape[0]
    vmem = pl.BlockSpec(memory_space=pltpu.VMEM)
    anywhere = pl.BlockSpec(memory_space=pl.ANY)
    full = lambda *shape: jax.ShapeDtypeStruct(shape, jnp.float32)
    room = lambda *shape: pltpu.VMEM(shape, jnp.bfloat16)
    wide = lambda *shape: pltpu.VMEM(shape, jnp.float32)
    if direct:
        outs = [full(D // dp, D // narrow)] * 4 + [full(D // dp, FF // narrow), full(FF // dp, D // narrow), full(16, 128)]
        places = [vmem] * 7
        depth = dp // 2
        extra = [
            room(*GRID, TOTAL, 128), room(4 * depth, 2 * STEP + SQUARE, 128), room(2 * depth, TOTAL, 128),
            room(depth, TOTAL, 128), room(depth - 1, TOTAL, 128), wide(TOTAL, 128),
            pltpu.SemaphoreType.DMA((2 * STEPS + 1, 32)), pltpu.SemaphoreType.DMA((2 * STEPS + 1, 32)),
            pltpu.SemaphoreType.REGULAR,
        ]
    else:
        outs = [full(FF, D), full(D, FF), full(FF, D), full(16, 896), full(32, 128)]
        places = [anywhere] * 3 + [vmem] * 2
        extra = [wide(2, D, D)]
    return pl.pallas_call(
        functools.partial(backward_kernel, direct),
        name="backward",
        out_shape=(full(rows, D), *outs),
        in_specs=[anywhere] * 4 + [vmem] + [anywhere] * 8 + [vmem],
        out_specs=(anywhere, *places),
        scratch_shapes=[
            room(FF, rows), room(rows, FF), room(FF, D), room(D, FF), wide(rows, D), wide(rows, D), wide(rows, 128),
            room(rows, D), room(2, HEADS, LEN, LEN), wide(16, 896), wide(32, 128),
            pltpu.SemaphoreType.DMA((12,)), pltpu.SemaphoreType.DMA((2,)), pltpu.SemaphoreType.DMA((2,)),
            *extra,
        ],
        compiler_params=pltpu.CompilerParams(
            vmem_limit_bytes=VMEM_LIMIT, **(dict(collective_id=1, has_side_effects=True) if direct else {})
        ),
    )(*operands)


def per_device(
    inputs,
    segments,
    row_kind,
    query_weight,
    query_bias,
    key_weight,
    value_weight,
    value_bias,
    output_weight,
    output_bias,
    first_gain,
    first_shift,
    up_weight,
    up_bias,
    down_weight,
    down_bias,
    second_gain,
    second_shift,
    out_cotangent,
    loss_cotangent,
):
    row_count = inputs.shape[0]
    matrices = (query_weight, key_weight, value_weight, output_weight, up_weight, down_weight)
    vectors = (
        query_bias,
        value_bias,
        output_bias,
        first_gain,
        first_shift,
        down_bias,
        second_gain,
        second_shift,
        up_bias,
    )
    dp, narrow = lax.axis_size("dp"), lax.axis_size("narrow")
    direct = (dp, narrow, row_count) == (*GRID, 4 * LEN)
    if direct:
        small = jnp.stack([jnp.pad(item, (0, 128 - BLOCK)) for item in vectors[:8]])
        small = jnp.concatenate([small, vectors[8].reshape(3, 128), jnp.zeros((5, 128), jnp.bfloat16)])
        weights = (*matrices, small)
    else:
        weights = fetch_weights(matrices, vectors)
    (square, up, down, vecs, qkv, prob, turned, norm_first, recip_first, active, slope, output_low, norm_second,
     recip_second) = forward_step(direct, weights, inputs, segments, dp, narrow)
    group_out = lax.all_gather(output_low, "narrow", axis=0, tiled=True)
    partial_value, d_second, d_branch, sums_second = transport_step(
        output_low, segments, row_kind, loss_cotangent, out_cotangent, norm_second, recip_second, vecs[6:7, :D]
    )
    transport_loss = lax.all_gather(partial_value[:, 0], "narrow", axis=0, tiled=True)
    grad_inputs, *grads = backward_step(
        direct,
        (active, slope, d_branch, d_second, sums_second, turned.reshape(3 * D, row_count), norm_first, recip_first, qkv, prob, square,
         up.reshape(D, FF), down, vecs),
        dp,
        narrow,
    )
    if direct:
        mats, vec = grads[:6], grads[6]
        vecs = [vec[i, :BLOCK] for i in range(8)] + [vec[8:11].reshape(FF // dp)]
    else:
        squares, g_up, g_down, small, tiles = grads
        mats, vecs = reduce_grads(
            [*squares.reshape(4, D, D), g_up, g_down], [*small[:8, :D], tiles[:24].reshape(FF)]
        )
    return (
        group_out,
        transport_loss,
        grad_inputs,
        mats[0],
        vecs[0],
        mats[1],
        mats[2],
        vecs[1],
        mats[3],
        vecs[2],
        vecs[3],
        vecs[4],
        mats[4],
        vecs[8],
        mats[5],
        vecs[5],
        vecs[6],
        vecs[7],
    )


def solution(mesh):
    return jax.shard_map(
        per_device,
        mesh=mesh,
        in_specs=(
            P(("dp", "narrow"), None),
            P("dp", None),
            P("dp", None),
            P("dp", "narrow"),
            P("dp"),
            P("dp", "narrow"),
            P("dp", "narrow"),
            P("dp"),
            P("dp", "narrow"),
            P("dp"),
            P("dp"),
            P("dp"),
            P("dp", "narrow"),
            P("dp"),
            P("dp", "narrow"),
            P("dp"),
            P("dp"),
            P("dp"),
            P(("dp", "narrow"), None),
            P("dp"),
        ),
        out_specs=(
            P("dp", None),
            P("dp"),
            P(("dp", "narrow"), None),
            P("dp", "narrow"),
            P("dp"),
            P("dp", "narrow"),
            P("dp", "narrow"),
            P("dp"),
            P("dp", "narrow"),
            P("dp"),
            P("dp"),
            P("dp"),
            P("dp", "narrow"),
            P("dp"),
            P("dp", "narrow"),
            P("dp"),
            P("dp"),
            P("dp"),
        ),
        check_vma=False,
    )
```

```python
import functools

import jax
import jax.numpy as jnp
from jax import lax
from jax.experimental import pallas as pl
from jax.experimental.pallas import tpu as pltpu
from jax.sharding import PartitionSpec as P

D = 768
HEADS = 12
HEAD_DIM = 64
LEN = 256
ITERS = 20
ROWS = 32
VMEM_LIMIT = 62 * 1024 * 1024

EPS_NORM = 1e-06
BETA = 0.5
MASKED = -1e30


def product(left, right):
    return jnp.dot(left, right, preferred_element_type=jnp.float32)


def product_left(left, right):
    return lax.dot_general(
        left, right, (((0,), (0,)), ((), ())), preferred_element_type=jnp.float32
    )


def product_right(left, right):
    return lax.dot_general(
        left, right, (((1,), (1,)), ((), ())), preferred_element_type=jnp.float32
    )


def fetch_weights(matrices, vectors):
    wide = [lax.all_gather(item, "narrow", axis=1, tiled=True) for item in matrices]
    query, keys, values, output, up, down = [lax.all_gather(item, "dp", axis=0, tiled=True) for item in wide]
    vecs = [lax.all_gather(item, "dp", axis=0, tiled=True).astype(jnp.float32) for item in vectors]
    up = up.reshape(GRID[0], BLOCK, GRID[1], 6, 128).transpose(0, 2, 3, 1, 4)
    up = up.reshape(GRID[0] // 2, 2, GRID[1] // 2, 2, 6 * BLOCK, 128)
    small = jnp.pad(jnp.stack(vecs[:8]), ((0, 8), (0, 128)))
    tiles = jnp.pad(vecs[8].reshape(24, 128), ((0, 8), (0, 0)))
    return (jnp.concatenate([query, keys, values, output], axis=1), up, down.T, small, tiles)


def reduce_grads(matrices, vectors):
    reduced = [lax.psum_scatter(item, "dp", scatter_dimension=0, tiled=True) for item in matrices]
    sums = [lax.psum_scatter(item, "dp", scatter_dimension=0, tiled=True) for item in vectors]
    return (
        [
            lax.psum_scatter(
                item.astype(jnp.bfloat16), "narrow", scatter_dimension=1, tiled=True
            ).astype(jnp.float32)
            for item in reduced
        ],
        lax.psum(sums, "narrow"),
    )


MESH = pl.DeviceIdType.MESH
FF = 4 * D
VEC, SQUARE, UP, DOWN, TOTAL = 0, 16, 592, 1168, 1744
PART = 144
CHUNK_ROWS = (80, 64) * 3 + (144,) * 9
CHUNKS = len(CHUNK_ROWS) + 1
SINGLES = (0, 1, 2, 3, 4, 5, CHUNKS - 1)
GRID = (8, 4)
BLOCK, SIDE = D // GRID[0], D // GRID[1]


def hops():
    dp, narrow = lax.axis_index("dp"), lax.axis_index("narrow")
    return (dp // 2, lax.rem(dp, 2), narrow // 2, lax.rem(narrow, 2))


def place(me, depth, item):
    s, a, b, c = item
    z, x, y, core = me
    z = z if s == 0 else lax.rem(z + s + depth, depth)
    x = 1 - x if a else x
    y = 1 - y if b else y
    core = 1 - core if c else core
    return (2 * z + x, 2 * y + core)


def greet(me, depth):
    peers = [place(me, depth, (s, 0, 0, 0)) for s in range(1, depth)]
    peers += [place(me, depth, (0, *bits)) for bits in ((1, 0, 0), (0, 1, 0), (0, 0, 1))]
    barrier = pltpu.get_barrier_semaphore()
    for peer in peers:
        pl.semaphore_signal(barrier, inc=1, device_id=peer, device_id_type=MESH)
    pl.semaphore_wait(barrier, len(peers))


def number(item):
    s, a, b, c = item
    return ((s * 2 + a) * 2 + b) * 2 + c


GATHER_AXES = (
    "zxy", "zxy", "zyx", "zyx", "zxy", "zxy", "zyx", "zxy", "zxy", "yxz", "zxy", "zyx", "zyx", "zxy", "yxz", "zxy",
)
FORWARD_ORDER = (
    "s1", "s15", "s5", "s2", "s14", "s3", "s4", "11", "115", "s9", "15", "s7", "s0", "12", "13", "14", "s6", "22",
    "s8", "25", "s12", "21", "215", "24", "114", "23", "17", "10", "31", "315", "s11", "19", "s10", "16", "s13", "20",
    "33", "27", "32", "18", "112", "c1", "c15", "34", "35", "30", "c3", "26", "c0", "111", "c2", "c4", "Q0", "29",
    "37", "28", "c5", "Q1", "Q2", "110", "36", "c7", "212", "A0", "214", "A1", "210", "113", "A2", "A3", "211", "c6",
    "39", "38", "O", "c8", "310", "213", "W0", "W1", "c10", "c9", "311", "312", "W2", "W3", "W4", "c11", "313", "W5",
    "c12", "c13", "314", "G", "c14", "F",
)


def split_order(order):
    after, mark = {"": []}, ""
    for word in order:
        if word[0] in "s123c":
            after[mark].append((word[0], int(word[1:])))
        else:
            mark = word
            after[mark] = []
    return after


def chunk_of(k, axes):
    if k == CHUNKS - 1:
        return (k, VEC, SQUARE - VEC, axes[k])
    return (k, SQUARE + sum(CHUNK_ROWS[:k]), CHUNK_ROWS[k], axes[k])


def arrivals(order, depth):
    have, stages = [(0, 0, 0)], []
    for axis in order:
        if axis == "z":
            new = [(far, a, b) for s, a, b in have for far in range(1, depth)]
        else:
            new = [(s, 1, b) if axis == "x" else (s, a, 1) for s, a, b in have]
        stages.append(new)
        have = have + new
    return stages


class Gather:
    def __init__(self, land, pad, send_sem, recv_sem):
        self.land, self.pad, self.send_sem, self.recv_sem = land, pad, send_sem, recv_sem
        self.me = hops()
        self.depth = land.shape[0]

    def block(self, chunk, z, x, y, core):
        return self.land.at[z, x, y, core, pl.ds(chunk[1], chunk[2]), :]

    def copy(self, chunk, block, hop, mark):
        return pltpu.make_async_remote_copy(
            src_ref=block,
            dst_ref=block,
            send_sem=self.send_sem.at[chunk[0]],
            recv_sem=self.recv_sem.at[chunk[0], mark],
            device_id=place(self.me, self.depth, hop),
            device_id_type=MESH,
        )

    def wait(self, chunk, block, mark):
        self.copy(chunk, block, (0, 0, 0, 1), mark).wait_recv()

    def single(self, chunk, item):
        s, a, b = item
        z, x, y, core = self.me
        source = lax.rem(z - s + self.depth, self.depth) if s else z
        return self.block(chunk, source, 1 - x if a else x, 1 - y if b else y, core)

    def send(self, chunk, item, axes):
        s, a, b = item
        block = self.single(chunk, item)
        for axis in axes:
            if axis == "z":
                for far in range(1, self.depth):
                    self.copy(chunk, block, (far, 0, 0, 0), number((far, a, b, 0))).start()
            elif axis == "x":
                self.copy(chunk, block, (0, 1, 0, 0), number((s, 1, b, 0))).start()
            elif axis == "y":
                self.copy(chunk, block, (0, 0, 1, 0), number((s, a, 1, 0))).start()
            else:
                self.copy(chunk, block, (0, 0, 0, 1), 1).start()

    def do(self, kind, k):
        chunk = chunk_of(k, GATHER_AXES)
        order = chunk[3]
        every = slice(None)
        z, x, y, core = self.me
        hop = {"x": (0, 1, 0, 0), "y": (0, 0, 1, 0), "c": (0, 0, 0, 1)}
        if kind == "c":
            self.wait(chunk, self.block(chunk, every, every, every, 1 - core), 1)
        elif k in SINGLES:
            if kind == "s":
                self.send(chunk, (0, 0, 0), order + "c")
            else:
                for item in arrivals(order, self.depth)[int(kind) - 1]:
                    self.wait(chunk, self.single(chunk, item), number((*item, 0)))
                    self.send(chunk, item, order[int(kind) :] + "c")
        elif order[0] == "z":
            column = self.block(chunk, every, x, y, core)
            if order[1] == "x":
                beside, behind = self.block(chunk, every, 1 - x, y, core), self.block(chunk, every, every, 1 - y, core)
            else:
                beside, behind = self.block(chunk, every, x, 1 - y, core), self.block(chunk, every, 1 - x, every, core)
            if kind == "s":
                for far in range(1, self.depth):
                    self.copy(chunk, self.single(chunk, (0, 0, 0)), (far, 0, 0, 0), 2 + far).start()
            elif kind == "1":
                for far in range(1, self.depth):
                    self.wait(chunk, self.single(chunk, (far, 0, 0)), 2 + far)
                for axis, mark in ((order[1], 6), (order[2], 7), ("c", 1)):
                    self.copy(chunk, column, hop[axis], mark).start()
            elif kind == "2":
                self.wait(chunk, beside, 6)
                for axis, mark in ((order[2], 7), ("c", 1)):
                    self.copy(chunk, beside, hop[axis], mark).start()
            else:
                self.wait(chunk, behind, 7)
                self.copy(chunk, behind, hop["c"], 1).start()
        else:
            own = self.single(chunk, (0, 0, 0))
            beside = self.single(chunk, (0, 1, 0) if order[0] == "x" else (0, 0, 1))
            behind = self.block(chunk, z, every, 1 - y, core) if order[0] == "x" else self.block(chunk, z, 1 - x, every, core)
            if kind == "s":
                for axis, mark in ((order[0], 6), (order[1], 7), ("c", 1)):
                    self.copy(chunk, own, hop[axis], mark).start()
            elif kind == "1":
                self.wait(chunk, beside, 6)
                for axis, mark in ((order[1], 7), ("c", 1)):
                    self.copy(chunk, beside, hop[axis], mark).start()
            elif kind == "2":
                self.wait(chunk, behind, 7)
                for far in range(1, self.depth):
                    self.copy(chunk, self.block(chunk, z, every, every, core), (far, 0, 0, 0), 2 + far).start()
                self.copy(chunk, behind, hop["c"], 1).start()
            else:
                for far in range(1, self.depth):
                    layer = self.block(chunk, lax.rem(z - far + self.depth, self.depth), every, every, core)
                    self.wait(chunk, layer, 2 + far)
                    self.copy(chunk, layer, hop["c"], 1).start()

    def drain(self, k):
        chunk = chunk_of(k, GATHER_AXES)
        size = self.pad.at[pl.ds(0, 16 * (8 * self.depth - 1)), pl.ds(0, 128 * chunk[2] // 16)]
        pltpu.make_async_remote_copy(
            src_ref=size,
            dst_ref=size,
            send_sem=self.send_sem.at[k],
            recv_sem=self.recv_sem.at[k, 0],
            device_id=place(self.me, self.depth, (0, 0, 0, 1)),
            device_id_type=MESH,
        ).wait_send()


def swap(half):
    return pltpu.roll(half, 64, 1)


def left_half(shape):
    return lax.broadcasted_iota(jnp.int32, shape, 1) < 64


def pack_block(wide, odd):
    rows = wide.shape[0]
    turned = pltpu.roll(wide, 192, 1)
    main = jnp.where(odd, turned[:, :128], wide[:, :128])
    rest = jnp.where(left_half((rows, 128)), jnp.where(odd, wide[:, :128], wide[:, 128:]), 0.0)
    top, low = rest[: rows // 2], rest[rows // 2 :]
    return main, jnp.where(odd, swap(top) + low, top + swap(low))


def middle_of(even, odd):
    left = left_half(even.shape)
    return jnp.where(left, even, odd), swap(jnp.where(left, odd, even))


def put_main(land, d, at, rows, ref, row, column):
    for pair in range(GRID[1] // 2):
        even, other = land.at[d // 2, d % 2, pair, 0], land.at[d // 2, d % 2, pair, 1]
        left = column + 384 * pair
        ref[pl.ds(row, rows), left : left + 128] = even[at : at + rows, :]
        ref[pl.ds(row, rows), left + 256 : left + 384] = other[at : at + rows, :]


def put_rest(land, d, at, rows, ref, row, column):
    half = rows // 2
    span = slice(at + rows, at + rows + half)
    for pair in range(GRID[1] // 2):
        even, other = land.at[d // 2, d % 2, pair, 0], land.at[d // 2, d % 2, pair, 1]
        top, low = middle_of(even[span, :].astype(jnp.float32), other[span, :].astype(jnp.float32))
        left = column + 384 * pair + 128
        ref[pl.ds(row, half), left : left + 128] = top.astype(jnp.bfloat16)
        ref[pl.ds(row + half, half), left : left + 128] = low.astype(jnp.bfloat16)


def norm_parts(values):
    centre = values - jnp.mean(values, axis=1, keepdims=True)
    spread = jnp.mean(centre * centre, axis=1, keepdims=True)
    recip = lax.rsqrt(spread + EPS_NORM)
    return centre * recip, recip


def gelu_parts(z):
    base = 1.0 + 0.2316419 * jnp.abs(z)
    t = pl.reciprocal(base, approx=True)
    t = t * (2.0 - base * t)
    density = jnp.exp2(z * z * (-0.5 * 1.4426950408889634))
    scale = 0.3989422804014327
    poly = 1.781477937 * scale + t * (-1.821255978 * scale + t * (1.330274429 * scale))
    tail = density * (t * (0.319381530 * scale + t * (-0.356563782 * scale + t * poly)))
    cdf = jnp.where(z < 0.0, tail, 1.0 - tail)
    return z * cdf, cdf + z * density * scale


def forward_kernel(direct, *refs):
    if direct:
        q_ref, k_ref, v_ref, o_ref, upw_ref, downw_ref = refs[:6]
        small_refs = refs[6:15]
        refs = refs[15:]
    else:
        square_in, up_in, down_in, vec_in, bup_in = refs[:5]
        refs = refs[5:]
    in_ref, seg_ref = refs[:2]
    (square_out, up_out, down_out, vec_ref, qkv_out, prob_out, turned_out, norm1_out, recip1_out,
     act_out, slope_out, mixed_out, norm2_out, recip2_out) = refs[2:16]
    (land, square, down, bup, qkv, qkv_turned, prob, turned, ctx, first, flow, norm, recip, act, slope, mixed,
     out_sem, pack_sem, tile_sem) = refs[16:35]
    packs = in_ref.shape[0] // LEN
    base = lax.axis_index("narrow") * packs
    pending = {}

    def save(name, src, dst):
        pending[name] = pltpu.make_async_copy(src, dst, out_sem.at[len(pending)])
        pending[name].start()

    if direct:
        send_sem, recv_sem = refs[35:37]
        dp, narrow = lax.axis_index("dp"), lax.axis_index("narrow")
        odd = lax.rem(narrow, 2) == 1
        own = land.at[dp // 2, lax.rem(dp, 2), narrow // 2, lax.rem(narrow, 2)]
        row = lambda ref: jnp.concatenate(
            [ref[...].astype(jnp.float32), jnp.zeros((1, 128 - BLOCK), jnp.float32)], axis=1
        )
        small = [row(ref) for ref in small_refs[:8]] + [small_refs[8][...].astype(jnp.float32)]
        own[0:16, :] = jnp.concatenate([*small, jnp.zeros((5, 128), jnp.float32)]).astype(jnp.bfloat16)
        for i, ref in enumerate((q_ref, k_ref, v_ref, o_ref)):
            main, rest = pack_block(
                jnp.concatenate([ref[...].astype(jnp.float32), jnp.zeros((BLOCK, 64), jnp.float32)], axis=1), odd
            )
            at = SQUARE + PART * i
            own[at : at + BLOCK, :] = main.astype(jnp.bfloat16)
            own[at + BLOCK : at + PART, :] = rest.astype(jnp.bfloat16)
        g = Gather(land, act, send_sem, recv_sem)
        greet(g.me, g.depth)
        after = split_order(FORWARD_ORDER)
        early = [piece for piece in after[""] if piece[1] < 7 or piece[1] == CHUNKS - 1]
        early = early[: next(i for i, piece in enumerate(early) if piece[0] != "s")]
        for piece in early:
            g.do(*piece)
        for t in range(6):
            own[UP + BLOCK * t : UP + BLOCK * (t + 1), :] = upw_ref[:, 128 * t : 128 * (t + 1)]
        for t in range(3):
            own[DOWN + SIDE * t : DOWN + SIDE * (t + 1), :] = downw_ref[:, 128 * t : 128 * (t + 1)]
        for piece in after[""]:
            if piece not in early:
                g.do(*piece)
        vec_ref[...] = jnp.zeros_like(vec_ref)
        for d in range(GRID[0]):
            tile = land[d // 2, d % 2, 0, 0, 0:16, :].astype(jnp.float32)
            wide = jnp.concatenate([tile, jnp.zeros((16, 128), jnp.float32)], axis=1)
            at, shift = divmod(BLOCK * d, 128)
            wide = pltpu.roll(wide, shift, 1) if shift else wide
            vec_ref[:, 128 * at : 128 * at + 256] += wide
            bup[3 * d : 3 * d + 3, :] = tile[8:11]

        def unpack(i):
            for d in range(GRID[0]):
                put_main(land, d, SQUARE + PART * i, BLOCK, square, BLOCK * d, D * i)
                put_rest(land, d, SQUARE + PART * i, BLOCK, square, BLOCK * d, D * i)

        def pieces_after(mark):
            for piece in after[mark]:
                g.do(*piece)

        def tick(mark, index):
            for name, pieces in after.items():
                if name[:1] == mark and pieces:

                    @pl.when(index == int(name[1:]))
                    def _():
                        for piece in pieces:
                            g.do(*piece)
    else:
        fills = [
            pltpu.make_async_copy(src, dst, out_sem.at[i])
            for i, (src, dst) in enumerate(
                ((square_in, square), (down_in, down), (up_in, land.at[:, :, :, :, pl.ds(UP, DOWN - UP), :]))
            )
        ]
        for copy in fills:
            copy.start()
        vec_ref[...] = vec_in[...]
        bup[...] = bup_in[...]
        for copy in fills:
            copy.wait()
        tick = lambda mark, index: None
        unpack = pieces_after = lambda mark: None

    for i in range(3):
        unpack(i)
        for j in range(3):
            columns = slice(256 * j, 256 * (j + 1))
            part = product(in_ref[...], square[:, D * i + 256 * j : D * i + 256 * (j + 1)])
            if i != 1:
                part = part + vec_ref[i // 2 : i // 2 + 1, columns]
            part = part.astype(jnp.bfloat16)
            qkv[:, D * i + 256 * j : D * i + 256 * (j + 1)] = part
            qkv_turned[D * i + 256 * j : D * i + 256 * (j + 1), :] = jnp.transpose(part)
        pieces_after(f"Q{i}")
    save("qkv", qkv_turned, qkv_out)

    def prob_copy(p):
        return pltpu.make_async_copy(prob.at[p % 2], prob_out.at[p], pack_sem.at[0, p % 2])

    def turned_copy(p):
        at = pl.ds(pl.multiple_of(p * LEN, LEN), LEN)
        return pltpu.make_async_copy(turned.at[p % 2], turned_out.at[:, :, at], pack_sem.at[1, p % 2])

    def attend(p, carry):
        rows = pl.ds(pl.multiple_of(p * LEN, LEN), LEN)
        k = p % 2

        pl.when(p >= 2)(lambda: prob_copy(p - 2).wait())
        seg_row = seg_ref[pl.ds(base + p, 1), :].astype(jnp.float32)
        seg_col = jnp.transpose(jnp.broadcast_to(seg_row, (128, LEN)))
        same = jnp.concatenate([seg_col, seg_col], axis=1) == seg_row
        left = left_half((LEN, 128))
        for h in range(HEADS // 2):
            columns = slice(128 * h, 128 * (h + 1))
            query = qkv[rows, columns] * jnp.asarray(HEAD_DIM**-0.5, jnp.bfloat16)
            keys = qkv[rows, D + 128 * h : D + 128 * (h + 1)]
            values = qkv[rows, 2 * D + 128 * h : 2 * D + 128 * (h + 1)]
            mixes = []
            for side in range(2):
                mine = left if side == 0 else jnp.logical_not(left)
                scores = product_right(jnp.where(mine, query, jnp.zeros_like(query)), keys)
                scores = jnp.where(same, scores, MASKED)
                shifted = jnp.exp(scores - jnp.max(scores, axis=1, keepdims=True))
                total = jnp.sum(shifted, axis=1, keepdims=True)
                low = (shifted * (1.0 / total)).astype(jnp.bfloat16)
                prob[k, 2 * h + side] = low
                mixes.append(product(low, values))
            ctx[rows, columns] = jnp.where(left, mixes[0], mixes[1]).astype(jnp.bfloat16)
        prob_copy(p).start()
        tick("A", p)
        return carry

    lax.fori_loop(0, packs, attend, 0)
    unpack(3)
    save("square", square, square_out)
    prob_copy(packs - 2).wait()
    prob_copy(packs - 1).wait()

    def project(p, carry):
        rows = pl.ds(pl.multiple_of(p * LEN, LEN), LEN)
        k = p % 2

        @pl.when(p >= 2)
        def _():
            turned_copy(p - 2).wait()

        x = in_ref[rows, :]
        context = ctx[rows, :]
        total = x.astype(jnp.float32) + (product(context, square[:, 3 * D :]) + vec_ref[2:3, :D])
        normed, scale = norm_parts(total)
        value = normed * vec_ref[3:4, :D] + vec_ref[4:5, :D]
        first[rows, :] = value
        low = value.astype(jnp.bfloat16)
        flow[rows, :] = low
        norm[rows, :] = normed
        recip[rows, :] = jnp.broadcast_to(scale, (LEN, 128))
        turned[k, 0] = jnp.transpose(x)
        turned[k, 1] = jnp.transpose(context)
        turned[k, 2] = jnp.transpose(low)
        turned_copy(p).start()
        return carry

    lax.fori_loop(0, packs, project, 0)
    pieces_after("O")
    save("norm", norm, norm1_out)
    save("recip", recip, recip1_out)
    turned_copy(packs - 2).wait()
    turned_copy(packs - 1).wait()

    def tile_copies(t):
        k = t % 2
        copies = []
        for n in range(GRID[1]):
            columns = pl.ds(pl.multiple_of(D * n + 128 * t, 128), 128)
            first_row = pl.multiple_of(UP + BLOCK * t, 16)
            copies += [
                pltpu.make_async_copy(slope.at[k, n], slope_out.at[:, columns], tile_sem.at[0, k, n]),
                pltpu.make_async_copy(act.at[:, columns], act_out.at[:, columns], tile_sem.at[1, k, n]),
                pltpu.make_async_copy(
                    land.at[:, :, n // 2, n % 2, pl.ds(first_row, BLOCK), :], up_out.at[:, :, :, columns], tile_sem.at[2, k, n]
                ),
            ]
        return copies

    def widen(t, carry):
        k = t % 2

        @pl.when(t >= 2)
        def _():
            for copy in tile_copies(t - 2):
                copy.wait()

        first_row = pl.multiple_of(UP + BLOCK * t, 16)
        for pair in range(2):
            weight = jnp.concatenate(
                [land[:, :, pair, i, pl.ds(first_row, BLOCK), :].reshape(D, 128) for i in range(2)], axis=1
            )
            bias = jnp.concatenate([bup[pl.ds(6 * (2 * pair + i) + t, 1), :] for i in range(2)], axis=1)
            for r in range(packs):
                rows = slice(LEN * r, LEN * (r + 1))
                value, turn = gelu_parts(product(flow[rows, :], weight) + bias)
                value, turn = value.astype(jnp.bfloat16), turn.astype(jnp.bfloat16)
                for i in range(2):
                    n = 2 * pair + i
                    columns = pl.ds(pl.multiple_of(D * n + 128 * t, 128), 128)
                    act[rows, columns] = value[:, 128 * i : 128 * (i + 1)]
                    slope[k, n, rows, :] = turn[:, 128 * i : 128 * (i + 1)]
        for copy in tile_copies(t):
            copy.start()
        tick("W", t)
        return carry

    lax.fori_loop(0, 6, widen, 0)
    def down_part(*tiles):
        if direct:
            for d in range(GRID[0]):
                for n in range(GRID[1]):
                    for t in tiles:
                        at = 384 * d + 128 * t
                        down[SIDE * n : SIDE * (n + 1), at : at + 128] = land[
                            d // 2, d % 2, n // 2, n % 2, DOWN + SIDE * t : DOWN + SIDE * (t + 1), :
                        ]
        spans = [slice(384 * d + 128 * t, 384 * d + 128 * (t + 1)) for d in range(GRID[0]) for t in tiles]
        for j in range(3):
            columns = slice(256 * j, 256 * (j + 1))
            weight = jnp.concatenate([down[columns, span] for span in spans], axis=1)
            for r in range(packs):
                rows = slice(LEN * r, LEN * (r + 1))
                hidden = jnp.concatenate([act[rows, span] for span in spans], axis=1)
                first[rows, columns] = first[rows, columns] + product_right(hidden, weight)

    down_part(0, 1)
    pieces_after("G")
    down_part(2)
    save("down", down, down_out)
    pending["norm"].wait()
    pending["recip"].wait()

    def finish(p, carry):
        rows = pl.ds(pl.multiple_of(p * LEN, LEN), LEN)
        normed, scale = norm_parts(first[rows, :] + vec_ref[5:6, :D])
        norm[rows, :] = normed
        recip[rows, :] = jnp.broadcast_to(scale, (LEN, 128))
        mixed[rows, :] = (normed * vec_ref[6:7, :D] + vec_ref[7:8, :D]).astype(jnp.bfloat16)
        return carry

    lax.fori_loop(0, packs, finish, 0)
    save("mixed", mixed, mixed_out)
    save("norm2", norm, norm2_out)
    save("recip2", recip, recip2_out)
    for t in (4, 5):
        for copy in tile_copies(t):
            copy.wait()
    if direct:
        for k in range(CHUNKS):
            g.drain(k)
    for name, copy in pending.items():
        if name not in ("norm", "recip"):
            copy.wait()


def forward_step(direct, weights, inputs, segments, dp, narrow):
    rows = inputs.shape[0]
    packs = rows // LEN
    vmem = pl.BlockSpec(memory_space=pltpu.VMEM)
    anywhere = pl.BlockSpec(memory_space=pl.ANY)
    low = lambda *shape: jax.ShapeDtypeStruct(shape, jnp.bfloat16)
    full = lambda *shape: jax.ShapeDtypeStruct(shape, jnp.float32)
    room = lambda *shape: pltpu.VMEM(shape, jnp.bfloat16)
    wide = lambda *shape: pltpu.VMEM(shape, jnp.float32)
    sems = [pltpu.SemaphoreType.DMA((CHUNKS,)), pltpu.SemaphoreType.DMA((CHUNKS, 32))] if direct else []
    return pl.pallas_call(
        functools.partial(forward_kernel, direct),
        name="forward",
        out_shape=(
            low(D, FF), low(GRID[0] // 2, 2, BLOCK, FF), low(D, FF), full(16, 896),
            low(3 * D, rows), low(packs, HEADS, LEN, LEN), low(3, D, rows), full(rows, D), full(rows, 128),
            low(rows, FF), low(rows, FF), low(rows, D), full(rows, D), full(rows, 128),
        ),
        in_specs=([vmem] * 15 if direct else [anywhere] * 3 + [vmem] * 2) + [vmem] * 2,
        out_specs=(anywhere,) * 3 + (vmem,) + (anywhere,) * 10,
        scratch_shapes=[
            room(GRID[0] // 2, 2, GRID[1] // 2, 2, TOTAL, 128), room(D, FF), room(D, FF), wide(32, 128),
            room(rows, 3 * D), room(3 * D, rows), room(2, HEADS, LEN, LEN), room(2, 3, D, LEN), room(rows, D), wide(rows, D), room(rows, D),
            wide(rows, D), wide(rows, 128), room(rows, FF), room(2, 4, rows, 128), room(rows, D),
            pltpu.SemaphoreType.DMA((12,)), pltpu.SemaphoreType.DMA((2, 2)), pltpu.SemaphoreType.DMA((3, 2, 4)),
            *sems,
        ],
        compiler_params=pltpu.CompilerParams(
            vmem_limit_bytes=VMEM_LIMIT, **(dict(collective_id=0, has_side_effects=True) if direct else {})
        ),
    )(*weights, inputs, segments)


def transport_kernel(
    mixed_ref, seg_ref, kind_ref, weight_ref, cot_in, normed_in, recip_in, gain_ref,
    value_ref, second_out, branch_out, turned_out, sums_ref,
    kern_ref, prod_ref, flow_ref, acc_ref, left_ref, sigma_ref,
    cot_ref, normed_ref, recip_ref, second_ref, branch_ref, turned_ref, load_sem, save_sem,
):
    loads = [
        pltpu.make_async_copy(src, dst, load_sem.at[i])
        for i, (src, dst) in enumerate(((cot_in, cot_ref), (normed_in, normed_ref), (recip_in, recip_ref)))
    ]
    for copy in loads:
        copy.start()
    packs = mixed_ref.shape[0] // LEN
    base = lax.axis_index("narrow") * packs
    blocks = LEN // ROWS
    lanes = lambda col: jnp.concatenate([col, col], axis=1)
    fold = lambda wide: wide[:, :128] + wide[:, 128:]
    eight = lambda wide: jnp.sum(wide.reshape(ROWS // 8, 8, LEN), axis=0)
    replicate = lambda col: jnp.broadcast_to(col, (ROWS, 128))

    def turned(row):
        return jnp.transpose(jnp.broadcast_to(row, (128, LEN)))

    for p in range(packs):
        rows = pl.ds(p * LEN, LEN)
        feats = mixed_ref[rows, :].astype(jnp.float32)
        recip = lax.rsqrt(jnp.sum(feats * feats, axis=1, keepdims=True) + EPS_NORM)
        unit = (feats * recip).astype(jnp.bfloat16)
        cosine = product_right(unit, unit)
        seg_row = seg_ref[pl.ds(base + p, 1), :].astype(jnp.float32)
        region_row = jnp.where(kind_ref[pl.ds(base + p, 1), :] == 0, 0.0, 1.0)
        seg_col = turned(seg_row)
        word_col = 1.0 - turned(region_row)
        same = jnp.where(lanes(seg_col) == seg_row, 1.0, 0.0)
        word_count = jnp.sum(same * (1.0 - region_row), axis=1, keepdims=True)
        region_count = jnp.sum(same * lanes(1.0 - word_col), axis=0, keepdims=True)
        kern_ref[p] = jnp.exp((cosine - 1.0) * (1.0 / BETA)) * same * lanes(word_col) * region_row
        left_ref[p, 0] = word_col
        left_ref[p, 1] = jnp.broadcast_to(word_count, (LEN, 128))
        left_ref[p, 2] = 1.0 - word_col
        prod_ref[0, p] = jnp.ones((LEN, LEN), jnp.float32)
        sigma_ref[0, p, 0:1] = region_row / region_count
        sigma_ref[0, p, 1:2] = region_row
        sigma_ref[0, p, 2:3] = region_count

    def advance(t, carry):
        for p in range(packs):
            sigma = sigma_ref[t, p, 0:1]
            scale = jnp.where(t == 0, 1.0, sigma)
            region = sigma_ref[0, p, 1:2]
            count = sigma_ref[0, p, 2:3]
            total = jnp.zeros((8, LEN), jnp.float32)
            for b in range(blocks):
                rows = pl.ds(b * ROWS, ROWS)
                weighted = kern_ref[p, rows, :] * (prod_ref[t, p, rows, :] * scale)
                row_sum = jnp.sum(fold(weighted * sigma), axis=1, keepdims=True)
                word = left_ref[p, 0, rows, :]
                base = left_ref[p, 1, rows, :] * replicate(row_sum) + left_ref[p, 2, rows, :]
                delta = pl.reciprocal(base, approx=True)
                delta = word * delta * (2.0 - base * delta)
                scaled = weighted * lanes(delta)
                prod_ref[t + 1, p, rows, :] = scaled
                total = total + eight(scaled)
            col_sum = jnp.sum(total, axis=0, keepdims=True)
            sigma_ref[t + 1, p, 0:1] = region / (count * col_sum + 1.0 - region)
        return carry

    lax.fori_loop(0, ITERS, advance, 0)

    starts = []
    for p in range(packs):
        rows = pl.ds(p * LEN, LEN)
        weight = weight_ref[base + p]
        feats = mixed_ref[rows, :].astype(jnp.float32)
        recip = lax.rsqrt(jnp.sum(feats * feats, axis=1, keepdims=True) + EPS_NORM)
        unit = (feats * recip).astype(jnp.bfloat16)
        cosine = product_right(unit, unit)
        moved = (prod_ref[ITERS, p] * sigma_ref[ITERS, p, 0:1]) * (1.0 - cosine)
        value_ref[p : p + 1, :] = jnp.broadcast_to(jnp.sum(moved), (1, 128))
        moved = moved * weight
        flow_ref[p] = moved
        acc_ref[p] = jnp.zeros((LEN, LEN), jnp.float32)
        starts += [jnp.sum(moved, axis=0, keepdims=True), jnp.zeros((1, LEN), jnp.float32)]

    def retreat(step, carry):
        t = ITERS - 1 - step
        out = []
        for p in range(packs):
            flow_sum, spread = carry[2 * p : 2 * p + 2]
            before = sigma_ref[t, p, 0:1]
            d_col = -sigma_ref[0, p, 2:3] * sigma_ref[t + 1, p, 0:1] * (spread + flow_sum)
            total = jnp.zeros((8, LEN), jnp.float32)
            shift = jnp.zeros((8, LEN), jnp.float32)
            for b in range(blocks):
                rows = pl.ds(b * ROWS, ROWS)
                scaled = prod_ref[t + 1, p, rows, :]
                flow = flow_ref[p, rows, :] + scaled * d_col
                d_row = replicate(jnp.sum(fold(flow), axis=1, keepdims=True))
                d_row = -left_ref[p, 1, rows, :] * d_row
                moved = scaled * lanes(d_row)
                flow = flow + moved * before
                flow_ref[p, rows, :] = flow
                acc_ref[p, rows, :] = acc_ref[p, rows, :] + flow
                total = total + eight(flow)
                shift = shift + eight(moved)
            out += [
                jnp.sum(total, axis=0, keepdims=True),
                before * jnp.sum(shift, axis=0, keepdims=True),
            ]
        return tuple(out)

    lax.fori_loop(0, ITERS, retreat, tuple(starts))

    for copy in loads:
        copy.wait()
    saves = []
    sums = [jnp.zeros((1, D), jnp.float32)] * 3
    for p in range(packs):
        rows = pl.ds(p * LEN, LEN)
        coupling = prod_ref[ITERS, p] * sigma_ref[ITERS, p, 0:1]
        d_cost = weight_ref[base + p] * coupling - acc_ref[p] * (1.0 / BETA)
        d_cosine = (-d_cost).astype(jnp.bfloat16)
        feats = mixed_ref[rows, :].astype(jnp.float32)
        recip = lax.rsqrt(jnp.sum(feats * feats, axis=1, keepdims=True) + EPS_NORM)
        unit = feats * recip
        unit_low = unit.astype(jnp.bfloat16)
        d_unit = product(d_cosine, unit_low) + product_left(d_cosine, unit_low)
        d_mixed = cot_ref[rows, :].astype(jnp.float32) + recip * (
            d_unit - unit * jnp.sum(d_unit * unit, axis=1, keepdims=True)
        )
        normed = normed_ref[rows, :]
        scaled = d_mixed * gain_ref[6:7, :D]
        inner_mean = jnp.mean(scaled, axis=1, keepdims=True)
        cross_mean = jnp.mean(scaled * normed, axis=1, keepdims=True)
        d_second = recip_ref[rows, 0:1] * (scaled - inner_mean - normed * cross_mean)
        d_branch = d_second.astype(jnp.bfloat16)
        second_ref[rows, :] = d_second
        branch_ref[rows, :] = d_branch
        turned_ref[:, rows] = jnp.transpose(d_branch)
        for src, dst in (
            (second_ref.at[rows, :], second_out.at[rows, :]),
            (branch_ref.at[rows, :], branch_out.at[rows, :]),
            (turned_ref.at[:, rows], turned_out.at[:, rows]),
        ):
            copy = pltpu.make_async_copy(src, dst, save_sem.at[len(saves)])
            copy.start()
            saves.append(copy)
        sums[0] = sums[0] + jnp.sum(d_mixed * normed, axis=0, keepdims=True)
        sums[1] = sums[1] + jnp.sum(d_mixed, axis=0, keepdims=True)
        sums[2] = sums[2] + jnp.sum(d_branch.astype(jnp.float32), axis=0, keepdims=True)
    for k in range(3):
        sums_ref[k : k + 1, :] = sums[k]
    for copy in saves:
        copy.wait()


def transport_step(mixed, segments, row_kind, weight, cotangent, normed, recip, gain):
    rows = mixed.shape[0]
    packs = rows // LEN
    vmem = pl.BlockSpec(memory_space=pltpu.VMEM)
    anywhere = pl.BlockSpec(memory_space=pl.ANY)
    square = (packs, LEN, LEN)
    return pl.pallas_call(
        transport_kernel,
        name="transport",
        out_shape=(
            jax.ShapeDtypeStruct((packs, 128), jnp.float32),
            jax.ShapeDtypeStruct((rows, D), jnp.float32),
            jax.ShapeDtypeStruct((rows, D), jnp.bfloat16),
            jax.ShapeDtypeStruct((D, rows), jnp.bfloat16),
            jax.ShapeDtypeStruct((8, D), jnp.float32),
        ),
        in_specs=[vmem, vmem, vmem, pl.BlockSpec(memory_space=pltpu.SMEM), anywhere, anywhere, anywhere, vmem],
        out_specs=(vmem, anywhere, anywhere, anywhere, vmem),
        scratch_shapes=[
            pltpu.VMEM(square, jnp.float32),
            pltpu.VMEM((ITERS + 1, *square), jnp.float32),
            pltpu.VMEM(square, jnp.float32),
            pltpu.VMEM(square, jnp.float32),
            pltpu.VMEM((packs, 3, LEN, 128), jnp.float32),
            pltpu.VMEM((ITERS + 1, packs, 8, LEN), jnp.float32),
            pltpu.VMEM((rows, D), jnp.bfloat16),
            pltpu.VMEM((rows, D), jnp.float32),
            pltpu.VMEM((rows, 128), jnp.float32),
            pltpu.VMEM((rows, D), jnp.float32),
            pltpu.VMEM((rows, D), jnp.bfloat16),
            pltpu.VMEM((D, rows), jnp.bfloat16),
            pltpu.SemaphoreType.DMA((3,)),
            pltpu.SemaphoreType.DMA((3 * packs,)),
        ],
        compiler_params=pltpu.CompilerParams(vmem_limit_bytes=VMEM_LIMIT),
    )(mixed, segments, row_kind, weight, cotangent, normed, recip, gain)


REST, OUT, MAIN = 16, 160, 304
SCATTER_ROWS = (80, 80, 80, 64, 80, 64, 80, 64) + (144,) * 4 + (96,) * 6
SCATTER_AXES = (
    "zyx", "yxz", "xyz", "xyz", "yxz", "xyz", "xyz", "xyz", "zxy", "xyz", "yxz", "xyz", "xyz", "yxz", "yxz", "zyx",
    "xyz", "yxz",
)
BACKWARD_ORDER = (
    "D0", "s12", "s13", "D1", "s14", "s15", "D2", "s16", "s17", "c12", "c13", "N0", "c14", "N1", "c15", "c16", "N2",
    "c17", "N3", "U0", "U1", "s8", "U2", "s9", "312", "313", "U3", "U4", "s10", "c8", "c9", "U5", "s11", "316", "314",
    "B0", "c10", "213", "c11", "B1", "315", "B2", "317", "B3", "212", "O", "s2", "s3", "39", "216", "T0", "c2", "214",
    "T1", "c3", "T2", "T3", "38", "310", "215", "T4", "311", "113", "T5", "29", "217", "T6", "112", "T7", "32", "116",
    "M", "s4", "s5", "s6", "s7", "211", "114", "X0", "c4", "33", "X1", "c5", "c6", "c7", "22", "28", "19", "X2",
    "210", "117", "X3", "115", "R", "s0", "s1", "34", "35", "23", "12", "111", "W0", "c0", "c1", "18", "W1", "36",
    "110", "W2", "25", "13", "37", "W3", "24", "31", "26", "27", "30", "21", "15", "14", "20", "16", "17", "10", "11",
)


class Scatter:
    def __init__(self, part, lands, send_sem, recv_sem, total):
        self.part, self.lands, self.send_sem, self.recv_sem, self.total = part, lands, send_sem, recv_sem, total
        self.me = hops()
        self.depth = part.shape[0]

    def copies(self, k):
        first, order = sum(SCATTER_ROWS[:k]), SCATTER_AXES[k]
        span = pl.ds(first, SCATTER_ROWS[k])
        every = slice(None)
        z, x, y, core = self.me
        part = lambda *at: self.part.at[*at, span, :]
        land_c, land_q, land_p, land_z = self.lands
        land = lambda ref, *at: ref.at[*at, span, :]
        to_x, to_y = (0, 1, 0, 0), (0, 0, 1, 0)
        stages = {"c": [], "3": [], "2": [], "1": []}
        ahead = lambda far: lax.rem(z + far, self.depth)
        if order[0] == "y":
            stages["c"] = [
                (part(every, every, 1 - y, 1 - core), land(land_c, every, every, 1 - y), None, part(every, every, 1 - y, core)),
                (part(every, every, y, 1 - core), land(land_c, every, every, y), None, part(every, every, y, core)),
            ]
        elif order[0] == "x":
            stages["c"] = [
                (part(every, 1 - x, every, 1 - core), land(land_c, every, 1 - x, every), None, part(every, 1 - x, every, core)),
                (part(every, x, every, 1 - core), land(land_c, every, x, every), None, part(every, x, every, core)),
            ]
        else:
            stages["c"] = [(part(every, every, every, 1 - core), land(land_c, every, every, every), None, part(every, every, every, core))]
        if order == "yxz":
            stages["3"] = [(part(every, every, 1 - y, core), land(land_q, every, every), to_y, part(every, every, y, core))]
            stages["2"] = [(part(every, 1 - x, y, core), land(land_p, every), to_x, part(every, x, y, core))]
        elif order == "xyz":
            stages["3"] = [(part(every, 1 - x, every, core), land(land_q, every, every), to_x, part(every, x, every, core))]
            stages["2"] = [(part(every, x, 1 - y, core), land(land_p, every), to_y, part(every, x, y, core))]
        else:
            for far in range(1, self.depth):
                for i in range(2):
                    slot = 2 * (far - 1) + i
                    where = land(land_q, slot, every) if slot < 4 else land(land_p, slice(2 * slot - 8, 2 * slot - 6))
                    stages["3"].append((part(ahead(far), i, every, core), where, (far, 0, 0, 0), part(z, i, every, core)))
            pair, last = land(land_z, slice(0, 2)), land(land_z, 2)
            if order[1] == "y":
                stages["2"] = [(part(z, every, 1 - y, core), pair, to_y, part(z, every, y, core))]
                stages["1"] = [(part(z, 1 - x, y, core), last, to_x, part(z, x, y, core))]
            else:
                stages["2"] = [(part(z, 1 - x, every, core), pair, to_x, part(z, x, every, core))]
                stages["1"] = [(part(z, x, 1 - y, core), last, to_y, part(z, x, y, core))]
        if order[2] == "z":
            stages["1"] = [
                (part(ahead(far), x, y, core), land(land_z, far - 1), (far, 0, 0, 0), part(z, x, y, core))
                for far in range(1, self.depth)
            ]
        made, mark = {}, 0
        for stage, items in stages.items():
            made[stage] = []
            for src, dst, hop, into in items:
                if stage != "c":
                    copy = functools.partial(self.copy, k, mark, src, dst, hop)
                    made[stage].append((copy, dst, into))
                    mark += 1
                else:
                    made[stage].append((None, dst, into))
        whole = functools.partial(
            self.copy, k, mark, part(every, every, every, 1 - core), land(land_c, every, every, every), (0, 0, 0, 1)
        )
        return whole, made

    def copy(self, k, mark, src, dst, hop):
        return pltpu.make_async_remote_copy(
            src_ref=src,
            dst_ref=dst,
            send_sem=self.send_sem.at[k, mark],
            recv_sem=self.recv_sem.at[k, mark],
            device_id=place(self.me, self.depth, hop),
            device_id_type=MESH,
        )

    def do(self, kind, k):
        whole, made = self.copies(k)
        if kind == "s":
            whole().start()
            return
        if kind == "c":
            whole().wait_recv()
        following = {"c": "3", "3": "2", "2": "1"}.get(kind)
        first, rows = sum(SCATTER_ROWS[:k]), SCATTER_ROWS[k]
        for i, (copy, land, into) in enumerate(made[kind]):
            if kind != "c":
                copy().wait_recv()
            if kind != "1":
                into[...] = into[...] + land[...]
            if kind == "c" and i == 0 and len(made["c"]) == 2:
                made["3"][0][0]().start()
        if kind == "1":
            value = made["1"][0][2][...].astype(jnp.float32)
            for copy, land, into in made["1"]:
                value = value + land[...].astype(jnp.float32)
            self.total[pl.ds(first, rows), :] = value
        elif not (kind == "c" and len(made["c"]) == 2):
            for copy, land, into in made[following]:
                copy().start()

    def drain(self, k):
        whole, made = self.copies(k)
        whole().wait_send()
        for stage in "321":
            for copy, land, into in made[stage]:
                copy().wait_send()


def fold_middle(top, low):
    left = left_half(top.shape)
    return jnp.where(left, top, swap(low)), jnp.where(left, swap(low), top)


def take_main(part, d, pair, at, even, other):
    rows = even.shape[0]
    part[d // 2, d % 2, pair, 0, at : at + rows, :] = even.astype(jnp.bfloat16)
    part[d // 2, d % 2, pair, 1, at : at + rows, :] = other.astype(jnp.bfloat16)


def take_rest(part, d, pair, at, block):
    half = block.shape[0] // 2
    one, two = fold_middle(block[:half], block[half:])
    take_main(part, d, pair, at, one, two)


def unpack_block(main, rest, odd):
    other = swap(rest)
    top, low = jnp.where(odd, other, rest), jnp.where(odd, rest, other)
    piece = jnp.concatenate([top, low], axis=0)
    left = left_half(piece.shape)
    swapped = swap(main)
    first = jnp.where(odd, jnp.where(left, piece, swapped), main)
    second = jnp.where(odd, swapped, piece)
    return jnp.concatenate([first, second], axis=1)


def backward_kernel(direct, *refs):
    (act_in, slope_in, branch_in, branch_turned_in, second_in, sums_in, turned_in, norm_in, recip_in, qkv_in, prob_in,
     square_in, up_in, down_in, vec_ref, value_ref) = refs[:16]
    refs = refs[16:]
    if direct:
        grad_in_out, total = refs[:2]
        refs = refs[2:]
    else:
        grad_in_out, gsquare_ref, gup_ref, gdown_ref, gvec_ref, gbup_ref = refs[:6]
        refs = refs[6:]
    (turned, slope, square, up, flow, norm, recip, branch, branch_turned, prob, sums, bup, load_sem, prob_sem,
     out_sem) = refs[:15]
    rows_all = slope.shape[0]
    packs = rows_all // LEN
    if direct:
        part, land_c, land_q, land_p, land_z, send_sem, recv_sem = refs[15:22]
        g = Scatter(part, (land_c, land_q, land_p, land_z), send_sem, recv_sem, total)
        dp, narrow = lax.axis_index("dp"), lax.axis_index("narrow")
    else:
        (stage,) = refs[15:16]

    loads, waited = {}, set()

    def load(name, *pairs):
        loads[name] = []
        for src, dst in pairs:
            copy = pltpu.make_async_copy(src, dst, load_sem.at[sum(map(len, loads.values()))])
            copy.start()
            loads[name].append(copy)

    def need(*names):
        for name in names:
            if name not in waited:
                waited.add(name)
                for copy in loads[name]:
                    copy.wait()

    blocks = [pl.ds(rows_all * i, rows_all) for i in range(3)]
    load("turned branch", (branch_turned_in, branch_turned))
    load("act", *[(act_in.at[:, span], turned.at[span, :]) for span in blocks])
    if direct:
        greet(g.me, g.depth)
    sums[...] = jnp.zeros_like(sums)
    bup[...] = jnp.zeros_like(bup)
    sums[5:6, :D] = sums_in[2:3, :]
    sums[6:7, :D] = sums_in[0:1, :]
    sums[7:8, :D] = sums_in[1:2, :]

    def put(src, dst):
        copy = pltpu.make_async_copy(src, dst, out_sem.at[0])
        copy.start()
        copy.wait()

    def put_down(t):
        at = pl.ds(pl.multiple_of(DOWN + SIDE * t, 16), SIDE)

        def two(i, carry):
            tiles = []
            for j in range(2):
                tile = 3 * (2 * i + j) + t
                rows = pl.ds(pl.multiple_of(tile // 8 * rows_all, 128), rows_all)
                tiles.append(turned[rows, pl.ds(pl.multiple_of(tile % 8 * 128, 128), 128)])
            grad = product(branch_turned[...], jnp.concatenate(tiles, axis=1))
            for j in range(2):
                block = grad[:, 128 * j : 128 * (j + 1)]
                if direct:
                    for n in range(GRID[1]):
                        part[i, j, n // 2, n % 2, at, :] = block[SIDE * n : SIDE * (n + 1)].astype(jnp.bfloat16)
                else:
                    stage[:, :128] = block
                    columns = pl.ds(pl.multiple_of(384 * (2 * i + j) + 128 * t, 128), 128)
                    put(stage.at[:, pl.ds(0, 128)], gdown_ref.at[:, columns])
            return carry

        lax.fori_loop(0, 4, two, 0)

    def narrow_down(c):
        at = pl.multiple_of(256 * c, 128)
        columns = pl.ds(at, 256)
        weight = square[:, columns]
        column_sum = jnp.zeros((1, 256), jnp.float32)
        for r in range(packs):
            rows = slice(LEN * r, LEN * (r + 1))
            value = product(branch[rows, :], weight) * slope[rows, columns].astype(jnp.float32)
            low = value.astype(jnp.bfloat16)
            slope[rows, columns] = low
            column_sum = column_sum + jnp.sum(low.astype(jnp.float32), axis=0, keepdims=True)
        bup[pl.ds(2 * c, 1), :] = column_sum[:, :128]
        bup[pl.ds(2 * c + 1, 1), :] = column_sum[:, 128:]

    def put_up(t, pair):
        first_row = pl.multiple_of(UP + BLOCK * t, 16)
        at = [pl.multiple_of(D * (2 * pair + j) + 128 * t, 128) for j in range(2)]
        columns = jnp.concatenate([slope[:, pl.ds(at[j], 128)] for j in range(2)], axis=1)
        grad = product(turned[2 * D : 3 * D, :], columns)
        for j in range(2):
            block = grad[:, 128 * j : 128 * (j + 1)]
            if direct:
                part[:, :, pair, j, pl.ds(first_row, BLOCK), :] = block.astype(jnp.bfloat16).reshape(
                    GRID[0] // 2, 2, BLOCK, 128
                )
            else:
                stage[:, :128] = block
                put(stage.at[:, pl.ds(0, 128)], gup_ref.at[:, pl.ds(at[j], 128)])

    def norm_back(r):
        rows = pl.ds(pl.multiple_of(r * LEN, LEN), LEN)
        d_first = flow[rows, :]
        for i in range(3):
            d_first = d_first + product_right(slope[rows, rows_all * i : rows_all * (i + 1)], up[D * i : D * (i + 1), :])
        normed = norm[rows, :]
        scaled = d_first * vec_ref[3:4, :D]
        inner_mean = jnp.mean(scaled, axis=1, keepdims=True)
        cross_mean = jnp.mean(scaled * normed, axis=1, keepdims=True)
        d_sum = recip[rows, 0:1] * (scaled - inner_mean - normed * cross_mean)
        flow[rows, :] = d_sum
        low = d_sum.astype(jnp.bfloat16)
        branch[rows, :] = low
        sums[3:4, :D] += jnp.sum(d_first * normed, axis=0, keepdims=True)
        sums[4:5, :D] += jnp.sum(d_first, axis=0, keepdims=True)
        sums[2:3, :D] += jnp.sum(low.astype(jnp.float32), axis=0, keepdims=True)

    def put_out():
        for pair in range(2):
            grad = product(turned[D : 2 * D, :], branch[:, 384 * pair : 384 * (pair + 1)])
            if direct:
                for d in range(GRID[0]):
                    block = grad[BLOCK * d : BLOCK * (d + 1)]
                    take_main(part, d, pair, OUT, block[:, :128], block[:, 256:])
                    take_rest(part, d, pair, OUT + BLOCK, block[:, 128:256])
            else:
                stage[:, :384] = grad
                put(stage.at[:, pl.ds(0, 384)], gsquare_ref.at[pl.ds(3 * D, D), pl.ds(384 * pair, 384)])

    def context_back():
        for r in range(packs):
            rows = slice(LEN * r, LEN * (r + 1))
            turned[3 * D :, rows] = product_right(square[:, 3 * D :], branch[rows, :]).astype(jnp.bfloat16)
        for r in range(packs):
            rows = slice(LEN * r, LEN * (r + 1))
            branch[rows, :] = product_right(branch[rows, :], square[:, 3 * D :]).astype(jnp.bfloat16)

    def unit_of(j, step):
        i, p = j // (packs // 2), 2 * (j % (packs // 2))
        return (i + (i + 1) // 2 if step == "T" else 3 * i + 1), p

    def prob_copy(j, step):
        h, p = unit_of(j, step)
        return pltpu.make_async_copy(prob_in.at[pl.ds(p, 2), pl.ds(2 * h, 2)], prob.at[j % 3], prob_sem.at[j % 3])

    def attend(j, step, count):
        h, p = unit_of(j, step)
        pl.when(j + 2 < count)(lambda: prob_copy(j + 2, step).start())
        prob_copy(j, step).wait()
        tile = pl.multiple_of(128 * h, 128)
        left = left_half((LEN, 128))
        at = [[pl.ds(pl.multiple_of(D * i + tile + 64 * side, 64), 64) for i in range(4)] for side in range(2)]
        parts = []
        for q in range(2):
            rows = pl.ds(pl.multiple_of((p + q) * LEN, LEN), LEN)
            context = branch[rows, pl.ds(tile, 128)]
            all_values = up[pl.ds(pl.multiple_of(2 * D + tile, 128), 128), rows]
            for side in range(2):
                mine = left if side == 0 else jnp.logical_not(left)
                d_prob = product(jnp.where(mine, context, jnp.zeros_like(context)), all_values)
                low = prob[j % 3, q, side]
                share = low.astype(jnp.float32)
                moved = share * d_prob
                d_scores = (moved - share * jnp.sum(moved, axis=1, keepdims=True)).astype(jnp.bfloat16)
                d_values = product(turned[at[side][3], rows], low)
                d_query = product_right(up[at[side][1], rows], d_scores) * HEAD_DIM**-0.5
                d_keys = product(up[at[side][0], rows], d_scores) * HEAD_DIM**-0.5
                parts.append((side, rows, [item.astype(jnp.bfloat16) for item in (d_query, d_keys, d_values)]))
        for side, rows, items in parts:
            for i in range(3):
                up[at[side][i], rows] = items[i]

    def put_tiles(tiles, at):
        for i in range(3):
            for one, two in tiles:
                right = jnp.concatenate(
                    [up[D * i + 128 * one : D * i + 128 * (one + 1), :], up[D * i + 128 * two : D * i + 128 * (two + 1), :]]
                )
                grad = product_right(turned[0:D, :], right)
                if direct:
                    for d in range(GRID[0]):
                        block = grad[BLOCK * d : BLOCK * (d + 1)]
                        if len(tiles) == 2:
                            take_main(part, d, one // 3, at + BLOCK * i, block[:, :128], block[:, 128:])
                        else:
                            take_rest(part, d, 0, at + BLOCK // 2 * i, block[:, :128])
                            take_rest(part, d, 1, at + BLOCK // 2 * i, block[:, 128:])
                else:
                    for k, tile in enumerate((one, two)):
                        stage[:, :128] = grad[:, 128 * k : 128 * (k + 1)]
                        put(stage.at[:, pl.ds(0, 128)], gsquare_ref.at[pl.ds(D * i, D), pl.ds(128 * tile, 128)])

    def put_vectors():
        ones = jnp.ones((8, rows_all), jnp.bfloat16)
        sums[0:1, :D] = product_right(ones, up[0:D, :])[0:1]
        sums[1:2, :D] = product_right(ones, up[2 * D : 3 * D, :])[0:1]
        if direct:
            lane = lax.broadcasted_iota(jnp.int32, (1, 128), 1)
            value = jnp.zeros((1, 128), jnp.float32)
            for p in range(packs):
                value = jnp.where(lane == narrow * packs + p, value_ref[p : p + 1, :], value)
            high = value.astype(jnp.bfloat16).astype(jnp.float32)
            zeros = jnp.zeros((3, 128), jnp.float32)
            for d in range(GRID[0]):
                at, shift = divmod(BLOCK * d, 128)
                wide = sums[:, 128 * at : 128 * at + 256]
                wide = pltpu.roll(wide, 256 - shift, 1) if shift else wide
                mine = lax.broadcasted_iota(jnp.int32, (8, 128), 1) < BLOCK
                own = jnp.where(dp == d, 1.0, 0.0)
                tile = jnp.concatenate(
                    [jnp.where(mine, wide[:8, :128], 0.0), bup[3 * d : 3 * d + 3, :], high * own, (value - high) * own, zeros]
                )
                for n in range(GRID[1]):
                    part[d // 2, d % 2, n // 2, n % 2, 0:16, :] = tile.astype(jnp.bfloat16)

    def widen_back(r):
        rows = pl.ds(pl.multiple_of(r * LEN, LEN), LEN)
        value = product(square[:, :D], up[:D, rows])
        for i in (1, 2):
            value = value + product(square[:, D * i : D * (i + 1)], up[D * i : D * (i + 1), rows])
        norm[rows, :] = flow[rows, :] + jnp.transpose(value)

    after = split_order(BACKWARD_ORDER)

    def tick(mark, index=None):
        if not direct:
            return
        for name, pieces in after.items():
            if name[:1] == mark and pieces:
                if index is None:
                    for piece in pieces:
                        g.do(*piece)
                else:

                    @pl.when(index == int(name[1:]))
                    def _():
                        for piece in pieces:
                            g.do(*piece)

    def repeat(mark, first, last, body):
        def step(i, carry):
            body(i)
            tick(mark, i)
            return carry

        lax.fori_loop(first, last, step, 0)

    def up_pair(t):
        put_up(t, 0)
        put_up(t, 1)

    def down_three(i):
        for j in range(3):
            narrow_down(3 * i + j)

    groups = []
    for name in [name for name in after if name]:
        if groups and groups[-1][0] == name[0]:
            groups[-1][1].append(int(name[1:]))
        else:
            groups.append((name[0], [int(name[1:] or 0)]))
    for mark, span in groups:
        first, last = span[0], span[-1] + 1
        if mark == "D":
            need("turned branch", "act")
            load("branch", (branch_in, branch))
            load("down", (down_in, square))
            load("slope", (slope_in, slope))
            load("up", *[(up_in.at[:, pl.ds(rows_all * i, rows_all)], up.at[pl.ds(D * i, D), :]) for i in range(3)])
            load("flow", (second_in, flow))
            load("norm", (norm_in, norm))
            load("recip", (recip_in, recip))
            repeat("D", first, last, put_down)
            load("turned", (turned_in, turned.at[pl.ds(0, 3 * D), :]))
        elif mark == "N":
            need("branch", "down", "slope")
            repeat("N", first, last, down_three)
            load("square", (square_in, square))
        elif mark == "U":
            need("turned")
            repeat("U", first, last, up_pair)
        elif mark == "B":
            need("up", "flow", "norm", "recip")
            repeat("B", first, last, norm_back)
            load("qkv", (qkv_in, up))
            for j in range(2):
                prob_copy(j, "T").start()
        elif mark == "O":
            need("turned", "square")
            put_out()
            context_back()
            tick("O")
        elif mark == "T":
            need("qkv")
            repeat("T", first, last, lambda j: attend(j, "T", 2 * packs))
            for j in range(2):
                prob_copy(j, "X").start()
        elif mark == "M":
            put_tiles(((0, 2), (3, 5)), MAIN)
            tick("M")
        elif mark == "X":
            repeat("X", first, last, lambda j: attend(j, "X", packs))
        elif mark == "R":
            put_tiles(((1, 4),), REST)
            put_vectors()
            tick("R")
        elif mark == "W":
            repeat("W", first, last, widen_back)
            result = pltpu.make_async_copy(norm, grad_in_out, out_sem.at[1])
            result.start()
    if direct:
        for k in range(len(SCATTER_ROWS)):
            g.drain(k)
    else:
        gvec_ref[...] = sums[...]
        gbup_ref[...] = bup[...]
    result.wait()


def backward_step(direct, operands, dp, narrow):
    rows = operands[1].shape[0]
    vmem = pl.BlockSpec(memory_space=pltpu.VMEM)
    anywhere = pl.BlockSpec(memory_space=pl.ANY)
    full = lambda *shape: jax.ShapeDtypeStruct(shape, jnp.float32)
    room = lambda *shape: pltpu.VMEM(shape, jnp.bfloat16)
    wide = lambda *shape: pltpu.VMEM(shape, jnp.float32)
    if direct:
        outs, places = [full(TOTAL, 128)], [vmem]
        depth = dp // 2
        count = len(SCATTER_ROWS)
        extra = [
            room(depth, 2, 2, 2, TOTAL, 128), room(depth, 2, 2, TOTAL, 128), room(depth, 2, TOTAL, 128),
            room(depth, TOTAL, 128), room(depth - 1, TOTAL, 128),
            pltpu.SemaphoreType.DMA((count, 12)), pltpu.SemaphoreType.DMA((count, 12)),
        ]
    else:
        outs = [full(FF, D), full(D, FF), full(D, FF), full(16, 896), full(32, 128)]
        places = [anywhere] * 3 + [vmem] * 2
        extra = [wide(D, D)]
    return pl.pallas_call(
        functools.partial(backward_kernel, direct),
        name="backward",
        out_shape=(full(rows, D), *outs),
        in_specs=[anywhere] * 5 + [vmem] + [anywhere] * 8 + [vmem] * 2,
        out_specs=(anywhere, *places),
        scratch_shapes=[
            room(FF, rows), room(rows, FF), room(D, FF), room(3 * D, rows), wide(rows, D), wide(rows, D), wide(rows, 128),
            room(rows, D), room(D, rows), room(3, 2, 2, LEN, LEN), wide(16, 896), wide(32, 128),
            pltpu.SemaphoreType.DMA((20,)), pltpu.SemaphoreType.DMA((3,)), pltpu.SemaphoreType.DMA((2,)),
            *extra,
        ],
        compiler_params=pltpu.CompilerParams(
            vmem_limit_bytes=VMEM_LIMIT, **(dict(collective_id=1, has_side_effects=True) if direct else {})
        ),
    )(*operands)


def collect_kernel(packs_all, total, group_in, grad_in, *refs):
    (group_out, loss, grad_out, gq, gqb, gk, gv, gvb, go, gob, gfg, gfs, gup, gupb, gdown, gdownb, gsg, gss, group, grad, in_sem, out_sem) = refs
    parts = [(group_in, group, group_out, i) for i in range(group.shape[0] // LEN)]
    parts += [(grad_in, grad, grad_out, i) for i in range(grad.shape[0] // LEN)]
    ins, outs = [], []
    for k, (src, via, dst, i) in enumerate(parts):
        rows = pl.ds(LEN * i, LEN)
        ins.append(pltpu.make_async_copy(src.at[rows, :], via.at[rows, :], in_sem.at[k]))
        outs.append(pltpu.make_async_copy(via.at[rows, :], dst.at[rows, :], out_sem.at[k]))
        ins[-1].start()
    odd = lax.rem(lax.axis_index("narrow"), 2) == 1
    for one, two in zip(ins, outs):
        one.wait()
        two.start()
    for i, ref in enumerate((gqb, gvb, gob, gfg, gfs, gdownb, gsg, gss)):
        ref[...] = total[i : i + 1, :BLOCK]
    gupb[...] = total[8:11, :]
    loss[...] = (total[11:12, :] + total[12:13, :])[:, :packs_all]
    for t in range(6):
        gup[:, 128 * t : 128 * (t + 1)] = total[UP + BLOCK * t : UP + BLOCK * (t + 1), :]
    for ref, main, rest in (
        (gq, MAIN, REST), (gk, MAIN + BLOCK, REST + BLOCK // 2), (gv, MAIN + 2 * BLOCK, REST + BLOCK), (go, OUT, OUT + BLOCK),
    ):
        block = unpack_block(total[main : main + BLOCK, :], total[rest : rest + BLOCK // 2, :], odd)
        ref[...] = block[:, :192]
    for t in range(3):
        gdown[:, 128 * t : 128 * (t + 1)] = total[DOWN + SIDE * t : DOWN + SIDE * (t + 1), :]
    for copy in outs:
        copy.wait()


def collect_step(total, group, grad_inputs, dp, narrow):
    packs_all = group.shape[0] // LEN
    vmem = pl.BlockSpec(memory_space=pltpu.VMEM)
    anywhere = pl.BlockSpec(memory_space=pl.ANY)
    full = lambda *shape: jax.ShapeDtypeStruct(shape, jnp.float32)
    square, vector = full(D // dp, D // narrow), full(1, D // dp)
    count = (group.shape[0] + grad_inputs.shape[0]) // LEN
    out = pl.pallas_call(
        functools.partial(collect_kernel, packs_all),
        name="collect",
        out_shape=(
            jax.ShapeDtypeStruct(group.shape, group.dtype), full(1, packs_all), full(*grad_inputs.shape),
            square, vector, square, square, vector, square, vector, vector, vector,
            full(D // dp, FF // narrow), full(FF // dp // 128, 128), full(D // narrow, FF // dp), vector, vector, vector,
        ),
        in_specs=[vmem, anywhere, anywhere],
        out_specs=(anywhere, vmem, anywhere) + (vmem,) * 15,
        scratch_shapes=[
            pltpu.VMEM(group.shape, group.dtype), pltpu.VMEM(grad_inputs.shape, jnp.float32),
            pltpu.SemaphoreType.DMA((count,)), pltpu.SemaphoreType.DMA((count,)),
        ],
        compiler_params=pltpu.CompilerParams(vmem_limit_bytes=VMEM_LIMIT),
    )(total, group, grad_inputs)
    out = [item.reshape(-1) if item.shape[0] in (1, 3) else item for item in out]
    out[14] = out[14].T
    return tuple(out)


def per_device(
    inputs,
    segments,
    row_kind,
    query_weight,
    query_bias,
    key_weight,
    value_weight,
    value_bias,
    output_weight,
    output_bias,
    first_gain,
    first_shift,
    up_weight,
    up_bias,
    down_weight,
    down_bias,
    second_gain,
    second_shift,
    out_cotangent,
    loss_cotangent,
):
    row_count = inputs.shape[0]
    matrices = (query_weight, key_weight, value_weight, output_weight, up_weight, down_weight)
    vectors = (
        query_bias,
        value_bias,
        output_bias,
        first_gain,
        first_shift,
        down_bias,
        second_gain,
        second_shift,
        up_bias,
    )
    dp, narrow = lax.axis_size("dp"), lax.axis_size("narrow")
    direct = (dp, narrow, row_count) == (*GRID, 4 * LEN)
    if direct:
        weights = (*matrices[:5], down_weight.T, *[item.reshape(1, -1) for item in vectors[:8]], up_bias.reshape(-1, 128))
    else:
        weights = fetch_weights(matrices, vectors)
    (square, up, down, vecs, qkv, prob, turned, norm_first, recip_first, active, slope, output_low, norm_second,
     recip_second) = forward_step(direct, weights, inputs, segments, dp, narrow)
    group_out = lax.all_gather(output_low, "narrow", axis=0, tiled=True)
    partial_value, d_second, d_branch, branch_turned, sums_second = transport_step(
        output_low, segments, row_kind, loss_cotangent, out_cotangent, norm_second, recip_second, vecs
    )
    grad_inputs, *grads = backward_step(
        direct,
        (active, slope, d_branch, branch_turned, d_second, sums_second, turned.reshape(3 * D, row_count), norm_first, recip_first, qkv, prob, square,
         up.reshape(D, FF), down, vecs, partial_value),
        dp,
        narrow,
    )
    if direct:
        return collect_step(grads[0], group_out, grad_inputs, dp, narrow)
    transport_loss = lax.all_gather(partial_value[:, 0], "narrow", axis=0, tiled=True)
    squares, g_up, g_down, small, tiles = grads
    mats, vecs = reduce_grads([*squares.reshape(4, D, D), g_up, g_down.T], [*small[:8, :D], tiles[:24].reshape(FF)])
    return (
        group_out,
        transport_loss,
        grad_inputs,
        mats[0],
        vecs[0],
        mats[1],
        mats[2],
        vecs[1],
        mats[3],
        vecs[2],
        vecs[3],
        vecs[4],
        mats[4],
        vecs[8],
        mats[5],
        vecs[5],
        vecs[6],
        vecs[7],
    )


def solution(mesh):
    return jax.shard_map(
        per_device,
        mesh=mesh,
        in_specs=(
            P(("dp", "narrow"), None),
            P("dp", None),
            P("dp", None),
            P("dp", "narrow"),
            P("dp"),
            P("dp", "narrow"),
            P("dp", "narrow"),
            P("dp"),
            P("dp", "narrow"),
            P("dp"),
            P("dp"),
            P("dp"),
            P("dp", "narrow"),
            P("dp"),
            P("dp", "narrow"),
            P("dp"),
            P("dp"),
            P("dp"),
            P(("dp", "narrow"), None),
            P("dp"),
        ),
        out_specs=(
            P("dp", None),
            P("dp"),
            P(("dp", "narrow"), None),
            P("dp", "narrow"),
            P("dp"),
            P("dp", "narrow"),
            P("dp", "narrow"),
            P("dp"),
            P("dp", "narrow"),
            P("dp"),
            P("dp"),
            P("dp"),
            P("dp", "narrow"),
            P("dp"),
            P("dp", "narrow"),
            P("dp"),
            P("dp"),
            P("dp"),
        ),
        check_vma=False,
    )
```

```python
import functools

import jax
import jax.numpy as jnp
from jax import lax
from jax.experimental import pallas as pl
from jax.experimental.pallas import tpu as pltpu
from jax.sharding import PartitionSpec as P

D = 768
HEADS = 12
HEAD_DIM = 64
LEN = 256
ITERS = 20
ROWS = 32
VMEM_LIMIT = 62 * 1024 * 1024

EPS_NORM = 1e-06
BETA = 0.5
MASKED = -1e30


def product(left, right):
    return jnp.dot(left, right, preferred_element_type=jnp.float32)


def product_left(left, right):
    return lax.dot_general(
        left, right, (((0,), (0,)), ((), ())), preferred_element_type=jnp.float32
    )


def product_right(left, right):
    return lax.dot_general(
        left, right, (((1,), (1,)), ((), ())), preferred_element_type=jnp.float32
    )


def fetch_weights(matrices, vectors):
    wide = [lax.all_gather(item, "narrow", axis=1, tiled=True) for item in matrices]
    query, keys, values, output, up, down = [lax.all_gather(item, "dp", axis=0, tiled=True) for item in wide]
    vecs = [lax.all_gather(item, "dp", axis=0, tiled=True).astype(jnp.float32) for item in vectors]
    up = up.reshape(GRID[0], BLOCK, GRID[1], 6, 128).transpose(0, 2, 3, 1, 4)
    up = up.reshape(GRID[0] // 2, 2, GRID[1] // 2, 2, 6 * BLOCK, 128)
    small = jnp.pad(jnp.stack(vecs[:8]), ((0, 8), (0, 128)))
    tiles = jnp.pad(vecs[8].reshape(24, 128), ((0, 8), (0, 0)))
    return (jnp.concatenate([query, keys, values, output], axis=1), up, down.T, small, tiles)


def reduce_grads(matrices, vectors):
    reduced = [lax.psum_scatter(item, "dp", scatter_dimension=0, tiled=True) for item in matrices]
    sums = [lax.psum_scatter(item, "dp", scatter_dimension=0, tiled=True) for item in vectors]
    return (
        [
            lax.psum_scatter(
                item.astype(jnp.bfloat16), "narrow", scatter_dimension=1, tiled=True
            ).astype(jnp.float32)
            for item in reduced
        ],
        lax.psum(sums, "narrow"),
    )


MESH = pl.DeviceIdType.MESH
FF = 4 * D
VEC, SQUARE, UP, DOWN, TOTAL = 0, 16, 592, 1168, 1744
PART = 144
CHUNK_ROWS = (80, 64) * 3 + (144,) * 9
CHUNKS = len(CHUNK_ROWS) + 1
SINGLES = (0, 1, 2, 3, 4, 5, CHUNKS - 1)
GRID = (8, 4)
BLOCK, SIDE = D // GRID[0], D // GRID[1]


def hops():
    dp, narrow = lax.axis_index("dp"), lax.axis_index("narrow")
    return (dp // 2, lax.rem(dp, 2), narrow // 2, lax.rem(narrow, 2))


def place(me, depth, item):
    s, a, b, c = item
    z, x, y, core = me
    z = z if s == 0 else lax.rem(z + s + depth, depth)
    x = 1 - x if a else x
    y = 1 - y if b else y
    core = 1 - core if c else core
    return (2 * z + x, 2 * y + core)


def greet(me, depth):
    peers = [place(me, depth, (s, 0, 0, 0)) for s in range(1, depth)]
    peers += [place(me, depth, (0, *bits)) for bits in ((1, 0, 0), (0, 1, 0), (0, 0, 1))]
    barrier = pltpu.get_barrier_semaphore()
    for peer in peers:
        pl.semaphore_signal(barrier, inc=1, device_id=peer, device_id_type=MESH)
    pl.semaphore_wait(barrier, len(peers))


def number(item):
    s, a, b, c = item
    return ((s * 2 + a) * 2 + b) * 2 + c


GATHER_AXES = (
    "zxy", "zyx", "zxy", "zyx", "zxy", "zyx", "zxy", "zyx", "zxy", "zyx", "zxy", "zyx", "zxy", "zyx", "zxy", "zxy",
)
FORWARD_ORDER = (
    0, 1, 15, 2, 3, 4, 5, 100, 6, 101, 115, 7, 200, 102, 201, 215, 8, 103, 300, 104, 202, 9, 400, 105, 301, 315, 203,
    401, 415, 500, 204, 106, 302, 10, 205, 11, 303, 402, 107, 403, 501, 304, 12, 404, 108, 206, 305, 405, 13, 502,
    109, 600, 207, 110, 601, 208, 602, 111, 603, 306, 112, 406, 700, 307, 209, 113, 210, 407, 800, 308, 408, 801, 14,
    802, 211, 212, 309, 409, 803, 114, 213, 311, 310, 411, 410, 804, 312, 214, 805, 412, 313, 413, 900, 314, 414,
    1000,
)


def split_order(order, kinds, marks):
    after, mark = {"": []}, ""
    for code in order:
        kind, index = divmod(code, 100)
        if kind < len(kinds):
            after[mark].append((kinds[kind], index))
        else:
            mark = marks[kind - len(kinds)] + str(index)
            after[mark] = []
    return after


def chunk_of(k, axes):
    if k == CHUNKS - 1:
        return (k, VEC, SQUARE - VEC, axes[k])
    return (k, SQUARE + sum(CHUNK_ROWS[:k]), CHUNK_ROWS[k], axes[k])


def arrivals(order, depth):
    have, stages = [(0, 0, 0)], []
    for axis in order:
        if axis == "z":
            new = [(far, a, b) for s, a, b in have for far in range(1, depth)]
        else:
            new = [(s, 1, b) if axis == "x" else (s, a, 1) for s, a, b in have]
        stages.append(new)
        have = have + new
    return stages


class Gather:
    def __init__(self, land, pad, send_sem, recv_sem):
        self.land, self.pad, self.send_sem, self.recv_sem = land, pad, send_sem, recv_sem
        self.me = hops()
        self.depth = land.shape[0]

    def block(self, chunk, z, x, y, core):
        return self.land.at[z, x, y, core, pl.ds(chunk[1], chunk[2]), :]

    def copy(self, chunk, block, hop, mark):
        return pltpu.make_async_remote_copy(
            src_ref=block,
            dst_ref=block,
            send_sem=self.send_sem.at[chunk[0]],
            recv_sem=self.recv_sem.at[chunk[0], mark],
            device_id=place(self.me, self.depth, hop),
            device_id_type=MESH,
        )

    def wait(self, chunk, block, mark):
        self.copy(chunk, block, (0, 0, 0, 1), mark).wait_recv()

    def single(self, chunk, item):
        s, a, b = item
        z, x, y, core = self.me
        source = lax.rem(z - s + self.depth, self.depth) if s else z
        return self.block(chunk, source, 1 - x if a else x, 1 - y if b else y, core)

    def send(self, chunk, item, axes):
        s, a, b = item
        block = self.single(chunk, item)
        for axis in axes:
            if axis == "z":
                for far in range(1, self.depth):
                    self.copy(chunk, block, (far, 0, 0, 0), number((far, a, b, 0))).start()
            elif axis == "x":
                self.copy(chunk, block, (0, 1, 0, 0), number((s, 1, b, 0))).start()
            elif axis == "y":
                self.copy(chunk, block, (0, 0, 1, 0), number((s, a, 1, 0))).start()
            else:
                self.copy(chunk, block, (0, 0, 0, 1), 1).start()

    def do(self, kind, k):
        chunk = chunk_of(k, GATHER_AXES)
        order = chunk[3]
        every = slice(None)
        z, x, y, core = self.me
        hop = {"x": (0, 1, 0, 0), "y": (0, 0, 1, 0), "c": (0, 0, 0, 1)}
        if kind == "c":
            self.wait(chunk, self.block(chunk, every, every, every, 1 - core), 1)
        elif k in SINGLES:
            if kind == "s":
                self.send(chunk, (0, 0, 0), order + "c")
            else:
                for item in arrivals(order, self.depth)[int(kind) - 1]:
                    self.wait(chunk, self.single(chunk, item), number((*item, 0)))
                    self.send(chunk, item, order[int(kind) :] + "c")
        elif order[0] == "z":
            column = self.block(chunk, every, x, y, core)
            if order[1] == "x":
                beside, behind = self.block(chunk, every, 1 - x, y, core), self.block(chunk, every, every, 1 - y, core)
            else:
                beside, behind = self.block(chunk, every, x, 1 - y, core), self.block(chunk, every, 1 - x, every, core)
            if kind == "s":
                for far in range(1, self.depth):
                    self.copy(chunk, self.single(chunk, (0, 0, 0)), (far, 0, 0, 0), 2 + far).start()
            elif kind == "1":
                for far in range(1, self.depth):
                    self.wait(chunk, self.single(chunk, (far, 0, 0)), 2 + far)
                for axis, mark in ((order[1], 6), (order[2], 7), ("c", 1)):
                    self.copy(chunk, column, hop[axis], mark).start()
            elif kind == "2":
                self.wait(chunk, beside, 6)
                for axis, mark in ((order[2], 7), ("c", 1)):
                    self.copy(chunk, beside, hop[axis], mark).start()
            else:
                self.wait(chunk, behind, 7)
                self.copy(chunk, behind, hop["c"], 1).start()
        else:
            own = self.single(chunk, (0, 0, 0))
            beside = self.single(chunk, (0, 1, 0) if order[0] == "x" else (0, 0, 1))
            behind = self.block(chunk, z, every, 1 - y, core) if order[0] == "x" else self.block(chunk, z, 1 - x, every, core)
            if kind == "s":
                for axis, mark in ((order[0], 6), (order[1], 7), ("c", 1)):
                    self.copy(chunk, own, hop[axis], mark).start()
            elif kind == "1":
                self.wait(chunk, beside, 6)
                for axis, mark in ((order[1], 7), ("c", 1)):
                    self.copy(chunk, beside, hop[axis], mark).start()
            elif kind == "2":
                self.wait(chunk, behind, 7)
                for far in range(1, self.depth):
                    self.copy(chunk, self.block(chunk, z, every, every, core), (far, 0, 0, 0), 2 + far).start()
                self.copy(chunk, behind, hop["c"], 1).start()
            else:
                for far in range(1, self.depth):
                    layer = self.block(chunk, lax.rem(z - far + self.depth, self.depth), every, every, core)
                    self.wait(chunk, layer, 2 + far)
                    self.copy(chunk, layer, hop["c"], 1).start()

    def drain(self, k):
        chunk = chunk_of(k, GATHER_AXES)
        size = self.pad.at[pl.ds(0, 16 * (8 * self.depth - 1)), pl.ds(0, 128 * chunk[2] // 16)]
        pltpu.make_async_remote_copy(
            src_ref=size,
            dst_ref=size,
            send_sem=self.send_sem.at[k],
            recv_sem=self.recv_sem.at[k, 0],
            device_id=place(self.me, self.depth, (0, 0, 0, 1)),
            device_id_type=MESH,
        ).wait_send()


def swap(half):
    return pltpu.roll(half, 64, 1)


def left_half(shape):
    return lax.broadcasted_iota(jnp.int32, shape, 1) < 64


def pack_block(wide, odd):
    rows = wide.shape[0]
    turned = pltpu.roll(wide, 192, 1)
    main = jnp.where(odd, turned[:, :128], wide[:, :128])
    rest = jnp.where(left_half((rows, 128)), jnp.where(odd, wide[:, :128], wide[:, 128:]), 0.0)
    top, low = rest[: rows // 2], rest[rows // 2 :]
    return main, jnp.where(odd, swap(top) + low, top + swap(low))


def middle_of(even, odd):
    left = left_half(even.shape)
    return jnp.where(left, even, odd), swap(jnp.where(left, odd, even))


def put_main(land, d, at, rows, ref, row, column):
    for pair in range(GRID[1] // 2):
        even, other = land.at[d // 2, d % 2, pair, 0], land.at[d // 2, d % 2, pair, 1]
        left = column + 384 * pair
        ref[pl.ds(row, rows), left : left + 128] = even[at : at + rows, :]
        ref[pl.ds(row, rows), left + 256 : left + 384] = other[at : at + rows, :]


def put_rest(land, d, at, rows, ref, row, column):
    half = rows // 2
    span = slice(at + rows, at + rows + half)
    for pair in range(GRID[1] // 2):
        even, other = land.at[d // 2, d % 2, pair, 0], land.at[d // 2, d % 2, pair, 1]
        top, low = middle_of(even[span, :].astype(jnp.float32), other[span, :].astype(jnp.float32))
        left = column + 384 * pair + 128
        ref[pl.ds(row, half), left : left + 128] = top.astype(jnp.bfloat16)
        ref[pl.ds(row + half, half), left : left + 128] = low.astype(jnp.bfloat16)


def norm_parts(values):
    centre = values - jnp.mean(values, axis=1, keepdims=True)
    spread = jnp.mean(centre * centre, axis=1, keepdims=True)
    recip = lax.rsqrt(spread + EPS_NORM)
    return centre * recip, recip


def gelu_parts(z):
    base = 1.0 + 0.2316419 * jnp.abs(z)
    t = pl.reciprocal(base, approx=True)
    t = t * (2.0 - base * t)
    density = jnp.exp2(z * z * (-0.5 * 1.4426950408889634))
    scale = 0.3989422804014327
    poly = 1.781477937 * scale + t * (-1.821255978 * scale + t * (1.330274429 * scale))
    tail = density * (t * (0.319381530 * scale + t * (-0.356563782 * scale + t * poly)))
    cdf = jnp.where(z < 0.0, tail, 1.0 - tail)
    return z * cdf, cdf + z * density * scale


def forward_kernel(direct, *refs):
    if direct:
        q_ref, k_ref, v_ref, o_ref, upw_ref, downw_ref = refs[:6]
        small_refs = refs[6:15]
        refs = refs[15:]
    else:
        square_in, up_in, down_in, vec_in, bup_in = refs[:5]
        refs = refs[5:]
    in_ref, seg_ref = refs[:2]
    (square_out, up_out, down_out, vec_ref, qkv_out, prob_out, turned_out, norm1_out, recip1_out,
     act_out, slope_out, mixed_out, norm2_out, recip2_out) = refs[2:16]
    (land, square, down, bup, qkv, qkv_turned, prob, turned, ctx, first, flow, norm, recip, act, slope, mixed,
     out_sem, pack_sem, tile_sem) = refs[16:35]
    packs = in_ref.shape[0] // LEN
    base = lax.axis_index("narrow") * packs
    pending = {}

    def save(name, src, dst):
        pending[name] = pltpu.make_async_copy(src, dst, out_sem.at[len(pending)])
        pending[name].start()

    if direct:
        send_sem, recv_sem = refs[35:37]
        dp, narrow = lax.axis_index("dp"), lax.axis_index("narrow")
        odd = lax.rem(narrow, 2) == 1
        own = land.at[dp // 2, lax.rem(dp, 2), narrow // 2, lax.rem(narrow, 2)]
        row = lambda ref: jnp.concatenate(
            [ref[...].astype(jnp.float32), jnp.zeros((1, 128 - BLOCK), jnp.float32)], axis=1
        )
        small = [row(ref) for ref in small_refs[:8]] + [small_refs[8][...].astype(jnp.float32)]
        own[0:16, :] = jnp.concatenate([*small, jnp.zeros((5, 128), jnp.float32)]).astype(jnp.bfloat16)
        for i, ref in enumerate((q_ref, k_ref, v_ref, o_ref)):
            main, rest = pack_block(
                jnp.concatenate([ref[...].astype(jnp.float32), jnp.zeros((BLOCK, 64), jnp.float32)], axis=1), odd
            )
            at = SQUARE + PART * i
            own[at : at + BLOCK, :] = main.astype(jnp.bfloat16)
            own[at + BLOCK : at + PART, :] = rest.astype(jnp.bfloat16)
        g = Gather(land, act, send_sem, recv_sem)
        greet(g.me, g.depth)
        after = split_order(FORWARD_ORDER, "s123c", "QAOWGF")
        early = [piece for piece in after[""] if piece[1] < 7 or piece[1] == CHUNKS - 1]
        early = early[: next(i for i, piece in enumerate(early) if piece[0] != "s")]
        for piece in early:
            g.do(*piece)
        for t in range(6):
            own[UP + BLOCK * t : UP + BLOCK * (t + 1), :] = upw_ref[:, 128 * t : 128 * (t + 1)]
        for t in range(3):
            own[DOWN + SIDE * t : DOWN + SIDE * (t + 1), :] = downw_ref[:, 128 * t : 128 * (t + 1)]
        for piece in after[""]:
            if piece not in early:
                g.do(*piece)
        vec_ref[...] = jnp.zeros_like(vec_ref)
        for d in range(GRID[0]):
            tile = land[d // 2, d % 2, 0, 0, 0:16, :].astype(jnp.float32)
            wide = jnp.concatenate([tile, jnp.zeros((16, 128), jnp.float32)], axis=1)
            at, shift = divmod(BLOCK * d, 128)
            wide = pltpu.roll(wide, shift, 1) if shift else wide
            vec_ref[:, 128 * at : 128 * at + 256] += wide
            bup[3 * d : 3 * d + 3, :] = tile[8:11]

        def unpack(i):
            for d in range(GRID[0]):
                put_main(land, d, SQUARE + PART * i, BLOCK, square, BLOCK * d, D * i)
                put_rest(land, d, SQUARE + PART * i, BLOCK, square, BLOCK * d, D * i)

        def pieces_after(mark):
            for piece in after[mark]:
                g.do(*piece)

        def tick(mark, index):
            for name, pieces in after.items():
                if name[:1] == mark and pieces:

                    @pl.when(index == int(name[1:]))
                    def _():
                        for piece in pieces:
                            g.do(*piece)
    else:
        fills = [
            pltpu.make_async_copy(src, dst, out_sem.at[i])
            for i, (src, dst) in enumerate(
                ((square_in, square), (down_in, down), (up_in, land.at[:, :, :, :, pl.ds(UP, DOWN - UP), :]))
            )
        ]
        for copy in fills:
            copy.start()
        vec_ref[...] = vec_in[...]
        bup[...] = bup_in[...]
        for copy in fills:
            copy.wait()
        tick = lambda mark, index: None
        unpack = pieces_after = lambda mark: None

    for i in range(3):
        unpack(i)
        for j in range(3):
            columns = slice(256 * j, 256 * (j + 1))
            part = product(in_ref[...], square[:, D * i + 256 * j : D * i + 256 * (j + 1)])
            if i != 1:
                part = part + vec_ref[i // 2 : i // 2 + 1, columns]
            part = part.astype(jnp.bfloat16)
            qkv[:, D * i + 256 * j : D * i + 256 * (j + 1)] = part
            qkv_turned[D * i + 256 * j : D * i + 256 * (j + 1), :] = jnp.transpose(part)
        pieces_after(f"Q{i}")
    save("qkv", qkv_turned, qkv_out)

    def prob_copy(p):
        return pltpu.make_async_copy(prob.at[p % 2], prob_out.at[p], pack_sem.at[0, p % 2])

    def turned_copy(p):
        at = pl.ds(pl.multiple_of(p * LEN, LEN), LEN)
        return pltpu.make_async_copy(turned.at[p % 2], turned_out.at[:, :, at], pack_sem.at[1, p % 2])

    def attend(p, carry):
        rows = pl.ds(pl.multiple_of(p * LEN, LEN), LEN)
        k = p % 2

        pl.when(p >= 2)(lambda: prob_copy(p - 2).wait())
        seg_row = seg_ref[pl.ds(base + p, 1), :].astype(jnp.float32)
        seg_col = jnp.transpose(jnp.broadcast_to(seg_row, (128, LEN)))
        same = jnp.concatenate([seg_col, seg_col], axis=1) == seg_row
        left = left_half((LEN, 128))
        for h in range(HEADS // 2):
            columns = slice(128 * h, 128 * (h + 1))
            query = qkv[rows, columns] * jnp.asarray(HEAD_DIM**-0.5, jnp.bfloat16)
            keys = qkv[rows, D + 128 * h : D + 128 * (h + 1)]
            values = qkv[rows, 2 * D + 128 * h : 2 * D + 128 * (h + 1)]
            mixes = []
            for side in range(2):
                mine = left if side == 0 else jnp.logical_not(left)
                scores = product_right(jnp.where(mine, query, jnp.zeros_like(query)), keys)
                scores = jnp.where(same, scores, MASKED)
                shifted = jnp.exp(scores - jnp.max(scores, axis=1, keepdims=True))
                total = jnp.sum(shifted, axis=1, keepdims=True)
                low = (shifted * (1.0 / total)).astype(jnp.bfloat16)
                prob[k, 2 * h + side] = low
                mixes.append(product(low, values))
            ctx[rows, columns] = jnp.where(left, mixes[0], mixes[1]).astype(jnp.bfloat16)
        prob_copy(p).start()
        tick("A", p)
        return carry

    lax.fori_loop(0, packs, attend, 0)
    unpack(3)
    save("square", square, square_out)
    prob_copy(packs - 2).wait()
    prob_copy(packs - 1).wait()

    def project(p, carry):
        rows = pl.ds(pl.multiple_of(p * LEN, LEN), LEN)
        k = p % 2

        @pl.when(p >= 2)
        def _():
            turned_copy(p - 2).wait()

        x = in_ref[rows, :]
        context = ctx[rows, :]
        total = x.astype(jnp.float32) + (product(context, square[:, 3 * D :]) + vec_ref[2:3, :D])
        normed, scale = norm_parts(total)
        value = normed * vec_ref[3:4, :D] + vec_ref[4:5, :D]
        first[rows, :] = value
        low = value.astype(jnp.bfloat16)
        flow[rows, :] = low
        norm[rows, :] = normed
        recip[rows, :] = jnp.broadcast_to(scale, (LEN, 128))
        turned[k, 0] = jnp.transpose(x)
        turned[k, 1] = jnp.transpose(context)
        turned[k, 2] = jnp.transpose(low)
        turned_copy(p).start()
        return carry

    lax.fori_loop(0, packs, project, 0)
    pieces_after("O0")
    save("norm", norm, norm1_out)
    save("recip", recip, recip1_out)
    turned_copy(packs - 2).wait()
    turned_copy(packs - 1).wait()

    def tile_copies(t):
        k = t % 2
        copies = []
        for n in range(GRID[1]):
            columns = pl.ds(pl.multiple_of(D * n + 128 * t, 128), 128)
            first_row = pl.multiple_of(UP + BLOCK * t, 16)
            copies += [
                pltpu.make_async_copy(slope.at[k, n], slope_out.at[:, columns], tile_sem.at[0, k, n]),
                pltpu.make_async_copy(act.at[:, columns], act_out.at[:, columns], tile_sem.at[1, k, n]),
                pltpu.make_async_copy(
                    land.at[:, :, n // 2, n % 2, pl.ds(first_row, BLOCK), :], up_out.at[:, :, :, columns], tile_sem.at[2, k, n]
                ),
            ]
        return copies

    def widen(t, carry):
        k = t % 2

        @pl.when(t >= 2)
        def _():
            for copy in tile_copies(t - 2):
                copy.wait()

        first_row = pl.multiple_of(UP + BLOCK * t, 16)
        for pair in range(2):
            weight = jnp.concatenate(
                [land[:, :, pair, i, pl.ds(first_row, BLOCK), :].reshape(D, 128) for i in range(2)], axis=1
            )
            bias = jnp.concatenate([bup[pl.ds(6 * (2 * pair + i) + t, 1), :] for i in range(2)], axis=1)
            for r in range(packs):
                rows = slice(LEN * r, LEN * (r + 1))
                value, turn = gelu_parts(product(flow[rows, :], weight) + bias)
                value, turn = value.astype(jnp.bfloat16), turn.astype(jnp.bfloat16)
                for i in range(2):
                    n = 2 * pair + i
                    columns = pl.ds(pl.multiple_of(D * n + 128 * t, 128), 128)
                    act[rows, columns] = value[:, 128 * i : 128 * (i + 1)]
                    slope[k, n, rows, :] = turn[:, 128 * i : 128 * (i + 1)]
        for copy in tile_copies(t):
            copy.start()
        tick("W", t)
        return carry

    lax.fori_loop(0, 6, widen, 0)
    def down_part(*tiles):
        if direct:
            for d in range(GRID[0]):
                for n in range(GRID[1]):
                    for t in tiles:
                        at = 384 * d + 128 * t
                        down[SIDE * n : SIDE * (n + 1), at : at + 128] = land[
                            d // 2, d % 2, n // 2, n % 2, DOWN + SIDE * t : DOWN + SIDE * (t + 1), :
                        ]
        spans = [slice(384 * d + 128 * t, 384 * d + 128 * (t + 1)) for d in range(GRID[0]) for t in tiles]
        for j in range(3):
            columns = slice(256 * j, 256 * (j + 1))
            weight = jnp.concatenate([down[columns, span] for span in spans], axis=1)
            for r in range(packs):
                rows = slice(LEN * r, LEN * (r + 1))
                hidden = jnp.concatenate([act[rows, span] for span in spans], axis=1)
                first[rows, columns] = first[rows, columns] + product_right(hidden, weight)

    down_part(0, 1)
    pieces_after("G0")
    down_part(2)
    save("down", down, down_out)
    pending["norm"].wait()
    pending["recip"].wait()

    def finish(p, carry):
        rows = pl.ds(pl.multiple_of(p * LEN, LEN), LEN)
        normed, scale = norm_parts(first[rows, :] + vec_ref[5:6, :D])
        norm[rows, :] = normed
        recip[rows, :] = jnp.broadcast_to(scale, (LEN, 128))
        mixed[rows, :] = (normed * vec_ref[6:7, :D] + vec_ref[7:8, :D]).astype(jnp.bfloat16)
        return carry

    lax.fori_loop(0, packs, finish, 0)
    save("mixed", mixed, mixed_out)
    save("norm2", norm, norm2_out)
    save("recip2", recip, recip2_out)
    for t in (4, 5):
        for copy in tile_copies(t):
            copy.wait()
    if direct:
        for k in range(CHUNKS):
            g.drain(k)
    for name, copy in pending.items():
        if name not in ("norm", "recip"):
            copy.wait()


def forward_step(direct, weights, inputs, segments, dp, narrow):
    rows = inputs.shape[0]
    packs = rows // LEN
    vmem = pl.BlockSpec(memory_space=pltpu.VMEM)
    anywhere = pl.BlockSpec(memory_space=pl.ANY)
    low = lambda *shape: jax.ShapeDtypeStruct(shape, jnp.bfloat16)
    full = lambda *shape: jax.ShapeDtypeStruct(shape, jnp.float32)
    room = lambda *shape: pltpu.VMEM(shape, jnp.bfloat16)
    wide = lambda *shape: pltpu.VMEM(shape, jnp.float32)
    sems = [pltpu.SemaphoreType.DMA((CHUNKS,)), pltpu.SemaphoreType.DMA((CHUNKS, 32))] if direct else []
    return pl.pallas_call(
        functools.partial(forward_kernel, direct),
        name="forward",
        out_shape=(
            low(D, FF), low(GRID[0] // 2, 2, BLOCK, FF), low(D, FF), full(16, 896),
            low(3 * D, rows), low(packs, HEADS, LEN, LEN), low(3, D, rows), full(rows, D), full(rows, 128),
            low(rows, FF), low(rows, FF), low(rows, D), full(rows, D), full(rows, 128),
        ),
        in_specs=([vmem] * 15 if direct else [anywhere] * 3 + [vmem] * 2) + [vmem] * 2,
        out_specs=(anywhere,) * 3 + (vmem,) + (anywhere,) * 10,
        scratch_shapes=[
            room(GRID[0] // 2, 2, GRID[1] // 2, 2, TOTAL, 128), room(D, FF), room(D, FF), wide(32, 128),
            room(rows, 3 * D), room(3 * D, rows), room(2, HEADS, LEN, LEN), room(2, 3, D, LEN), room(rows, D), wide(rows, D), room(rows, D),
            wide(rows, D), wide(rows, 128), room(rows, FF), room(2, 4, rows, 128), room(rows, D),
            pltpu.SemaphoreType.DMA((12,)), pltpu.SemaphoreType.DMA((2, 2)), pltpu.SemaphoreType.DMA((3, 2, 4)),
            *sems,
        ],
        compiler_params=pltpu.CompilerParams(
            vmem_limit_bytes=VMEM_LIMIT, **(dict(collective_id=0, has_side_effects=True) if direct else {})
        ),
    )(*weights, inputs, segments)


def transport_kernel(
    mixed_ref, seg_ref, kind_ref, weight_ref, cot_in, normed_in, recip_in, gain_ref,
    value_ref, second_out, branch_out, turned_out, sums_ref,
    kern_ref, prod_ref, flow_ref, acc_ref, left_ref, sigma_ref,
    cot_ref, normed_ref, recip_ref, second_ref, branch_ref, turned_ref, load_sem, save_sem,
):
    loads = [
        pltpu.make_async_copy(src, dst, load_sem.at[i])
        for i, (src, dst) in enumerate(((cot_in, cot_ref), (normed_in, normed_ref), (recip_in, recip_ref)))
    ]
    for copy in loads:
        copy.start()
    packs = mixed_ref.shape[0] // LEN
    base = lax.axis_index("narrow") * packs
    blocks = LEN // ROWS
    lanes = lambda col: jnp.concatenate([col, col], axis=1)
    fold = lambda wide: wide[:, :128] + wide[:, 128:]
    eight = lambda wide: jnp.sum(wide.reshape(ROWS // 8, 8, LEN), axis=0)
    replicate = lambda col: jnp.broadcast_to(col, (ROWS, 128))

    def turned(row):
        return jnp.transpose(jnp.broadcast_to(row, (128, LEN)))

    for p in range(packs):
        rows = pl.ds(p * LEN, LEN)
        feats = mixed_ref[rows, :].astype(jnp.float32)
        recip = lax.rsqrt(jnp.sum(feats * feats, axis=1, keepdims=True) + EPS_NORM)
        unit = (feats * recip).astype(jnp.bfloat16)
        cosine = product_right(unit, unit)
        seg_row = seg_ref[pl.ds(base + p, 1), :].astype(jnp.float32)
        region_row = jnp.where(kind_ref[pl.ds(base + p, 1), :] == 0, 0.0, 1.0)
        seg_col = turned(seg_row)
        word_col = 1.0 - turned(region_row)
        same = jnp.where(lanes(seg_col) == seg_row, 1.0, 0.0)
        word_count = jnp.sum(same * (1.0 - region_row), axis=1, keepdims=True)
        region_count = jnp.sum(same * lanes(1.0 - word_col), axis=0, keepdims=True)
        kern_ref[p] = jnp.exp((cosine - 1.0) * (1.0 / BETA)) * same * lanes(word_col) * region_row
        left_ref[p, 0] = word_col
        left_ref[p, 1] = jnp.broadcast_to(word_count, (LEN, 128))
        left_ref[p, 2] = 1.0 - word_col
        prod_ref[0, p] = jnp.ones((LEN, LEN), jnp.float32)
        sigma_ref[0, p, 0:1] = region_row / region_count
        sigma_ref[0, p, 1:2] = region_row
        sigma_ref[0, p, 2:3] = region_count

    def advance(t, carry):
        for p in range(packs):
            sigma = sigma_ref[t, p, 0:1]
            scale = jnp.where(t == 0, 1.0, sigma)
            region = sigma_ref[0, p, 1:2]
            count = sigma_ref[0, p, 2:3]
            total = jnp.zeros((8, LEN), jnp.float32)
            for b in range(blocks):
                rows = pl.ds(b * ROWS, ROWS)
                weighted = kern_ref[p, rows, :] * (prod_ref[t, p, rows, :] * scale)
                row_sum = jnp.sum(fold(weighted * sigma), axis=1, keepdims=True)
                word = left_ref[p, 0, rows, :]
                base = left_ref[p, 1, rows, :] * replicate(row_sum) + left_ref[p, 2, rows, :]
                delta = pl.reciprocal(base, approx=True)
                delta = word * delta * (2.0 - base * delta)
                scaled = weighted * lanes(delta)
                prod_ref[t + 1, p, rows, :] = scaled
                total = total + eight(scaled)
            col_sum = jnp.sum(total, axis=0, keepdims=True)
            sigma_ref[t + 1, p, 0:1] = region / (count * col_sum + 1.0 - region)
        return carry

    lax.fori_loop(0, ITERS, advance, 0)

    starts = []
    for p in range(packs):
        rows = pl.ds(p * LEN, LEN)
        weight = weight_ref[base + p]
        feats = mixed_ref[rows, :].astype(jnp.float32)
        recip = lax.rsqrt(jnp.sum(feats * feats, axis=1, keepdims=True) + EPS_NORM)
        unit = (feats * recip).astype(jnp.bfloat16)
        cosine = product_right(unit, unit)
        moved = (prod_ref[ITERS, p] * sigma_ref[ITERS, p, 0:1]) * (1.0 - cosine)
        value_ref[p : p + 1, :] = jnp.broadcast_to(jnp.sum(moved), (1, 128))
        moved = moved * weight
        flow_ref[p] = moved
        acc_ref[p] = jnp.zeros((LEN, LEN), jnp.float32)
        starts += [jnp.sum(moved, axis=0, keepdims=True), jnp.zeros((1, LEN), jnp.float32)]

    def retreat(step, carry):
        t = ITERS - 1 - step
        out = []
        for p in range(packs):
            flow_sum, spread = carry[2 * p : 2 * p + 2]
            before = sigma_ref[t, p, 0:1]
            d_col = -sigma_ref[0, p, 2:3] * sigma_ref[t + 1, p, 0:1] * (spread + flow_sum)
            total = jnp.zeros((8, LEN), jnp.float32)
            shift = jnp.zeros((8, LEN), jnp.float32)
            for b in range(blocks):
                rows = pl.ds(b * ROWS, ROWS)
                scaled = prod_ref[t + 1, p, rows, :]
                flow = flow_ref[p, rows, :] + scaled * d_col
                d_row = replicate(jnp.sum(fold(flow), axis=1, keepdims=True))
                d_row = -left_ref[p, 1, rows, :] * d_row
                moved = scaled * lanes(d_row)
                flow = flow + moved * before
                flow_ref[p, rows, :] = flow
                acc_ref[p, rows, :] = acc_ref[p, rows, :] + flow
                total = total + eight(flow)
                shift = shift + eight(moved)
            out += [
                jnp.sum(total, axis=0, keepdims=True),
                before * jnp.sum(shift, axis=0, keepdims=True),
            ]
        return tuple(out)

    lax.fori_loop(0, ITERS, retreat, tuple(starts))

    for copy in loads:
        copy.wait()
    saves = []
    sums = [jnp.zeros((1, D), jnp.float32)] * 3
    for p in range(packs):
        rows = pl.ds(p * LEN, LEN)
        coupling = prod_ref[ITERS, p] * sigma_ref[ITERS, p, 0:1]
        d_cost = weight_ref[base + p] * coupling - acc_ref[p] * (1.0 / BETA)
        d_cosine = (-d_cost).astype(jnp.bfloat16)
        feats = mixed_ref[rows, :].astype(jnp.float32)
        recip = lax.rsqrt(jnp.sum(feats * feats, axis=1, keepdims=True) + EPS_NORM)
        unit = feats * recip
        unit_low = unit.astype(jnp.bfloat16)
        d_unit = product(d_cosine, unit_low) + product_left(d_cosine, unit_low)
        d_mixed = cot_ref[rows, :].astype(jnp.float32) + recip * (
            d_unit - unit * jnp.sum(d_unit * unit, axis=1, keepdims=True)
        )
        normed = normed_ref[rows, :]
        scaled = d_mixed * gain_ref[6:7, :D]
        inner_mean = jnp.mean(scaled, axis=1, keepdims=True)
        cross_mean = jnp.mean(scaled * normed, axis=1, keepdims=True)
        d_second = recip_ref[rows, 0:1] * (scaled - inner_mean - normed * cross_mean)
        d_branch = d_second.astype(jnp.bfloat16)
        second_ref[rows, :] = d_second
        branch_ref[rows, :] = d_branch
        turned_ref[:, rows] = jnp.transpose(d_branch)
        for src, dst in (
            (second_ref.at[rows, :], second_out.at[rows, :]),
            (branch_ref.at[rows, :], branch_out.at[rows, :]),
            (turned_ref.at[:, rows], turned_out.at[:, rows]),
        ):
            copy = pltpu.make_async_copy(src, dst, save_sem.at[len(saves)])
            copy.start()
            saves.append(copy)
        sums[0] = sums[0] + jnp.sum(d_mixed * normed, axis=0, keepdims=True)
        sums[1] = sums[1] + jnp.sum(d_mixed, axis=0, keepdims=True)
        sums[2] = sums[2] + jnp.sum(d_branch.astype(jnp.float32), axis=0, keepdims=True)
    for k in range(3):
        sums_ref[k : k + 1, :] = sums[k]
    for copy in saves:
        copy.wait()


def transport_step(mixed, segments, row_kind, weight, cotangent, normed, recip, gain):
    rows = mixed.shape[0]
    packs = rows // LEN
    vmem = pl.BlockSpec(memory_space=pltpu.VMEM)
    anywhere = pl.BlockSpec(memory_space=pl.ANY)
    square = (packs, LEN, LEN)
    return pl.pallas_call(
        transport_kernel,
        name="transport",
        out_shape=(
            jax.ShapeDtypeStruct((packs, 128), jnp.float32),
            jax.ShapeDtypeStruct((rows, D), jnp.float32),
            jax.ShapeDtypeStruct((rows, D), jnp.bfloat16),
            jax.ShapeDtypeStruct((D, rows), jnp.bfloat16),
            jax.ShapeDtypeStruct((8, D), jnp.float32),
        ),
        in_specs=[vmem, vmem, vmem, pl.BlockSpec(memory_space=pltpu.SMEM), anywhere, anywhere, anywhere, vmem],
        out_specs=(vmem, anywhere, anywhere, anywhere, vmem),
        scratch_shapes=[
            pltpu.VMEM(square, jnp.float32),
            pltpu.VMEM((ITERS + 1, *square), jnp.float32),
            pltpu.VMEM(square, jnp.float32),
            pltpu.VMEM(square, jnp.float32),
            pltpu.VMEM((packs, 3, LEN, 128), jnp.float32),
            pltpu.VMEM((ITERS + 1, packs, 8, LEN), jnp.float32),
            pltpu.VMEM((rows, D), jnp.bfloat16),
            pltpu.VMEM((rows, D), jnp.float32),
            pltpu.VMEM((rows, 128), jnp.float32),
            pltpu.VMEM((rows, D), jnp.float32),
            pltpu.VMEM((rows, D), jnp.bfloat16),
            pltpu.VMEM((D, rows), jnp.bfloat16),
            pltpu.SemaphoreType.DMA((3,)),
            pltpu.SemaphoreType.DMA((3 * packs,)),
        ],
        compiler_params=pltpu.CompilerParams(vmem_limit_bytes=VMEM_LIMIT),
    )(mixed, segments, row_kind, weight, cotangent, normed, recip, gain)


REST, OUT, MAIN = 16, 160, 304
SCATTER_ROWS = (80, 80, 80, 64, 80, 64, 80, 64) + (144,) * 4 + (96,) * 6
SCATTER_AXES = (
    "zyx", "yxz", "xyz", "xyz", "yxz", "xyz", "xyz", "xyz", "zxy", "xyz", "yxz", "xyz", "xyz", "yxz", "yxz", "zyx",
    "xyz", "yxz",
)
BACKWARD_ORDER = (
    500, 12, 13, 501, 14, 15, 502, 16, 17, 112, 113, 600, 114, 601, 115, 116, 602, 117, 603, 700, 701, 8, 702, 9, 212,
    213, 703, 704, 10, 108, 109, 705, 11, 216, 214, 800, 110, 313, 111, 801, 215, 802, 217, 803, 312, 900, 2, 3, 209,
    316, 1000, 102, 314, 1001, 103, 1002, 1003, 208, 210, 315, 1004, 211, 413, 1005, 309, 317, 1006, 412, 1007, 202,
    416, 1100, 4, 5, 6, 7, 311, 414, 1200, 104, 203, 1201, 105, 106, 107, 302, 308, 409, 1202, 310, 417, 1203, 415,
    1300, 0, 1, 204, 205, 303, 402, 411, 1400, 100, 101, 408, 1401, 206, 410, 1402, 305, 403, 207, 1403, 304, 201,
    306, 307, 200, 301, 405, 404, 300, 406, 407, 400, 401,
)


class Scatter:
    def __init__(self, part, lands, send_sem, recv_sem, total):
        self.part, self.lands, self.send_sem, self.recv_sem, self.total = part, lands, send_sem, recv_sem, total
        self.me = hops()
        self.depth = part.shape[0]

    def copies(self, k):
        first, order = sum(SCATTER_ROWS[:k]), SCATTER_AXES[k]
        span = pl.ds(first, SCATTER_ROWS[k])
        every = slice(None)
        z, x, y, core = self.me
        part = lambda *at: self.part.at[*at, span, :]
        land_c, land_q, land_p, land_z = self.lands
        land = lambda ref, *at: ref.at[*at, span, :]
        to_x, to_y = (0, 1, 0, 0), (0, 0, 1, 0)
        stages = {"c": [], "3": [], "2": [], "1": []}
        ahead = lambda far: lax.rem(z + far, self.depth)
        if order[0] == "y":
            stages["c"] = [
                (part(every, every, 1 - y, 1 - core), land(land_c, every, every, 1 - y), None, part(every, every, 1 - y, core)),
                (part(every, every, y, 1 - core), land(land_c, every, every, y), None, part(every, every, y, core)),
            ]
        elif order[0] == "x":
            stages["c"] = [
                (part(every, 1 - x, every, 1 - core), land(land_c, every, 1 - x, every), None, part(every, 1 - x, every, core)),
                (part(every, x, every, 1 - core), land(land_c, every, x, every), None, part(every, x, every, core)),
            ]
        else:
            stages["c"] = [(part(every, every, every, 1 - core), land(land_c, every, every, every), None, part(every, every, every, core))]
        if order == "yxz":
            stages["3"] = [(part(every, every, 1 - y, core), land(land_q, every, every), to_y, part(every, every, y, core))]
            stages["2"] = [(part(every, 1 - x, y, core), land(land_p, every), to_x, part(every, x, y, core))]
        elif order == "xyz":
            stages["3"] = [(part(every, 1 - x, every, core), land(land_q, every, every), to_x, part(every, x, every, core))]
            stages["2"] = [(part(every, x, 1 - y, core), land(land_p, every), to_y, part(every, x, y, core))]
        else:
            for far in range(1, self.depth):
                for i in range(2):
                    slot = 2 * (far - 1) + i
                    where = land(land_q, slot, every) if slot < 4 else land(land_p, slice(2 * slot - 8, 2 * slot - 6))
                    stages["3"].append((part(ahead(far), i, every, core), where, (far, 0, 0, 0), part(z, i, every, core)))
            pair, last = land(land_z, slice(0, 2)), land(land_z, 2)
            if order[1] == "y":
                stages["2"] = [(part(z, every, 1 - y, core), pair, to_y, part(z, every, y, core))]
                stages["1"] = [(part(z, 1 - x, y, core), last, to_x, part(z, x, y, core))]
            else:
                stages["2"] = [(part(z, 1 - x, every, core), pair, to_x, part(z, x, every, core))]
                stages["1"] = [(part(z, x, 1 - y, core), last, to_y, part(z, x, y, core))]
        if order[2] == "z":
            stages["1"] = [
                (part(ahead(far), x, y, core), land(land_z, far - 1), (far, 0, 0, 0), part(z, x, y, core))
                for far in range(1, self.depth)
            ]
        made, mark = {}, 0
        for stage, items in stages.items():
            made[stage] = []
            for src, dst, hop, into in items:
                if stage != "c":
                    copy = functools.partial(self.copy, k, mark, src, dst, hop)
                    made[stage].append((copy, dst, into))
                    mark += 1
                else:
                    made[stage].append((None, dst, into))
        whole = functools.partial(
            self.copy, k, mark, part(every, every, every, 1 - core), land(land_c, every, every, every), (0, 0, 0, 1)
        )
        return whole, made

    def copy(self, k, mark, src, dst, hop):
        return pltpu.make_async_remote_copy(
            src_ref=src,
            dst_ref=dst,
            send_sem=self.send_sem.at[k, mark],
            recv_sem=self.recv_sem.at[k, mark],
            device_id=place(self.me, self.depth, hop),
            device_id_type=MESH,
        )

    def do(self, kind, k):
        whole, made = self.copies(k)
        if kind == "s":
            whole().start()
            return
        if kind == "c":
            whole().wait_recv()
        following = {"c": "3", "3": "2", "2": "1"}.get(kind)
        first, rows = sum(SCATTER_ROWS[:k]), SCATTER_ROWS[k]
        for i, (copy, land, into) in enumerate(made[kind]):
            if kind != "c":
                copy().wait_recv()
            if kind != "1":
                into[...] = into[...] + land[...]
            if kind == "c" and i == 0 and len(made["c"]) == 2:
                made["3"][0][0]().start()
        if kind == "1":
            value = made["1"][0][2][...].astype(jnp.float32)
            for copy, land, into in made["1"]:
                value = value + land[...].astype(jnp.float32)
            self.total[pl.ds(first, rows), :] = value
        elif not (kind == "c" and len(made["c"]) == 2):
            for copy, land, into in made[following]:
                copy().start()

    def drain(self, k):
        whole, made = self.copies(k)
        whole().wait_send()
        for stage in "321":
            for copy, land, into in made[stage]:
                copy().wait_send()


def fold_middle(top, low):
    left = left_half(top.shape)
    return jnp.where(left, top, swap(low)), jnp.where(left, swap(low), top)


def take_main(part, d, pair, at, even, other):
    rows = even.shape[0]
    part[d // 2, d % 2, pair, 0, at : at + rows, :] = even.astype(jnp.bfloat16)
    part[d // 2, d % 2, pair, 1, at : at + rows, :] = other.astype(jnp.bfloat16)


def take_rest(part, d, pair, at, block):
    half = block.shape[0] // 2
    one, two = fold_middle(block[:half], block[half:])
    take_main(part, d, pair, at, one, two)


def unpack_block(main, rest, odd):
    other = swap(rest)
    top, low = jnp.where(odd, other, rest), jnp.where(odd, rest, other)
    piece = jnp.concatenate([top, low], axis=0)
    left = left_half(piece.shape)
    swapped = swap(main)
    first = jnp.where(odd, jnp.where(left, piece, swapped), main)
    second = jnp.where(odd, swapped, piece)
    return jnp.concatenate([first, second], axis=1)


def backward_kernel(direct, *refs):
    (act_in, slope_in, branch_in, branch_turned_in, second_in, sums_in, turned_in, norm_in, recip_in, qkv_in, prob_in,
     square_in, up_in, down_in, vec_ref, value_ref) = refs[:16]
    refs = refs[16:]
    if direct:
        grad_in_out, total = refs[:2]
        refs = refs[2:]
    else:
        grad_in_out, gsquare_ref, gup_ref, gdown_ref, gvec_ref, gbup_ref = refs[:6]
        refs = refs[6:]
    (turned, slope, square, up, flow, norm, recip, branch, branch_turned, prob, sums, bup, load_sem, prob_sem,
     out_sem) = refs[:15]
    rows_all = slope.shape[0]
    packs = rows_all // LEN
    if direct:
        part, land_c, land_q, land_p, land_z, send_sem, recv_sem = refs[15:22]
        g = Scatter(part, (land_c, land_q, land_p, land_z), send_sem, recv_sem, total)
        dp, narrow = lax.axis_index("dp"), lax.axis_index("narrow")
    else:
        (stage,) = refs[15:16]

    loads, waited = {}, set()

    def load(name, *pairs):
        loads[name] = []
        for src, dst in pairs:
            copy = pltpu.make_async_copy(src, dst, load_sem.at[sum(map(len, loads.values()))])
            copy.start()
            loads[name].append(copy)

    def need(*names):
        for name in names:
            if name not in waited:
                waited.add(name)
                for copy in loads[name]:
                    copy.wait()

    blocks = [pl.ds(rows_all * i, rows_all) for i in range(3)]
    load("turned branch", (branch_turned_in, branch_turned))
    load("act", *[(act_in.at[:, span], turned.at[span, :]) for span in blocks])
    if direct:
        greet(g.me, g.depth)
    sums[...] = jnp.zeros_like(sums)
    bup[...] = jnp.zeros_like(bup)
    sums[5:6, :D] = sums_in[2:3, :]
    sums[6:7, :D] = sums_in[0:1, :]
    sums[7:8, :D] = sums_in[1:2, :]

    def put(src, dst):
        copy = pltpu.make_async_copy(src, dst, out_sem.at[0])
        copy.start()
        copy.wait()

    def put_down(t):
        at = pl.ds(pl.multiple_of(DOWN + SIDE * t, 16), SIDE)

        def two(i, carry):
            tiles = []
            for j in range(2):
                tile = 3 * (2 * i + j) + t
                rows = pl.ds(pl.multiple_of(tile // 8 * rows_all, 128), rows_all)
                tiles.append(turned[rows, pl.ds(pl.multiple_of(tile % 8 * 128, 128), 128)])
            grad = product(branch_turned[...], jnp.concatenate(tiles, axis=1))
            for j in range(2):
                block = grad[:, 128 * j : 128 * (j + 1)]
                if direct:
                    for n in range(GRID[1]):
                        part[i, j, n // 2, n % 2, at, :] = block[SIDE * n : SIDE * (n + 1)].astype(jnp.bfloat16)
                else:
                    stage[:, :128] = block
                    columns = pl.ds(pl.multiple_of(384 * (2 * i + j) + 128 * t, 128), 128)
                    put(stage.at[:, pl.ds(0, 128)], gdown_ref.at[:, columns])
            return carry

        lax.fori_loop(0, 4, two, 0)

    def narrow_down(c):
        at = pl.multiple_of(256 * c, 128)
        columns = pl.ds(at, 256)
        weight = square[:, columns]
        column_sum = jnp.zeros((1, 256), jnp.float32)
        for r in range(packs):
            rows = slice(LEN * r, LEN * (r + 1))
            value = product(branch[rows, :], weight) * slope[rows, columns].astype(jnp.float32)
            low = value.astype(jnp.bfloat16)
            slope[rows, columns] = low
            column_sum = column_sum + jnp.sum(low.astype(jnp.float32), axis=0, keepdims=True)
        bup[pl.ds(2 * c, 1), :] = column_sum[:, :128]
        bup[pl.ds(2 * c + 1, 1), :] = column_sum[:, 128:]

    def put_up(t, pair):
        first_row = pl.multiple_of(UP + BLOCK * t, 16)
        at = [pl.multiple_of(D * (2 * pair + j) + 128 * t, 128) for j in range(2)]
        columns = jnp.concatenate([slope[:, pl.ds(at[j], 128)] for j in range(2)], axis=1)
        grad = product(turned[2 * D : 3 * D, :], columns)
        for j in range(2):
            block = grad[:, 128 * j : 128 * (j + 1)]
            if direct:
                part[:, :, pair, j, pl.ds(first_row, BLOCK), :] = block.astype(jnp.bfloat16).reshape(
                    GRID[0] // 2, 2, BLOCK, 128
                )
            else:
                stage[:, :128] = block
                put(stage.at[:, pl.ds(0, 128)], gup_ref.at[:, pl.ds(at[j], 128)])

    def norm_back(r):
        rows = pl.ds(pl.multiple_of(r * LEN, LEN), LEN)
        d_first = flow[rows, :]
        for i in range(3):
            d_first = d_first + product_right(slope[rows, rows_all * i : rows_all * (i + 1)], up[D * i : D * (i + 1), :])
        normed = norm[rows, :]
        scaled = d_first * vec_ref[3:4, :D]
        inner_mean = jnp.mean(scaled, axis=1, keepdims=True)
        cross_mean = jnp.mean(scaled * normed, axis=1, keepdims=True)
        d_sum = recip[rows, 0:1] * (scaled - inner_mean - normed * cross_mean)
        flow[rows, :] = d_sum
        low = d_sum.astype(jnp.bfloat16)
        branch[rows, :] = low
        sums[3:4, :D] += jnp.sum(d_first * normed, axis=0, keepdims=True)
        sums[4:5, :D] += jnp.sum(d_first, axis=0, keepdims=True)
        sums[2:3, :D] += jnp.sum(low.astype(jnp.float32), axis=0, keepdims=True)

    def put_out():
        for pair in range(2):
            grad = product(turned[D : 2 * D, :], branch[:, 384 * pair : 384 * (pair + 1)])
            if direct:
                for d in range(GRID[0]):
                    block = grad[BLOCK * d : BLOCK * (d + 1)]
                    take_main(part, d, pair, OUT, block[:, :128], block[:, 256:])
                    take_rest(part, d, pair, OUT + BLOCK, block[:, 128:256])
            else:
                stage[:, :384] = grad
                put(stage.at[:, pl.ds(0, 384)], gsquare_ref.at[pl.ds(3 * D, D), pl.ds(384 * pair, 384)])

    def context_back():
        for r in range(packs):
            rows = slice(LEN * r, LEN * (r + 1))
            turned[3 * D :, rows] = product_right(square[:, 3 * D :], branch[rows, :]).astype(jnp.bfloat16)
        for r in range(packs):
            rows = slice(LEN * r, LEN * (r + 1))
            branch[rows, :] = product_right(branch[rows, :], square[:, 3 * D :]).astype(jnp.bfloat16)

    def unit_of(j, step):
        i, p = j // (packs // 2), 2 * (j % (packs // 2))
        return (i + (i + 1) // 2 if step == "T" else 3 * i + 1), p

    def prob_copy(j, step):
        h, p = unit_of(j, step)
        return pltpu.make_async_copy(prob_in.at[pl.ds(p, 2), pl.ds(2 * h, 2)], prob.at[j % 3], prob_sem.at[j % 3])

    def attend(j, step, count):
        h, p = unit_of(j, step)
        pl.when(j + 2 < count)(lambda: prob_copy(j + 2, step).start())
        prob_copy(j, step).wait()
        tile = pl.multiple_of(128 * h, 128)
        left = left_half((LEN, 128))
        at = [[pl.ds(pl.multiple_of(D * i + tile + 64 * side, 64), 64) for i in range(4)] for side in range(2)]
        parts = []
        for q in range(2):
            rows = pl.ds(pl.multiple_of((p + q) * LEN, LEN), LEN)
            context = branch[rows, pl.ds(tile, 128)]
            all_values = up[pl.ds(pl.multiple_of(2 * D + tile, 128), 128), rows]
            for side in range(2):
                mine = left if side == 0 else jnp.logical_not(left)
                d_prob = product(jnp.where(mine, context, jnp.zeros_like(context)), all_values)
                low = prob[j % 3, q, side]
                share = low.astype(jnp.float32)
                moved = share * d_prob
                d_scores = (moved - share * jnp.sum(moved, axis=1, keepdims=True)).astype(jnp.bfloat16)
                d_values = product(turned[at[side][3], rows], low)
                d_query = product_right(up[at[side][1], rows], d_scores) * HEAD_DIM**-0.5
                d_keys = product(up[at[side][0], rows], d_scores) * HEAD_DIM**-0.5
                parts.append((side, rows, [item.astype(jnp.bfloat16) for item in (d_query, d_keys, d_values)]))
        for side, rows, items in parts:
            for i in range(3):
                up[at[side][i], rows] = items[i]

    def put_tiles(tiles, at):
        for i in range(3):
            for one, two in tiles:
                right = jnp.concatenate(
                    [up[D * i + 128 * one : D * i + 128 * (one + 1), :], up[D * i + 128 * two : D * i + 128 * (two + 1), :]]
                )
                grad = product_right(turned[0:D, :], right)
                if direct:
                    for d in range(GRID[0]):
                        block = grad[BLOCK * d : BLOCK * (d + 1)]
                        if len(tiles) == 2:
                            take_main(part, d, one // 3, at + BLOCK * i, block[:, :128], block[:, 128:])
                        else:
                            take_rest(part, d, 0, at + BLOCK // 2 * i, block[:, :128])
                            take_rest(part, d, 1, at + BLOCK // 2 * i, block[:, 128:])
                else:
                    for k, tile in enumerate((one, two)):
                        stage[:, :128] = grad[:, 128 * k : 128 * (k + 1)]
                        put(stage.at[:, pl.ds(0, 128)], gsquare_ref.at[pl.ds(D * i, D), pl.ds(128 * tile, 128)])

    def put_vectors():
        ones = jnp.ones((8, rows_all), jnp.bfloat16)
        sums[0:1, :D] = product_right(ones, up[0:D, :])[0:1]
        sums[1:2, :D] = product_right(ones, up[2 * D : 3 * D, :])[0:1]
        if direct:
            lane = lax.broadcasted_iota(jnp.int32, (1, 128), 1)
            value = jnp.zeros((1, 128), jnp.float32)
            for p in range(packs):
                value = jnp.where(lane == narrow * packs + p, value_ref[p : p + 1, :], value)
            high = value.astype(jnp.bfloat16).astype(jnp.float32)
            zeros = jnp.zeros((3, 128), jnp.float32)
            for d in range(GRID[0]):
                at, shift = divmod(BLOCK * d, 128)
                wide = sums[:, 128 * at : 128 * at + 256]
                wide = pltpu.roll(wide, 256 - shift, 1) if shift else wide
                mine = lax.broadcasted_iota(jnp.int32, (8, 128), 1) < BLOCK
                own = jnp.where(dp == d, 1.0, 0.0)
                tile = jnp.concatenate(
                    [jnp.where(mine, wide[:8, :128], 0.0), bup[3 * d : 3 * d + 3, :], high * own, (value - high) * own, zeros]
                )
                for n in range(GRID[1]):
                    part[d // 2, d % 2, n // 2, n % 2, 0:16, :] = tile.astype(jnp.bfloat16)

    def widen_back(r):
        rows = pl.ds(pl.multiple_of(r * LEN, LEN), LEN)
        value = product(square[:, :D], up[:D, rows])
        for i in (1, 2):
            value = value + product(square[:, D * i : D * (i + 1)], up[D * i : D * (i + 1), rows])
        norm[rows, :] = flow[rows, :] + jnp.transpose(value)

    after = split_order(BACKWARD_ORDER, "sc321", "DNUBOTMXRW")

    def tick(mark, index=None):
        if not direct:
            return
        for name, pieces in after.items():
            if name[:1] == mark and pieces:
                if index is None:
                    for piece in pieces:
                        g.do(*piece)
                else:

                    @pl.when(index == int(name[1:]))
                    def _():
                        for piece in pieces:
                            g.do(*piece)

    def repeat(mark, first, last, body):
        def step(i, carry):
            body(i)
            tick(mark, i)
            return carry

        lax.fori_loop(first, last, step, 0)

    def up_pair(t):
        put_up(t, 0)
        put_up(t, 1)

    def down_three(i):
        for j in range(3):
            narrow_down(3 * i + j)

    groups = []
    for name in [name for name in after if name]:
        if groups and groups[-1][0] == name[0]:
            groups[-1][1].append(int(name[1:]))
        else:
            groups.append((name[0], [int(name[1:])]))
    for mark, span in groups:
        first, last = span[0], span[-1] + 1
        if mark == "D":
            need("turned branch", "act")
            load("branch", (branch_in, branch))
            load("down", (down_in, square))
            load("slope", (slope_in, slope))
            load("up", *[(up_in.at[:, pl.ds(rows_all * i, rows_all)], up.at[pl.ds(D * i, D), :]) for i in range(3)])
            load("flow", (second_in, flow))
            load("norm", (norm_in, norm))
            load("recip", (recip_in, recip))
            repeat("D", first, last, put_down)
            load("turned", (turned_in, turned.at[pl.ds(0, 3 * D), :]))
        elif mark == "N":
            need("branch", "down", "slope")
            repeat("N", first, last, down_three)
            load("square", (square_in, square))
        elif mark == "U":
            need("turned")
            repeat("U", first, last, up_pair)
        elif mark == "B":
            need("up", "flow", "norm", "recip")
            repeat("B", first, last, norm_back)
            load("qkv", (qkv_in, up))
            for j in range(2):
                prob_copy(j, "T").start()
        elif mark == "O":
            need("turned", "square")
            put_out()
            context_back()
            tick("O", None)
        elif mark == "T":
            need("qkv")
            repeat("T", first, last, lambda j: attend(j, "T", 2 * packs))
            for j in range(2):
                prob_copy(j, "X").start()
        elif mark == "M":
            put_tiles(((0, 2), (3, 5)), MAIN)
            tick("M")
        elif mark == "X":
            repeat("X", first, last, lambda j: attend(j, "X", packs))
        elif mark == "R":
            put_tiles(((1, 4),), REST)
            put_vectors()
            tick("R")
        elif mark == "W":
            repeat("W", first, last, widen_back)
            result = pltpu.make_async_copy(norm, grad_in_out, out_sem.at[1])
            result.start()
    if direct:
        for k in range(len(SCATTER_ROWS)):
            g.drain(k)
    else:
        gvec_ref[...] = sums[...]
        gbup_ref[...] = bup[...]
    result.wait()


def backward_step(direct, operands, dp, narrow):
    rows = operands[1].shape[0]
    vmem = pl.BlockSpec(memory_space=pltpu.VMEM)
    anywhere = pl.BlockSpec(memory_space=pl.ANY)
    full = lambda *shape: jax.ShapeDtypeStruct(shape, jnp.float32)
    room = lambda *shape: pltpu.VMEM(shape, jnp.bfloat16)
    wide = lambda *shape: pltpu.VMEM(shape, jnp.float32)
    if direct:
        outs, places = [full(TOTAL, 128)], [vmem]
        depth = dp // 2
        count = len(SCATTER_ROWS)
        extra = [
            room(depth, 2, 2, 2, TOTAL, 128), room(depth, 2, 2, TOTAL, 128), room(depth, 2, TOTAL, 128),
            room(depth, TOTAL, 128), room(depth - 1, TOTAL, 128),
            pltpu.SemaphoreType.DMA((count, 12)), pltpu.SemaphoreType.DMA((count, 12)),
        ]
    else:
        outs = [full(FF, D), full(D, FF), full(D, FF), full(16, 896), full(32, 128)]
        places = [anywhere] * 3 + [vmem] * 2
        extra = [wide(D, D)]
    return pl.pallas_call(
        functools.partial(backward_kernel, direct),
        name="backward",
        out_shape=(full(rows, D), *outs),
        in_specs=[anywhere] * 5 + [vmem] + [anywhere] * 8 + [vmem] * 2,
        out_specs=(anywhere, *places),
        scratch_shapes=[
            room(FF, rows), room(rows, FF), room(D, FF), room(3 * D, rows), wide(rows, D), wide(rows, D), wide(rows, 128),
            room(rows, D), room(D, rows), room(3, 2, 2, LEN, LEN), wide(16, 896), wide(32, 128),
            pltpu.SemaphoreType.DMA((20,)), pltpu.SemaphoreType.DMA((3,)), pltpu.SemaphoreType.DMA((2,)),
            *extra,
        ],
        compiler_params=pltpu.CompilerParams(
            vmem_limit_bytes=VMEM_LIMIT, **(dict(collective_id=1, has_side_effects=True) if direct else {})
        ),
    )(*operands)


def collect_kernel(packs_all, total, group_in, grad_in, *refs):
    (group_out, loss, grad_out, gq, gqb, gk, gv, gvb, go, gob, gfg, gfs, gup, gupb, gdown, gdownb, gsg, gss, group, grad, in_sem, out_sem) = refs
    parts = [(group_in, group, group_out, i) for i in range(group.shape[0] // LEN)]
    parts += [(grad_in, grad, grad_out, i) for i in range(grad.shape[0] // LEN)]
    ins, outs = [], []
    for k, (src, via, dst, i) in enumerate(parts):
        rows = pl.ds(LEN * i, LEN)
        ins.append(pltpu.make_async_copy(src.at[rows, :], via.at[rows, :], in_sem.at[k]))
        outs.append(pltpu.make_async_copy(via.at[rows, :], dst.at[rows, :], out_sem.at[k]))
        ins[-1].start()
    odd = lax.rem(lax.axis_index("narrow"), 2) == 1
    for one, two in zip(ins, outs):
        one.wait()
        two.start()
    for i, ref in enumerate((gqb, gvb, gob, gfg, gfs, gdownb, gsg, gss)):
        ref[...] = total[i : i + 1, :BLOCK]
    gupb[...] = total[8:11, :]
    loss[...] = (total[11:12, :] + total[12:13, :])[:, :packs_all]
    for t in range(6):
        gup[:, 128 * t : 128 * (t + 1)] = total[UP + BLOCK * t : UP + BLOCK * (t + 1), :]
    for ref, main, rest in (
        (gq, MAIN, REST), (gk, MAIN + BLOCK, REST + BLOCK // 2), (gv, MAIN + 2 * BLOCK, REST + BLOCK), (go, OUT, OUT + BLOCK),
    ):
        block = unpack_block(total[main : main + BLOCK, :], total[rest : rest + BLOCK // 2, :], odd)
        ref[...] = block[:, :192]
    for t in range(3):
        gdown[:, 128 * t : 128 * (t + 1)] = total[DOWN + SIDE * t : DOWN + SIDE * (t + 1), :]
    for copy in outs:
        copy.wait()


def collect_step(total, group, grad_inputs, dp, narrow):
    packs_all = group.shape[0] // LEN
    vmem = pl.BlockSpec(memory_space=pltpu.VMEM)
    anywhere = pl.BlockSpec(memory_space=pl.ANY)
    full = lambda *shape: jax.ShapeDtypeStruct(shape, jnp.float32)
    square, vector = full(D // dp, D // narrow), full(1, D // dp)
    count = (group.shape[0] + grad_inputs.shape[0]) // LEN
    out = pl.pallas_call(
        functools.partial(collect_kernel, packs_all),
        name="collect",
        out_shape=(
            jax.ShapeDtypeStruct(group.shape, group.dtype), full(1, packs_all), full(*grad_inputs.shape),
            square, vector, square, square, vector, square, vector, vector, vector,
            full(D // dp, FF // narrow), full(FF // dp // 128, 128), full(D // narrow, FF // dp), vector, vector, vector,
        ),
        in_specs=[vmem, anywhere, anywhere],
        out_specs=(anywhere, vmem, anywhere) + (vmem,) * 15,
        scratch_shapes=[
            pltpu.VMEM(group.shape, group.dtype), pltpu.VMEM(grad_inputs.shape, jnp.float32),
            pltpu.SemaphoreType.DMA((count,)), pltpu.SemaphoreType.DMA((count,)),
        ],
        compiler_params=pltpu.CompilerParams(vmem_limit_bytes=VMEM_LIMIT),
    )(total, group, grad_inputs)
    out = [item.reshape(-1) if item.shape[0] in (1, 3) else item for item in out]
    out[14] = out[14].T
    return tuple(out)


def per_device(
    inputs,
    segments,
    row_kind,
    query_weight,
    query_bias,
    key_weight,
    value_weight,
    value_bias,
    output_weight,
    output_bias,
    first_gain,
    first_shift,
    up_weight,
    up_bias,
    down_weight,
    down_bias,
    second_gain,
    second_shift,
    out_cotangent,
    loss_cotangent,
):
    row_count = inputs.shape[0]
    matrices = (query_weight, key_weight, value_weight, output_weight, up_weight, down_weight)
    vectors = (
        query_bias,
        value_bias,
        output_bias,
        first_gain,
        first_shift,
        down_bias,
        second_gain,
        second_shift,
        up_bias,
    )
    dp, narrow = lax.axis_size("dp"), lax.axis_size("narrow")
    direct = (dp, narrow, row_count) == (*GRID, 4 * LEN)
    if direct:
        weights = (*matrices[:5], down_weight.T, *[item.reshape(1, -1) for item in vectors[:8]], up_bias.reshape(-1, 128))
    else:
        weights = fetch_weights(matrices, vectors)
    (square, up, down, vecs, qkv, prob, turned, norm_first, recip_first, active, slope, output_low, norm_second,
     recip_second) = forward_step(direct, weights, inputs, segments, dp, narrow)
    group_out = lax.all_gather(output_low, "narrow", axis=0, tiled=True)
    partial_value, d_second, d_branch, branch_turned, sums_second = transport_step(
        output_low, segments, row_kind, loss_cotangent, out_cotangent, norm_second, recip_second, vecs
    )
    grad_inputs, *grads = backward_step(
        direct,
        (active, slope, d_branch, branch_turned, d_second, sums_second, turned.reshape(3 * D, row_count), norm_first, recip_first, qkv, prob, square,
         up.reshape(D, FF), down, vecs, partial_value),
        dp,
        narrow,
    )
    if direct:
        return collect_step(grads[0], group_out, grad_inputs, dp, narrow)
    transport_loss = lax.all_gather(partial_value[:, 0], "narrow", axis=0, tiled=True)
    squares, g_up, g_down, small, tiles = grads
    mats, vecs = reduce_grads([*squares.reshape(4, D, D), g_up, g_down.T], [*small[:8, :D], tiles[:24].reshape(FF)])
    return (
        group_out,
        transport_loss,
        grad_inputs,
        mats[0],
        vecs[0],
        mats[1],
        mats[2],
        vecs[1],
        mats[3],
        vecs[2],
        vecs[3],
        vecs[4],
        mats[4],
        vecs[8],
        mats[5],
        vecs[5],
        vecs[6],
        vecs[7],
    )


def solution(mesh):
    return jax.shard_map(
        per_device,
        mesh=mesh,
        in_specs=(
            P(("dp", "narrow"), None),
            P("dp", None),
            P("dp", None),
            P("dp", "narrow"),
            P("dp"),
            P("dp", "narrow"),
            P("dp", "narrow"),
            P("dp"),
            P("dp", "narrow"),
            P("dp"),
            P("dp"),
            P("dp"),
            P("dp", "narrow"),
            P("dp"),
            P("dp", "narrow"),
            P("dp"),
            P("dp"),
            P("dp"),
            P(("dp", "narrow"), None),
            P("dp"),
        ),
        out_specs=(
            P("dp", None),
            P("dp"),
            P(("dp", "narrow"), None),
            P("dp", "narrow"),
            P("dp"),
            P("dp", "narrow"),
            P("dp", "narrow"),
            P("dp"),
            P("dp", "narrow"),
            P("dp"),
            P("dp"),
            P("dp"),
            P("dp", "narrow"),
            P("dp"),
            P("dp", "narrow"),
            P("dp"),
            P("dp"),
            P("dp"),
        ),
        check_vma=False,
    )
```

```python
import functools

import jax
import jax.numpy as jnp
from jax import lax
from jax.experimental import pallas as pl
from jax.experimental.pallas import tpu as pltpu
from jax.sharding import PartitionSpec as P

D = 768
HEADS = 12
HEAD_DIM = 64
LEN = 256
ITERS = 20
ROWS = 32
VMEM_LIMIT = 62 * 1024 * 1024

EPS_NORM = 1e-06
BETA = 0.5
MASKED = -1e30


def product(left, right):
    return jnp.dot(left, right, preferred_element_type=jnp.float32)


def product_left(left, right):
    return lax.dot_general(
        left, right, (((0,), (0,)), ((), ())), preferred_element_type=jnp.float32
    )


def product_right(left, right):
    return lax.dot_general(
        left, right, (((1,), (1,)), ((), ())), preferred_element_type=jnp.float32
    )


def fetch_weights(matrices, vectors):
    wide = [lax.all_gather(item, "narrow", axis=1, tiled=True) for item in matrices]
    query, keys, values, output, up, down = [lax.all_gather(item, "dp", axis=0, tiled=True) for item in wide]
    vecs = [lax.all_gather(item, "dp", axis=0, tiled=True).astype(jnp.float32) for item in vectors]
    up = up.reshape(GRID[0], BLOCK, GRID[1], 6, 128).transpose(0, 2, 3, 1, 4)
    up = up.reshape(GRID[0] // 2, 2, GRID[1] // 2, 2, 6 * BLOCK, 128)
    small = jnp.pad(jnp.stack(vecs[:8]), ((0, 8), (0, 128)))
    tiles = jnp.pad(vecs[8].reshape(24, 128), ((0, 8), (0, 0)))
    return (jnp.concatenate([query, keys, values, output], axis=1), up, down.T, small, tiles)


def reduce_grads(matrices, vectors):
    reduced = [lax.psum_scatter(item, "dp", scatter_dimension=0, tiled=True) for item in matrices]
    sums = [lax.psum_scatter(item, "dp", scatter_dimension=0, tiled=True) for item in vectors]
    return (
        [
            lax.psum_scatter(
                item.astype(jnp.bfloat16), "narrow", scatter_dimension=1, tiled=True
            ).astype(jnp.float32)
            for item in reduced
        ],
        lax.psum(sums, "narrow"),
    )


MESH = pl.DeviceIdType.MESH
FF = 4 * D
VEC, SQUARE, UP, DOWN, TOTAL = 0, 16, 592, 1168, 1744
PART = 144
CHUNK_ROWS = (80, 64) * 3 + (144,) * 9
CHUNKS = len(CHUNK_ROWS) + 1
SINGLES = (0, 1, 2, 3, 4, 5, CHUNKS - 1)
GRID = (8, 4)
BLOCK, SIDE = D // GRID[0], D // GRID[1]


def hops():
    dp, narrow = lax.axis_index("dp"), lax.axis_index("narrow")
    return (dp // 2, lax.rem(dp, 2), narrow // 2, lax.rem(narrow, 2))


def place(me, depth, item):
    s, a, b, c = item
    z, x, y, core = me
    z = z if s == 0 else lax.rem(z + s + depth, depth)
    x = 1 - x if a else x
    y = 1 - y if b else y
    core = 1 - core if c else core
    return (2 * z + x, 2 * y + core)


def greet(me, depth):
    peers = [place(me, depth, (s, 0, 0, 0)) for s in range(1, depth)]
    peers += [place(me, depth, (0, *bits)) for bits in ((1, 0, 0), (0, 1, 0), (0, 0, 1))]
    barrier = pltpu.get_barrier_semaphore()
    for peer in peers:
        pl.semaphore_signal(barrier, inc=1, device_id=peer, device_id_type=MESH)
    pl.semaphore_wait(barrier, len(peers))


def number(item):
    s, a, b, c = item
    return ((s * 2 + a) * 2 + b) * 2 + c


GATHER_AXES = (
    "zxy", "zyx", "zxy", "zyx", "zxy", "zyx", "zxy", "zyx", "zxy", "zyx", "zxy", "zyx", "zxy", "zyx", "zxy", "zxy",
)
FORWARD_ORDER = (
    0, 1, 15, 2, 3, 4, 5, 100, 6, 101, 115, 7, 200, 102, 201, 215, 8, 103, 300, 104, 202, 9, 400, 105, 301, 315, 203,
    401, 415, 500, 204, 106, 302, 10, 205, 11, 303, 402, 107, 403, 501, 304, 12, 404, 108, 206, 305, 405, 13, 502,
    109, 600, 207, 110, 601, 208, 602, 111, 603, 306, 112, 406, 700, 307, 209, 113, 210, 407, 800, 308, 408, 801, 14,
    802, 211, 212, 309, 409, 803, 114, 213, 311, 310, 411, 410, 804, 312, 214, 805, 412, 313, 413, 900, 314, 414,
    1000,
)


def split_order(order, kinds, marks):
    after, mark = {"": []}, ""
    for code in order:
        kind, index = divmod(code, 100)
        if kind < len(kinds):
            after[mark].append((kinds[kind], index))
        else:
            mark = marks[kind - len(kinds)] + str(index)
            after[mark] = []
    return after


def chunk_of(k, axes):
    if k == CHUNKS - 1:
        return (k, VEC, SQUARE - VEC, axes[k])
    return (k, SQUARE + sum(CHUNK_ROWS[:k]), CHUNK_ROWS[k], axes[k])


def arrivals(order, depth):
    have, stages = [(0, 0, 0)], []
    for axis in order:
        if axis == "z":
            new = [(far, a, b) for s, a, b in have for far in range(1, depth)]
        else:
            new = [(s, 1, b) if axis == "x" else (s, a, 1) for s, a, b in have]
        stages.append(new)
        have = have + new
    return stages


class Gather:
    def __init__(self, land, pad, send_sem, recv_sem):
        self.land, self.pad, self.send_sem, self.recv_sem = land, pad, send_sem, recv_sem
        self.me = hops()
        self.depth = land.shape[0]

    def block(self, chunk, z, x, y, core):
        return self.land.at[z, x, y, core, pl.ds(chunk[1], chunk[2]), :]

    def copy(self, chunk, block, hop, mark):
        return pltpu.make_async_remote_copy(
            src_ref=block,
            dst_ref=block,
            send_sem=self.send_sem.at[chunk[0]],
            recv_sem=self.recv_sem.at[chunk[0], mark],
            device_id=place(self.me, self.depth, hop),
            device_id_type=MESH,
        )

    def wait(self, chunk, block, mark):
        self.copy(chunk, block, (0, 0, 0, 1), mark).wait_recv()

    def single(self, chunk, item):
        s, a, b = item
        z, x, y, core = self.me
        source = lax.rem(z - s + self.depth, self.depth) if s else z
        return self.block(chunk, source, 1 - x if a else x, 1 - y if b else y, core)

    def send(self, chunk, item, axes):
        s, a, b = item
        block = self.single(chunk, item)
        for axis in axes:
            if axis == "z":
                for far in range(1, self.depth):
                    self.copy(chunk, block, (far, 0, 0, 0), number((far, a, b, 0))).start()
            elif axis == "x":
                self.copy(chunk, block, (0, 1, 0, 0), number((s, 1, b, 0))).start()
            elif axis == "y":
                self.copy(chunk, block, (0, 0, 1, 0), number((s, a, 1, 0))).start()
            else:
                self.copy(chunk, block, (0, 0, 0, 1), 1).start()

    def do(self, kind, k):
        chunk = chunk_of(k, GATHER_AXES)
        order = chunk[3]
        every = slice(None)
        z, x, y, core = self.me
        hop = {"x": (0, 1, 0, 0), "y": (0, 0, 1, 0), "c": (0, 0, 0, 1)}
        if kind == "c":
            self.wait(chunk, self.block(chunk, every, every, every, 1 - core), 1)
        elif k in SINGLES:
            if kind == "s":
                self.send(chunk, (0, 0, 0), order + "c")
            else:
                for item in arrivals(order, self.depth)[int(kind) - 1]:
                    self.wait(chunk, self.single(chunk, item), number((*item, 0)))
                    self.send(chunk, item, order[int(kind) :] + "c")
        elif order[0] == "z":
            column = self.block(chunk, every, x, y, core)
            if order[1] == "x":
                beside, behind = self.block(chunk, every, 1 - x, y, core), self.block(chunk, every, every, 1 - y, core)
            else:
                beside, behind = self.block(chunk, every, x, 1 - y, core), self.block(chunk, every, 1 - x, every, core)
            if kind == "s":
                for far in range(1, self.depth):
                    self.copy(chunk, self.single(chunk, (0, 0, 0)), (far, 0, 0, 0), 2 + far).start()
            elif kind == "1":
                for far in range(1, self.depth):
                    self.wait(chunk, self.single(chunk, (far, 0, 0)), 2 + far)
                for axis, mark in ((order[1], 6), (order[2], 7), ("c", 1)):
                    self.copy(chunk, column, hop[axis], mark).start()
            elif kind == "2":
                self.wait(chunk, beside, 6)
                for axis, mark in ((order[2], 7), ("c", 1)):
                    self.copy(chunk, beside, hop[axis], mark).start()
            else:
                self.wait(chunk, behind, 7)
                self.copy(chunk, behind, hop["c"], 1).start()
        else:
            own = self.single(chunk, (0, 0, 0))
            beside = self.single(chunk, (0, 1, 0) if order[0] == "x" else (0, 0, 1))
            behind = self.block(chunk, z, every, 1 - y, core) if order[0] == "x" else self.block(chunk, z, 1 - x, every, core)
            if kind == "s":
                for axis, mark in ((order[0], 6), (order[1], 7), ("c", 1)):
                    self.copy(chunk, own, hop[axis], mark).start()
            elif kind == "1":
                self.wait(chunk, beside, 6)
                for axis, mark in ((order[1], 7), ("c", 1)):
                    self.copy(chunk, beside, hop[axis], mark).start()
            elif kind == "2":
                self.wait(chunk, behind, 7)
                for far in range(1, self.depth):
                    self.copy(chunk, self.block(chunk, z, every, every, core), (far, 0, 0, 0), 2 + far).start()
                self.copy(chunk, behind, hop["c"], 1).start()
            else:
                for far in range(1, self.depth):
                    layer = self.block(chunk, lax.rem(z - far + self.depth, self.depth), every, every, core)
                    self.wait(chunk, layer, 2 + far)
                    self.copy(chunk, layer, hop["c"], 1).start()

    def drain(self, k):
        chunk = chunk_of(k, GATHER_AXES)
        size = self.pad.at[pl.ds(0, 16 * (8 * self.depth - 1)), pl.ds(0, 128 * chunk[2] // 16)]
        pltpu.make_async_remote_copy(
            src_ref=size,
            dst_ref=size,
            send_sem=self.send_sem.at[k],
            recv_sem=self.recv_sem.at[k, 0],
            device_id=place(self.me, self.depth, (0, 0, 0, 1)),
            device_id_type=MESH,
        ).wait_send()


def swap(half):
    return pltpu.roll(half, 64, 1)


def left_half(shape):
    return lax.broadcasted_iota(jnp.int32, shape, 1) < 64


def pack_block(wide, odd):
    rows = wide.shape[0]
    turned = pltpu.roll(wide, 192, 1)
    main = jnp.where(odd, turned[:, :128], wide[:, :128])
    rest = jnp.where(left_half((rows, 128)), jnp.where(odd, wide[:, :128], wide[:, 128:]), 0.0)
    top, low = rest[: rows // 2], rest[rows // 2 :]
    return main, jnp.where(odd, swap(top) + low, top + swap(low))


def middle_of(even, odd):
    left = left_half(even.shape)
    return jnp.where(left, even, odd), swap(jnp.where(left, odd, even))


def put_main(land, d, at, rows, ref, row, column):
    for pair in range(GRID[1] // 2):
        even, other = land.at[d // 2, d % 2, pair, 0], land.at[d // 2, d % 2, pair, 1]
        left = column + 384 * pair
        ref[pl.ds(row, rows), left : left + 128] = even[at : at + rows, :]
        ref[pl.ds(row, rows), left + 256 : left + 384] = other[at : at + rows, :]


def put_rest(land, d, at, rows, ref, row, column):
    half = rows // 2
    span = slice(at + rows, at + rows + half)
    for pair in range(GRID[1] // 2):
        even, other = land.at[d // 2, d % 2, pair, 0], land.at[d // 2, d % 2, pair, 1]
        top, low = middle_of(even[span, :].astype(jnp.float32), other[span, :].astype(jnp.float32))
        left = column + 384 * pair + 128
        ref[pl.ds(row, half), left : left + 128] = top.astype(jnp.bfloat16)
        ref[pl.ds(row + half, half), left : left + 128] = low.astype(jnp.bfloat16)


def norm_parts(values):
    centre = values - jnp.mean(values, axis=1, keepdims=True)
    spread = jnp.mean(centre * centre, axis=1, keepdims=True)
    recip = lax.rsqrt(spread + EPS_NORM)
    return centre * recip, recip


def gelu_parts(z):
    base = 1.0 + 0.2316419 * jnp.abs(z)
    t = pl.reciprocal(base, approx=True)
    t = t * (2.0 - base * t)
    density = jnp.exp2(z * z * (-0.5 * 1.4426950408889634))
    scale = 0.3989422804014327
    poly = 1.781477937 * scale + t * (-1.821255978 * scale + t * (1.330274429 * scale))
    tail = density * (t * (0.319381530 * scale + t * (-0.356563782 * scale + t * poly)))
    cdf = jnp.where(z < 0.0, tail, 1.0 - tail)
    return z * cdf, cdf + z * density * scale


def forward_kernel(direct, *refs):
    if direct:
        q_ref, k_ref, v_ref, o_ref, upw_ref, downw_ref = refs[:6]
        small_refs = refs[6:15]
        refs = refs[15:]
    else:
        square_in, up_in, down_in, vec_in, bup_in = refs[:5]
        refs = refs[5:]
    in_ref, seg_ref = refs[:2]
    (square_out, up_out, down_out, vec_ref, qkv_out, prob_out, turned_out, norm1_out, recip1_out,
     act_out, slope_out, mixed_out, norm2_out, recip2_out) = refs[2:16]
    (land, square, down, bup, qkv, qkv_turned, prob, turned, ctx, first, flow, norm, recip, act, slope, mixed,
     out_sem, pack_sem, tile_sem) = refs[16:35]
    packs = in_ref.shape[0] // LEN
    base = lax.axis_index("narrow") * packs
    pending = {}

    def save(name, src, dst):
        pending[name] = pltpu.make_async_copy(src, dst, out_sem.at[len(pending)])
        pending[name].start()

    if direct:
        send_sem, recv_sem = refs[35:37]
        dp, narrow = lax.axis_index("dp"), lax.axis_index("narrow")
        odd = lax.rem(narrow, 2) == 1
        own = land.at[dp // 2, lax.rem(dp, 2), narrow // 2, lax.rem(narrow, 2)]
        row = lambda ref: jnp.concatenate(
            [ref[...].astype(jnp.float32), jnp.zeros((1, 128 - BLOCK), jnp.float32)], axis=1
        )
        small = [row(ref) for ref in small_refs[:8]] + [small_refs[8][...].astype(jnp.float32)]
        own[0:16, :] = jnp.concatenate([*small, jnp.zeros((5, 128), jnp.float32)]).astype(jnp.bfloat16)
        for i, ref in enumerate((q_ref, k_ref, v_ref, o_ref)):
            main, rest = pack_block(
                jnp.concatenate([ref[...].astype(jnp.float32), jnp.zeros((BLOCK, 64), jnp.float32)], axis=1), odd
            )
            at = SQUARE + PART * i
            own[at : at + BLOCK, :] = main.astype(jnp.bfloat16)
            own[at + BLOCK : at + PART, :] = rest.astype(jnp.bfloat16)
        g = Gather(land, act, send_sem, recv_sem)
        greet(g.me, g.depth)
        after = split_order(FORWARD_ORDER, "s123c", "QAOWGF")
        early = [piece for piece in after[""] if piece[1] < 7 or piece[1] == CHUNKS - 1]
        early = early[: next(i for i, piece in enumerate(early) if piece[0] != "s")]
        for piece in early:
            g.do(*piece)
        for t in range(6):
            own[UP + BLOCK * t : UP + BLOCK * (t + 1), :] = upw_ref[:, 128 * t : 128 * (t + 1)]
        for t in range(3):
            own[DOWN + SIDE * t : DOWN + SIDE * (t + 1), :] = downw_ref[:, 128 * t : 128 * (t + 1)]
        for piece in after[""]:
            if piece not in early:
                g.do(*piece)
        vec_ref[...] = jnp.zeros_like(vec_ref)
        for d in range(GRID[0]):
            tile = land[d // 2, d % 2, 0, 0, 0:16, :].astype(jnp.float32)
            wide = jnp.concatenate([tile, jnp.zeros((16, 128), jnp.float32)], axis=1)
            at, shift = divmod(BLOCK * d, 128)
            wide = pltpu.roll(wide, shift, 1) if shift else wide
            vec_ref[:, 128 * at : 128 * at + 256] += wide
            bup[3 * d : 3 * d + 3, :] = tile[8:11]

        def unpack(i):
            for d in range(GRID[0]):
                put_main(land, d, SQUARE + PART * i, BLOCK, square, BLOCK * d, D * i)
                put_rest(land, d, SQUARE + PART * i, BLOCK, square, BLOCK * d, D * i)

        def pieces_after(mark):
            for piece in after[mark]:
                g.do(*piece)

        def tick(mark, index):
            for name, pieces in after.items():
                if name[:1] == mark and pieces:

                    @pl.when(index == int(name[1:]))
                    def _():
                        for piece in pieces:
                            g.do(*piece)
    else:
        fills = [
            pltpu.make_async_copy(src, dst, out_sem.at[i])
            for i, (src, dst) in enumerate(
                ((square_in, square), (down_in, down), (up_in, land.at[:, :, :, :, pl.ds(UP, DOWN - UP), :]))
            )
        ]
        for copy in fills:
            copy.start()
        vec_ref[...] = vec_in[...]
        bup[...] = bup_in[...]
        for copy in fills:
            copy.wait()
        tick = lambda mark, index: None
        unpack = pieces_after = lambda mark: None

    for i in range(3):
        unpack(i)
        for j in range(3):
            columns = slice(256 * j, 256 * (j + 1))
            part = product(in_ref[...], square[:, D * i + 256 * j : D * i + 256 * (j + 1)])
            if i != 1:
                part = part + vec_ref[i // 2 : i // 2 + 1, columns]
            part = part.astype(jnp.bfloat16)
            qkv[:, D * i + 256 * j : D * i + 256 * (j + 1)] = part
            qkv_turned[D * i + 256 * j : D * i + 256 * (j + 1), :] = jnp.transpose(part)
        pieces_after(f"Q{i}")
    save("qkv", qkv_turned, qkv_out)

    def prob_copy(p):
        return pltpu.make_async_copy(prob.at[p % 2], prob_out.at[p], pack_sem.at[0, p % 2])

    def turned_copy(p):
        at = pl.ds(pl.multiple_of(p * LEN, LEN), LEN)
        return pltpu.make_async_copy(turned.at[p % 2], turned_out.at[:, :, at], pack_sem.at[1, p % 2])

    def attend(p, carry):
        rows = pl.ds(pl.multiple_of(p * LEN, LEN), LEN)
        k = p % 2

        pl.when(p >= 2)(lambda: prob_copy(p - 2).wait())
        seg_row = seg_ref[pl.ds(base + p, 1), :].astype(jnp.float32)
        seg_col = jnp.transpose(jnp.broadcast_to(seg_row, (128, LEN)))
        same = jnp.concatenate([seg_col, seg_col], axis=1) == seg_row
        left = left_half((LEN, 128))
        for h in range(HEADS // 2):
            columns = slice(128 * h, 128 * (h + 1))
            query = qkv[rows, columns] * jnp.asarray(HEAD_DIM**-0.5, jnp.bfloat16)
            keys = qkv[rows, D + 128 * h : D + 128 * (h + 1)]
            values = qkv[rows, 2 * D + 128 * h : 2 * D + 128 * (h + 1)]
            mixes = []
            for side in range(2):
                mine = left if side == 0 else jnp.logical_not(left)
                scores = product_right(jnp.where(mine, query, jnp.zeros_like(query)), keys)
                scores = jnp.where(same, scores, MASKED)
                shifted = jnp.exp(scores - jnp.max(scores, axis=1, keepdims=True))
                total = jnp.sum(shifted, axis=1, keepdims=True)
                low = (shifted * (1.0 / total)).astype(jnp.bfloat16)
                prob[k, 2 * h + side] = low
                mixes.append(product(low, values))
            ctx[rows, columns] = jnp.where(left, mixes[0], mixes[1]).astype(jnp.bfloat16)
        prob_copy(p).start()
        tick("A", p)
        return carry

    lax.fori_loop(0, packs, attend, 0)
    unpack(3)
    save("square", square, square_out)
    prob_copy(packs - 2).wait()
    prob_copy(packs - 1).wait()

    def project(p, carry):
        rows = pl.ds(pl.multiple_of(p * LEN, LEN), LEN)
        k = p % 2

        @pl.when(p >= 2)
        def _():
            turned_copy(p - 2).wait()

        x = in_ref[rows, :]
        context = ctx[rows, :]
        total = x.astype(jnp.float32) + (product(context, square[:, 3 * D :]) + vec_ref[2:3, :D])
        normed, scale = norm_parts(total)
        value = normed * vec_ref[3:4, :D] + vec_ref[4:5, :D]
        first[rows, :] = value
        low = value.astype(jnp.bfloat16)
        flow[rows, :] = low
        norm[rows, :] = normed
        recip[rows, :] = jnp.broadcast_to(scale, (LEN, 128))
        turned[k, 0] = jnp.transpose(x)
        turned[k, 1] = jnp.transpose(context)
        turned[k, 2] = jnp.transpose(low)
        turned_copy(p).start()
        return carry

    lax.fori_loop(0, packs, project, 0)
    pieces_after("O0")
    save("norm", norm, norm1_out)
    save("recip", recip, recip1_out)
    turned_copy(packs - 2).wait()
    turned_copy(packs - 1).wait()

    def tile_copies(t):
        k = t % 2
        copies = []
        for n in range(GRID[1]):
            columns = pl.ds(pl.multiple_of(D * n + 128 * t, 128), 128)
            first_row = pl.multiple_of(UP + BLOCK * t, 16)
            copies += [
                pltpu.make_async_copy(slope.at[k, n], slope_out.at[:, columns], tile_sem.at[0, k, n]),
                pltpu.make_async_copy(act.at[:, columns], act_out.at[:, columns], tile_sem.at[1, k, n]),
                pltpu.make_async_copy(
                    land.at[:, :, n // 2, n % 2, pl.ds(first_row, BLOCK), :], up_out.at[:, :, :, columns], tile_sem.at[2, k, n]
                ),
            ]
        return copies

    def widen(t, carry):
        k = t % 2

        @pl.when(t >= 2)
        def _():
            for copy in tile_copies(t - 2):
                copy.wait()

        first_row = pl.multiple_of(UP + BLOCK * t, 16)
        for pair in range(2):
            weight = jnp.concatenate(
                [land[:, :, pair, i, pl.ds(first_row, BLOCK), :].reshape(D, 128) for i in range(2)], axis=1
            )
            bias = jnp.concatenate([bup[pl.ds(6 * (2 * pair + i) + t, 1), :] for i in range(2)], axis=1)
            for r in range(packs):
                rows = slice(LEN * r, LEN * (r + 1))
                value, turn = gelu_parts(product(flow[rows, :], weight) + bias)
                value, turn = value.astype(jnp.bfloat16), turn.astype(jnp.bfloat16)
                for i in range(2):
                    n = 2 * pair + i
                    columns = pl.ds(pl.multiple_of(D * n + 128 * t, 128), 128)
                    act[rows, columns] = value[:, 128 * i : 128 * (i + 1)]
                    slope[k, n, rows, :] = turn[:, 128 * i : 128 * (i + 1)]
        for copy in tile_copies(t):
            copy.start()
        tick("W", t)
        return carry

    lax.fori_loop(0, 6, widen, 0)
    def down_part(*tiles):
        if direct:
            for d in range(GRID[0]):
                for n in range(GRID[1]):
                    for t in tiles:
                        at = 384 * d + 128 * t
                        down[SIDE * n : SIDE * (n + 1), at : at + 128] = land[
                            d // 2, d % 2, n // 2, n % 2, DOWN + SIDE * t : DOWN + SIDE * (t + 1), :
                        ]
        spans = [slice(384 * d + 128 * t, 384 * d + 128 * (t + 1)) for d in range(GRID[0]) for t in tiles]
        for j in range(3):
            columns = slice(256 * j, 256 * (j + 1))
            weight = jnp.concatenate([down[columns, span] for span in spans], axis=1)
            for r in range(packs):
                rows = slice(LEN * r, LEN * (r + 1))
                hidden = jnp.concatenate([act[rows, span] for span in spans], axis=1)
                first[rows, columns] = first[rows, columns] + product_right(hidden, weight)

    down_part(0, 1)
    pieces_after("G0")
    down_part(2)
    save("down", down, down_out)
    pending["norm"].wait()
    pending["recip"].wait()

    def finish(p, carry):
        rows = pl.ds(pl.multiple_of(p * LEN, LEN), LEN)
        normed, scale = norm_parts(first[rows, :] + vec_ref[5:6, :D])
        norm[rows, :] = normed
        recip[rows, :] = jnp.broadcast_to(scale, (LEN, 128))
        mixed[rows, :] = (normed * vec_ref[6:7, :D] + vec_ref[7:8, :D]).astype(jnp.bfloat16)
        return carry

    lax.fori_loop(0, packs, finish, 0)
    save("mixed", mixed, mixed_out)
    save("norm2", norm, norm2_out)
    save("recip2", recip, recip2_out)
    for t in (4, 5):
        for copy in tile_copies(t):
            copy.wait()
    if direct:
        for k in range(CHUNKS):
            g.drain(k)
    for name, copy in pending.items():
        if name not in ("norm", "recip"):
            copy.wait()


def forward_step(direct, weights, inputs, segments, dp, narrow):
    rows = inputs.shape[0]
    packs = rows // LEN
    vmem = pl.BlockSpec(memory_space=pltpu.VMEM)
    anywhere = pl.BlockSpec(memory_space=pl.ANY)
    low = lambda *shape: jax.ShapeDtypeStruct(shape, jnp.bfloat16)
    full = lambda *shape: jax.ShapeDtypeStruct(shape, jnp.float32)
    room = lambda *shape: pltpu.VMEM(shape, jnp.bfloat16)
    wide = lambda *shape: pltpu.VMEM(shape, jnp.float32)
    sems = [pltpu.SemaphoreType.DMA((CHUNKS,)), pltpu.SemaphoreType.DMA((CHUNKS, 32))] if direct else []
    return pl.pallas_call(
        functools.partial(forward_kernel, direct),
        name="forward",
        out_shape=(
            low(D, FF), low(GRID[0] // 2, 2, BLOCK, FF), low(D, FF), full(16, 896),
            low(3 * D, rows), low(packs, HEADS, LEN, LEN), low(3, D, rows), full(rows, D), full(rows, 128),
            low(rows, FF), low(rows, FF), low(rows, D), full(rows, D), full(rows, 128),
        ),
        in_specs=([vmem] * 15 if direct else [anywhere] * 3 + [vmem] * 2) + [vmem] * 2,
        out_specs=(anywhere,) * 3 + (vmem,) + (anywhere,) * 10,
        scratch_shapes=[
            room(GRID[0] // 2, 2, GRID[1] // 2, 2, TOTAL, 128), room(D, FF), room(D, FF), wide(32, 128),
            room(rows, 3 * D), room(3 * D, rows), room(2, HEADS, LEN, LEN), room(2, 3, D, LEN), room(rows, D), wide(rows, D), room(rows, D),
            wide(rows, D), wide(rows, 128), room(rows, FF), room(2, 4, rows, 128), room(rows, D),
            pltpu.SemaphoreType.DMA((12,)), pltpu.SemaphoreType.DMA((2, 2)), pltpu.SemaphoreType.DMA((3, 2, 4)),
            *sems,
        ],
        compiler_params=pltpu.CompilerParams(
            vmem_limit_bytes=VMEM_LIMIT, **(dict(collective_id=0, has_side_effects=True) if direct else {})
        ),
    )(*weights, inputs, segments)


def transport_kernel(
    mixed_ref, seg_ref, kind_ref, weight_ref, cot_in, normed_in, recip_in, gain_ref,
    value_ref, second_out, branch_out, turned_out, sums_ref,
    kern_ref, prod_ref, flow_ref, acc_ref, left_ref, sigma_ref,
    cot_ref, normed_ref, recip_ref, second_ref, branch_ref, turned_ref, load_sem, save_sem,
):
    loads = [
        pltpu.make_async_copy(src, dst, load_sem.at[i])
        for i, (src, dst) in enumerate(((cot_in, cot_ref), (normed_in, normed_ref), (recip_in, recip_ref)))
    ]
    for copy in loads:
        copy.start()
    packs = mixed_ref.shape[0] // LEN
    base = lax.axis_index("narrow") * packs
    blocks = LEN // ROWS
    lanes = lambda col: jnp.concatenate([col, col], axis=1)
    fold = lambda wide: wide[:, :128] + wide[:, 128:]
    eight = lambda wide: jnp.sum(wide.reshape(ROWS // 8, 8, LEN), axis=0)
    replicate = lambda col: jnp.broadcast_to(col, (ROWS, 128))

    def turned(row):
        return jnp.transpose(jnp.broadcast_to(row, (128, LEN)))

    for p in range(packs):
        rows = pl.ds(p * LEN, LEN)
        feats = mixed_ref[rows, :].astype(jnp.float32)
        recip = lax.rsqrt(jnp.sum(feats * feats, axis=1, keepdims=True) + EPS_NORM)
        unit = (feats * recip).astype(jnp.bfloat16)
        cosine = product_right(unit, unit)
        seg_row = seg_ref[pl.ds(base + p, 1), :].astype(jnp.float32)
        region_row = jnp.where(kind_ref[pl.ds(base + p, 1), :] == 0, 0.0, 1.0)
        seg_col = turned(seg_row)
        word_col = 1.0 - turned(region_row)
        same = jnp.where(lanes(seg_col) == seg_row, 1.0, 0.0)
        word_count = jnp.sum(same * (1.0 - region_row), axis=1, keepdims=True)
        region_count = jnp.sum(same * lanes(1.0 - word_col), axis=0, keepdims=True)
        kern_ref[p] = jnp.exp((cosine - 1.0) * (1.0 / BETA)) * same * lanes(word_col) * region_row
        left_ref[p, 0] = word_col
        left_ref[p, 1] = jnp.broadcast_to(word_count, (LEN, 128))
        left_ref[p, 2] = 1.0 - word_col
        prod_ref[0, p] = jnp.ones((LEN, LEN), jnp.float32)
        sigma_ref[0, p, 0:1] = region_row / region_count
        sigma_ref[0, p, 1:2] = region_row
        sigma_ref[0, p, 2:3] = region_count

    def advance(t, carry):
        for p in range(packs):
            sigma = sigma_ref[t, p, 0:1]
            scale = jnp.where(t == 0, 1.0, sigma)
            region = sigma_ref[0, p, 1:2]
            count = sigma_ref[0, p, 2:3]
            total = jnp.zeros((8, LEN), jnp.float32)
            for b in range(blocks):
                rows = pl.ds(b * ROWS, ROWS)
                weighted = kern_ref[p, rows, :] * (prod_ref[t, p, rows, :] * scale)
                row_sum = jnp.sum(fold(weighted * sigma), axis=1, keepdims=True)
                word = left_ref[p, 0, rows, :]
                base = left_ref[p, 1, rows, :] * replicate(row_sum) + left_ref[p, 2, rows, :]
                delta = pl.reciprocal(base, approx=True)
                delta = word * delta * (2.0 - base * delta)
                scaled = weighted * lanes(delta)
                prod_ref[t + 1, p, rows, :] = scaled
                total = total + eight(scaled)
            col_sum = jnp.sum(total, axis=0, keepdims=True)
            sigma_ref[t + 1, p, 0:1] = region / (count * col_sum + 1.0 - region)
        return carry

    lax.fori_loop(0, ITERS, advance, 0, unroll=2)

    starts = []
    for p in range(packs):
        rows = pl.ds(p * LEN, LEN)
        weight = weight_ref[base + p]
        feats = mixed_ref[rows, :].astype(jnp.float32)
        recip = lax.rsqrt(jnp.sum(feats * feats, axis=1, keepdims=True) + EPS_NORM)
        unit = (feats * recip).astype(jnp.bfloat16)
        cosine = product_right(unit, unit)
        moved = (prod_ref[ITERS, p] * sigma_ref[ITERS, p, 0:1]) * (1.0 - cosine)
        value_ref[p : p + 1, :] = jnp.broadcast_to(jnp.sum(moved), (1, 128))
        moved = moved * weight
        flow_ref[p] = moved
        acc_ref[p] = jnp.zeros((LEN, LEN), jnp.float32)
        starts += [jnp.sum(moved, axis=0, keepdims=True), jnp.zeros((1, LEN), jnp.float32)]

    def retreat(step, carry):
        t = ITERS - 1 - step
        out = []
        for p in range(packs):
            flow_sum, spread = carry[2 * p : 2 * p + 2]
            before = sigma_ref[t, p, 0:1]
            d_col = -sigma_ref[0, p, 2:3] * sigma_ref[t + 1, p, 0:1] * (spread + flow_sum)
            total = jnp.zeros((8, LEN), jnp.float32)
            shift = jnp.zeros((8, LEN), jnp.float32)
            for b in range(blocks):
                rows = pl.ds(b * ROWS, ROWS)
                scaled = prod_ref[t + 1, p, rows, :]
                flow = flow_ref[p, rows, :] + scaled * d_col
                d_row = replicate(jnp.sum(fold(flow), axis=1, keepdims=True))
                d_row = -left_ref[p, 1, rows, :] * d_row
                moved = scaled * lanes(d_row)
                flow = flow + moved * before
                flow_ref[p, rows, :] = flow
                acc_ref[p, rows, :] = acc_ref[p, rows, :] + flow
                total = total + eight(flow)
                shift = shift + eight(moved)
            out += [
                jnp.sum(total, axis=0, keepdims=True),
                before * jnp.sum(shift, axis=0, keepdims=True),
            ]
        return tuple(out)

    lax.fori_loop(0, ITERS, retreat, tuple(starts), unroll=2)

    for copy in loads:
        copy.wait()
    saves = []
    sums = [jnp.zeros((1, D), jnp.float32)] * 3
    for p in range(packs):
        rows = pl.ds(p * LEN, LEN)
        coupling = prod_ref[ITERS, p] * sigma_ref[ITERS, p, 0:1]
        d_cost = weight_ref[base + p] * coupling - acc_ref[p] * (1.0 / BETA)
        d_cosine = (-d_cost).astype(jnp.bfloat16)
        feats = mixed_ref[rows, :].astype(jnp.float32)
        recip = lax.rsqrt(jnp.sum(feats * feats, axis=1, keepdims=True) + EPS_NORM)
        unit = feats * recip
        unit_low = unit.astype(jnp.bfloat16)
        d_unit = product(d_cosine, unit_low) + product_left(d_cosine, unit_low)
        d_mixed = cot_ref[rows, :].astype(jnp.float32) + recip * (
            d_unit - unit * jnp.sum(d_unit * unit, axis=1, keepdims=True)
        )
        normed = normed_ref[rows, :]
        scaled = d_mixed * gain_ref[6:7, :D]
        inner_mean = jnp.mean(scaled, axis=1, keepdims=True)
        cross_mean = jnp.mean(scaled * normed, axis=1, keepdims=True)
        d_second = recip_ref[rows, 0:1] * (scaled - inner_mean - normed * cross_mean)
        d_branch = d_second.astype(jnp.bfloat16)
        second_ref[rows, :] = d_second
        branch_ref[rows, :] = d_branch
        turned_ref[:, rows] = jnp.transpose(d_branch)
        for src, dst in (
            (second_ref.at[rows, :], second_out.at[rows, :]),
            (branch_ref.at[rows, :], branch_out.at[rows, :]),
            (turned_ref.at[:, rows], turned_out.at[:, rows]),
        ):
            copy = pltpu.make_async_copy(src, dst, save_sem.at[len(saves)])
            copy.start()
            saves.append(copy)
        sums[0] = sums[0] + jnp.sum(d_mixed * normed, axis=0, keepdims=True)
        sums[1] = sums[1] + jnp.sum(d_mixed, axis=0, keepdims=True)
        sums[2] = sums[2] + jnp.sum(d_branch.astype(jnp.float32), axis=0, keepdims=True)
    for k in range(3):
        sums_ref[k : k + 1, :] = sums[k]
    for copy in saves:
        copy.wait()


def transport_step(mixed, segments, row_kind, weight, cotangent, normed, recip, gain):
    rows = mixed.shape[0]
    packs = rows // LEN
    vmem = pl.BlockSpec(memory_space=pltpu.VMEM)
    anywhere = pl.BlockSpec(memory_space=pl.ANY)
    square = (packs, LEN, LEN)
    return pl.pallas_call(
        transport_kernel,
        name="transport",
        out_shape=(
            jax.ShapeDtypeStruct((packs, 128), jnp.float32),
            jax.ShapeDtypeStruct((rows, D), jnp.float32),
            jax.ShapeDtypeStruct((rows, D), jnp.bfloat16),
            jax.ShapeDtypeStruct((D, rows), jnp.bfloat16),
            jax.ShapeDtypeStruct((8, D), jnp.float32),
        ),
        in_specs=[vmem, vmem, vmem, pl.BlockSpec(memory_space=pltpu.SMEM), anywhere, anywhere, anywhere, vmem],
        out_specs=(vmem, anywhere, anywhere, anywhere, vmem),
        scratch_shapes=[
            pltpu.VMEM(square, jnp.float32),
            pltpu.VMEM((ITERS + 1, *square), jnp.float32),
            pltpu.VMEM(square, jnp.float32),
            pltpu.VMEM(square, jnp.float32),
            pltpu.VMEM((packs, 3, LEN, 128), jnp.float32),
            pltpu.VMEM((ITERS + 1, packs, 8, LEN), jnp.float32),
            pltpu.VMEM((rows, D), jnp.bfloat16),
            pltpu.VMEM((rows, D), jnp.float32),
            pltpu.VMEM((rows, 128), jnp.float32),
            pltpu.VMEM((rows, D), jnp.float32),
            pltpu.VMEM((rows, D), jnp.bfloat16),
            pltpu.VMEM((D, rows), jnp.bfloat16),
            pltpu.SemaphoreType.DMA((3,)),
            pltpu.SemaphoreType.DMA((3 * packs,)),
        ],
        compiler_params=pltpu.CompilerParams(vmem_limit_bytes=VMEM_LIMIT),
    )(mixed, segments, row_kind, weight, cotangent, normed, recip, gain)


REST, OUT, MAIN = 16, 160, 304
SCATTER_ROWS = (80, 80, 80, 64, 80, 64, 80, 64) + (144,) * 4 + (96,) * 6
SCATTER_AXES = (
    "zyx", "yxz", "xyz", "xyz", "yxz", "xyz", "xyz", "xyz", "zxy", "xyz", "yxz", "xyz", "xyz", "yxz", "yxz", "zyx",
    "xyz", "yxz",
)
BACKWARD_ORDER = (
    500, 12, 13, 501, 14, 15, 502, 16, 17, 112, 113, 600, 114, 601, 115, 116, 602, 117, 603, 700, 701, 8, 702, 9, 212,
    213, 703, 704, 10, 108, 109, 705, 11, 216, 214, 800, 110, 313, 111, 801, 215, 802, 217, 803, 312, 900, 2, 3, 209,
    316, 1000, 102, 314, 1001, 103, 1002, 1003, 208, 210, 315, 1004, 211, 413, 1005, 309, 317, 1006, 412, 1007, 202,
    416, 1100, 4, 5, 6, 7, 311, 414, 1200, 104, 203, 1201, 105, 106, 107, 302, 308, 409, 1202, 310, 417, 1203, 415,
    1300, 0, 1, 204, 205, 303, 402, 411, 1400, 100, 101, 408, 1401, 206, 410, 1402, 305, 403, 207, 1403, 304, 201,
    306, 307, 200, 301, 405, 404, 300, 406, 407, 400, 401,
)


class Scatter:
    def __init__(self, part, lands, send_sem, recv_sem, total):
        self.part, self.lands, self.send_sem, self.recv_sem, self.total = part, lands, send_sem, recv_sem, total
        self.me = hops()
        self.depth = part.shape[0]

    def copies(self, k):
        first, order = sum(SCATTER_ROWS[:k]), SCATTER_AXES[k]
        span = pl.ds(first, SCATTER_ROWS[k])
        every = slice(None)
        z, x, y, core = self.me
        part = lambda *at: self.part.at[*at, span, :]
        land_c, land_q, land_p, land_z = self.lands
        land = lambda ref, *at: ref.at[*at, span, :]
        to_x, to_y = (0, 1, 0, 0), (0, 0, 1, 0)
        stages = {"c": [], "3": [], "2": [], "1": []}
        ahead = lambda far: lax.rem(z + far, self.depth)
        if order[0] == "y":
            stages["c"] = [
                (part(every, every, 1 - y, 1 - core), land(land_c, every, every, 1 - y), None, part(every, every, 1 - y, core)),
                (part(every, every, y, 1 - core), land(land_c, every, every, y), None, part(every, every, y, core)),
            ]
        elif order[0] == "x":
            stages["c"] = [
                (part(every, 1 - x, every, 1 - core), land(land_c, every, 1 - x, every), None, part(every, 1 - x, every, core)),
                (part(every, x, every, 1 - core), land(land_c, every, x, every), None, part(every, x, every, core)),
            ]
        else:
            stages["c"] = [(part(every, every, every, 1 - core), land(land_c, every, every, every), None, part(every, every, every, core))]
        if order == "yxz":
            stages["3"] = [(part(every, every, 1 - y, core), land(land_q, every, every), to_y, part(every, every, y, core))]
            stages["2"] = [(part(every, 1 - x, y, core), land(land_p, every), to_x, part(every, x, y, core))]
        elif order == "xyz":
            stages["3"] = [(part(every, 1 - x, every, core), land(land_q, every, every), to_x, part(every, x, every, core))]
            stages["2"] = [(part(every, x, 1 - y, core), land(land_p, every), to_y, part(every, x, y, core))]
        else:
            for far in range(1, self.depth):
                for i in range(2):
                    slot = 2 * (far - 1) + i
                    where = land(land_q, slot, every) if slot < 4 else land(land_p, slice(2 * slot - 8, 2 * slot - 6))
                    stages["3"].append((part(ahead(far), i, every, core), where, (far, 0, 0, 0), part(z, i, every, core)))
            pair, last = land(land_z, slice(0, 2)), land(land_z, 2)
            if order[1] == "y":
                stages["2"] = [(part(z, every, 1 - y, core), pair, to_y, part(z, every, y, core))]
                stages["1"] = [(part(z, 1 - x, y, core), last, to_x, part(z, x, y, core))]
            else:
                stages["2"] = [(part(z, 1 - x, every, core), pair, to_x, part(z, x, every, core))]
                stages["1"] = [(part(z, x, 1 - y, core), last, to_y, part(z, x, y, core))]
        if order[2] == "z":
            stages["1"] = [
                (part(ahead(far), x, y, core), land(land_z, far - 1), (far, 0, 0, 0), part(z, x, y, core))
                for far in range(1, self.depth)
            ]
        made, mark = {}, 0
        for stage, items in stages.items():
            made[stage] = []
            for src, dst, hop, into in items:
                if stage != "c":
                    copy = functools.partial(self.copy, k, mark, src, dst, hop)
                    made[stage].append((copy, dst, into))
                    mark += 1
                else:
                    made[stage].append((None, dst, into))
        whole = functools.partial(
            self.copy, k, mark, part(every, every, every, 1 - core), land(land_c, every, every, every), (0, 0, 0, 1)
        )
        return whole, made

    def copy(self, k, mark, src, dst, hop):
        return pltpu.make_async_remote_copy(
            src_ref=src,
            dst_ref=dst,
            send_sem=self.send_sem.at[k, mark],
            recv_sem=self.recv_sem.at[k, mark],
            device_id=place(self.me, self.depth, hop),
            device_id_type=MESH,
        )

    def do(self, kind, k):
        whole, made = self.copies(k)
        if kind == "s":
            whole().start()
            return
        if kind == "c":
            whole().wait_recv()
        following = {"c": "3", "3": "2", "2": "1"}.get(kind)
        first, rows = sum(SCATTER_ROWS[:k]), SCATTER_ROWS[k]
        for i, (copy, land, into) in enumerate(made[kind]):
            if kind != "c":
                copy().wait_recv()
            if kind != "1":
                into[...] = into[...] + land[...]
            if kind == "c" and i == 0 and len(made["c"]) == 2:
                made["3"][0][0]().start()
        if kind == "1":
            value = made["1"][0][2][...].astype(jnp.float32)
            for copy, land, into in made["1"]:
                value = value + land[...].astype(jnp.float32)
            self.total[pl.ds(first, rows), :] = value
        elif not (kind == "c" and len(made["c"]) == 2):
            for copy, land, into in made[following]:
                copy().start()

    def drain(self, k):
        whole, made = self.copies(k)
        whole().wait_send()
        for stage in "321":
            for copy, land, into in made[stage]:
                copy().wait_send()


def fold_middle(top, low):
    left = left_half(top.shape)
    return jnp.where(left, top, swap(low)), jnp.where(left, swap(low), top)


def take_main(part, d, pair, at, even, other):
    rows = even.shape[0]
    part[d // 2, d % 2, pair, 0, at : at + rows, :] = even.astype(jnp.bfloat16)
    part[d // 2, d % 2, pair, 1, at : at + rows, :] = other.astype(jnp.bfloat16)


def take_rest(part, d, pair, at, block):
    half = block.shape[0] // 2
    one, two = fold_middle(block[:half], block[half:])
    take_main(part, d, pair, at, one, two)


def unpack_block(main, rest, odd):
    other = swap(rest)
    top, low = jnp.where(odd, other, rest), jnp.where(odd, rest, other)
    piece = jnp.concatenate([top, low], axis=0)
    left = left_half(piece.shape)
    swapped = swap(main)
    first = jnp.where(odd, jnp.where(left, piece, swapped), main)
    second = jnp.where(odd, swapped, piece)
    return jnp.concatenate([first, second], axis=1)


def backward_kernel(direct, *refs):
    (act_in, slope_in, branch_in, branch_turned_in, second_in, sums_in, turned_in, norm_in, recip_in, qkv_in, prob_in,
     square_in, up_in, down_in, vec_ref, value_ref) = refs[:16]
    refs = refs[16:]
    if direct:
        grad_in_out, total = refs[:2]
        refs = refs[2:]
    else:
        grad_in_out, gsquare_ref, gup_ref, gdown_ref, gvec_ref, gbup_ref = refs[:6]
        refs = refs[6:]
    (turned, slope, square, up, flow, norm, recip, branch, branch_turned, prob, sums, bup, load_sem, prob_sem,
     out_sem) = refs[:15]
    rows_all = slope.shape[0]
    packs = rows_all // LEN
    if direct:
        part, land_c, land_q, land_p, land_z, send_sem, recv_sem = refs[15:22]
        g = Scatter(part, (land_c, land_q, land_p, land_z), send_sem, recv_sem, total)
        dp, narrow = lax.axis_index("dp"), lax.axis_index("narrow")
    else:
        (stage,) = refs[15:16]

    loads, waited = {}, set()

    def load(name, *pairs):
        loads[name] = []
        for src, dst in pairs:
            copy = pltpu.make_async_copy(src, dst, load_sem.at[sum(map(len, loads.values()))])
            copy.start()
            loads[name].append(copy)

    def need(*names):
        for name in names:
            if name not in waited:
                waited.add(name)
                for copy in loads[name]:
                    copy.wait()

    blocks = [pl.ds(rows_all * i, rows_all) for i in range(3)]
    load("turned branch", (branch_turned_in, branch_turned))
    load("act", *[(act_in.at[:, span], turned.at[span, :]) for span in blocks])
    if direct:
        greet(g.me, g.depth)
    sums[...] = jnp.zeros_like(sums)
    bup[...] = jnp.zeros_like(bup)
    sums[5:6, :D] = sums_in[2:3, :]
    sums[6:7, :D] = sums_in[0:1, :]
    sums[7:8, :D] = sums_in[1:2, :]

    def put(src, dst):
        copy = pltpu.make_async_copy(src, dst, out_sem.at[0])
        copy.start()
        copy.wait()

    def put_down(t):
        at = pl.ds(pl.multiple_of(DOWN + SIDE * t, 16), SIDE)

        def two(i, carry):
            tiles = []
            for j in range(2):
                tile = 3 * (2 * i + j) + t
                rows = pl.ds(pl.multiple_of(tile // 8 * rows_all, 128), rows_all)
                tiles.append(turned[rows, pl.ds(pl.multiple_of(tile % 8 * 128, 128), 128)])
            grad = product(branch_turned[...], jnp.concatenate(tiles, axis=1))
            for j in range(2):
                block = grad[:, 128 * j : 128 * (j + 1)]
                if direct:
                    for n in range(GRID[1]):
                        part[i, j, n // 2, n % 2, at, :] = block[SIDE * n : SIDE * (n + 1)].astype(jnp.bfloat16)
                else:
                    stage[:, :128] = block
                    columns = pl.ds(pl.multiple_of(384 * (2 * i + j) + 128 * t, 128), 128)
                    put(stage.at[:, pl.ds(0, 128)], gdown_ref.at[:, columns])
            return carry

        lax.fori_loop(0, 4, two, 0)

    def narrow_down(c):
        at = pl.multiple_of(256 * c, 128)
        columns = pl.ds(at, 256)
        weight = square[:, columns]
        column_sum = jnp.zeros((1, 256), jnp.float32)
        for r in range(packs):
            rows = slice(LEN * r, LEN * (r + 1))
            value = product(branch[rows, :], weight) * slope[rows, columns].astype(jnp.float32)
            low = value.astype(jnp.bfloat16)
            slope[rows, columns] = low
            column_sum = column_sum + jnp.sum(low.astype(jnp.float32), axis=0, keepdims=True)
        bup[pl.ds(2 * c, 1), :] = column_sum[:, :128]
        bup[pl.ds(2 * c + 1, 1), :] = column_sum[:, 128:]

    def put_up(t, pair):
        first_row = pl.multiple_of(UP + BLOCK * t, 16)
        at = [pl.multiple_of(D * (2 * pair + j) + 128 * t, 128) for j in range(2)]
        columns = jnp.concatenate([slope[:, pl.ds(at[j], 128)] for j in range(2)], axis=1)
        grad = product(turned[2 * D : 3 * D, :], columns)
        for j in range(2):
            block = grad[:, 128 * j : 128 * (j + 1)]
            if direct:
                part[:, :, pair, j, pl.ds(first_row, BLOCK), :] = block.astype(jnp.bfloat16).reshape(
                    GRID[0] // 2, 2, BLOCK, 128
                )
            else:
                stage[:, :128] = block
                put(stage.at[:, pl.ds(0, 128)], gup_ref.at[:, pl.ds(at[j], 128)])

    def norm_back(r):
        rows = pl.ds(pl.multiple_of(r * LEN, LEN), LEN)
        d_first = flow[rows, :]
        for i in range(3):
            d_first = d_first + product_right(slope[rows, rows_all * i : rows_all * (i + 1)], up[D * i : D * (i + 1), :])
        normed = norm[rows, :]
        scaled = d_first * vec_ref[3:4, :D]
        inner_mean = jnp.mean(scaled, axis=1, keepdims=True)
        cross_mean = jnp.mean(scaled * normed, axis=1, keepdims=True)
        d_sum = recip[rows, 0:1] * (scaled - inner_mean - normed * cross_mean)
        flow[rows, :] = d_sum
        low = d_sum.astype(jnp.bfloat16)
        branch[rows, :] = low
        sums[3:4, :D] += jnp.sum(d_first * normed, axis=0, keepdims=True)
        sums[4:5, :D] += jnp.sum(d_first, axis=0, keepdims=True)
        sums[2:3, :D] += jnp.sum(low.astype(jnp.float32), axis=0, keepdims=True)

    def put_out():
        for pair in range(2):
            grad = product(turned[D : 2 * D, :], branch[:, 384 * pair : 384 * (pair + 1)])
            if direct:
                for d in range(GRID[0]):
                    block = grad[BLOCK * d : BLOCK * (d + 1)]
                    take_main(part, d, pair, OUT, block[:, :128], block[:, 256:])
                    take_rest(part, d, pair, OUT + BLOCK, block[:, 128:256])
            else:
                stage[:, :384] = grad
                put(stage.at[:, pl.ds(0, 384)], gsquare_ref.at[pl.ds(3 * D, D), pl.ds(384 * pair, 384)])

    def context_back():
        for r in range(packs):
            rows = slice(LEN * r, LEN * (r + 1))
            turned[3 * D :, rows] = product_right(square[:, 3 * D :], branch[rows, :]).astype(jnp.bfloat16)
        for r in range(packs):
            rows = slice(LEN * r, LEN * (r + 1))
            branch[rows, :] = product_right(branch[rows, :], square[:, 3 * D :]).astype(jnp.bfloat16)

    def unit_of(j, step):
        i, p = j // (packs // 2), 2 * (j % (packs // 2))
        return (i + (i + 1) // 2 if step == "T" else 3 * i + 1), p

    def prob_copy(j, step):
        h, p = unit_of(j, step)
        return pltpu.make_async_copy(prob_in.at[pl.ds(p, 2), pl.ds(2 * h, 2)], prob.at[j % 3], prob_sem.at[j % 3])

    def attend(j, step, count):
        h, p = unit_of(j, step)
        pl.when(j + 2 < count)(lambda: prob_copy(j + 2, step).start())
        prob_copy(j, step).wait()
        tile = pl.multiple_of(128 * h, 128)
        left = left_half((LEN, 128))
        at = [[pl.ds(pl.multiple_of(D * i + tile + 64 * side, 64), 64) for i in range(4)] for side in range(2)]
        parts = []
        for q in range(2):
            rows = pl.ds(pl.multiple_of((p + q) * LEN, LEN), LEN)
            context = branch[rows, pl.ds(tile, 128)]
            all_values = up[pl.ds(pl.multiple_of(2 * D + tile, 128), 128), rows]
            for side in range(2):
                mine = left if side == 0 else jnp.logical_not(left)
                d_prob = product(jnp.where(mine, context, jnp.zeros_like(context)), all_values)
                low = prob[j % 3, q, side]
                share = low.astype(jnp.float32)
                moved = share * d_prob
                d_scores = (moved - share * jnp.sum(moved, axis=1, keepdims=True)).astype(jnp.bfloat16)
                d_values = product(turned[at[side][3], rows], low)
                d_query = product_right(up[at[side][1], rows], d_scores) * HEAD_DIM**-0.5
                d_keys = product(up[at[side][0], rows], d_scores) * HEAD_DIM**-0.5
                parts.append((side, rows, [item.astype(jnp.bfloat16) for item in (d_query, d_keys, d_values)]))
        for side, rows, items in parts:
            for i in range(3):
                up[at[side][i], rows] = items[i]

    def put_tiles(tiles, at):
        for i in range(3):
            for one, two in tiles:
                right = jnp.concatenate(
                    [up[D * i + 128 * one : D * i + 128 * (one + 1), :], up[D * i + 128 * two : D * i + 128 * (two + 1), :]]
                )
                grad = product_right(turned[0:D, :], right)
                if direct:
                    for d in range(GRID[0]):
                        block = grad[BLOCK * d : BLOCK * (d + 1)]
                        if len(tiles) == 2:
                            take_main(part, d, one // 3, at + BLOCK * i, block[:, :128], block[:, 128:])
                        else:
                            take_rest(part, d, 0, at + BLOCK // 2 * i, block[:, :128])
                            take_rest(part, d, 1, at + BLOCK // 2 * i, block[:, 128:])
                else:
                    for k, tile in enumerate((one, two)):
                        stage[:, :128] = grad[:, 128 * k : 128 * (k + 1)]
                        put(stage.at[:, pl.ds(0, 128)], gsquare_ref.at[pl.ds(D * i, D), pl.ds(128 * tile, 128)])

    def put_vectors():
        ones = jnp.ones((8, rows_all), jnp.bfloat16)
        sums[0:1, :D] = product_right(ones, up[0:D, :])[0:1]
        sums[1:2, :D] = product_right(ones, up[2 * D : 3 * D, :])[0:1]
        if direct:
            lane = lax.broadcasted_iota(jnp.int32, (1, 128), 1)
            value = jnp.zeros((1, 128), jnp.float32)
            for p in range(packs):
                value = jnp.where(lane == narrow * packs + p, value_ref[p : p + 1, :], value)
            high = value.astype(jnp.bfloat16).astype(jnp.float32)
            zeros = jnp.zeros((3, 128), jnp.float32)
            for d in range(GRID[0]):
                at, shift = divmod(BLOCK * d, 128)
                wide = sums[:, 128 * at : 128 * at + 256]
                wide = pltpu.roll(wide, 256 - shift, 1) if shift else wide
                mine = lax.broadcasted_iota(jnp.int32, (8, 128), 1) < BLOCK
                own = jnp.where(dp == d, 1.0, 0.0)
                tile = jnp.concatenate(
                    [jnp.where(mine, wide[:8, :128], 0.0), bup[3 * d : 3 * d + 3, :], high * own, (value - high) * own, zeros]
                )
                for n in range(GRID[1]):
                    part[d // 2, d % 2, n // 2, n % 2, 0:16, :] = tile.astype(jnp.bfloat16)

    def widen_back(r):
        rows = pl.ds(pl.multiple_of(r * LEN, LEN), LEN)
        value = product(square[:, :D], up[:D, rows])
        for i in (1, 2):
            value = value + product(square[:, D * i : D * (i + 1)], up[D * i : D * (i + 1), rows])
        norm[rows, :] = flow[rows, :] + jnp.transpose(value)

    after = split_order(BACKWARD_ORDER, "sc321", "DNUBOTMXRW")

    def tick(mark, index=None):
        if not direct:
            return
        for name, pieces in after.items():
            if name[:1] == mark and pieces:
                if index is None:
                    for piece in pieces:
                        g.do(*piece)
                else:

                    @pl.when(index == int(name[1:]))
                    def _():
                        for piece in pieces:
                            g.do(*piece)

    def repeat(mark, first, last, body):
        def step(i, carry):
            body(i)
            tick(mark, i)
            return carry

        lax.fori_loop(first, last, step, 0)

    def up_pair(t):
        put_up(t, 0)
        put_up(t, 1)

    def down_three(i):
        for j in range(3):
            narrow_down(3 * i + j)

    groups = []
    for name in [name for name in after if name]:
        if groups and groups[-1][0] == name[0]:
            groups[-1][1].append(int(name[1:]))
        else:
            groups.append((name[0], [int(name[1:])]))
    for mark, span in groups:
        first, last = span[0], span[-1] + 1
        if mark == "D":
            need("turned branch", "act")
            load("branch", (branch_in, branch))
            load("down", (down_in, square))
            load("slope", (slope_in, slope))
            load("up", *[(up_in.at[:, pl.ds(rows_all * i, rows_all)], up.at[pl.ds(D * i, D), :]) for i in range(3)])
            load("flow", (second_in, flow))
            load("norm", (norm_in, norm))
            load("recip", (recip_in, recip))
            repeat("D", first, last, put_down)
            load("turned", (turned_in, turned.at[pl.ds(0, 3 * D), :]))
        elif mark == "N":
            need("branch", "down", "slope")
            repeat("N", first, last, down_three)
            load("square", (square_in, square))
        elif mark == "U":
            need("turned")
            repeat("U", first, last, up_pair)
        elif mark == "B":
            need("up", "flow", "norm", "recip")
            repeat("B", first, last, norm_back)
            load("qkv", (qkv_in, up))
            for j in range(2):
                prob_copy(j, "T").start()
        elif mark == "O":
            need("turned", "square")
            put_out()
            context_back()
            tick("O", None)
        elif mark == "T":
            need("qkv")
            repeat("T", first, last, lambda j: attend(j, "T", 2 * packs))
            for j in range(2):
                prob_copy(j, "X").start()
        elif mark == "M":
            put_tiles(((0, 2), (3, 5)), MAIN)
            tick("M")
        elif mark == "X":
            repeat("X", first, last, lambda j: attend(j, "X", packs))
        elif mark == "R":
            put_tiles(((1, 4),), REST)
            put_vectors()
            tick("R")
        elif mark == "W":
            repeat("W", first, last, widen_back)
            result = pltpu.make_async_copy(norm, grad_in_out, out_sem.at[1])
            result.start()
    if direct:
        for k in range(len(SCATTER_ROWS)):
            g.drain(k)
    else:
        gvec_ref[...] = sums[...]
        gbup_ref[...] = bup[...]
    result.wait()


def backward_step(direct, operands, dp, narrow):
    rows = operands[1].shape[0]
    vmem = pl.BlockSpec(memory_space=pltpu.VMEM)
    anywhere = pl.BlockSpec(memory_space=pl.ANY)
    full = lambda *shape: jax.ShapeDtypeStruct(shape, jnp.float32)
    room = lambda *shape: pltpu.VMEM(shape, jnp.bfloat16)
    wide = lambda *shape: pltpu.VMEM(shape, jnp.float32)
    if direct:
        outs, places = [full(TOTAL, 128)], [vmem]
        depth = dp // 2
        count = len(SCATTER_ROWS)
        extra = [
            room(depth, 2, 2, 2, TOTAL, 128), room(depth, 2, 2, TOTAL, 128), room(depth, 2, TOTAL, 128),
            room(depth, TOTAL, 128), room(depth - 1, TOTAL, 128),
            pltpu.SemaphoreType.DMA((count, 12)), pltpu.SemaphoreType.DMA((count, 12)),
        ]
    else:
        outs = [full(FF, D), full(D, FF), full(D, FF), full(16, 896), full(32, 128)]
        places = [anywhere] * 3 + [vmem] * 2
        extra = [wide(D, D)]
    return pl.pallas_call(
        functools.partial(backward_kernel, direct),
        name="backward",
        out_shape=(full(rows, D), *outs),
        in_specs=[anywhere] * 5 + [vmem] + [anywhere] * 8 + [vmem] * 2,
        out_specs=(anywhere, *places),
        scratch_shapes=[
            room(FF, rows), room(rows, FF), room(D, FF), room(3 * D, rows), wide(rows, D), wide(rows, D), wide(rows, 128),
            room(rows, D), room(D, rows), room(3, 2, 2, LEN, LEN), wide(16, 896), wide(32, 128),
            pltpu.SemaphoreType.DMA((20,)), pltpu.SemaphoreType.DMA((3,)), pltpu.SemaphoreType.DMA((2,)),
            *extra,
        ],
        compiler_params=pltpu.CompilerParams(
            vmem_limit_bytes=VMEM_LIMIT, **(dict(collective_id=1, has_side_effects=True) if direct else {})
        ),
    )(*operands)


def collect_kernel(packs_all, total, group_in, grad_in, *refs):
    (group_out, loss, grad_out, gq, gqb, gk, gv, gvb, go, gob, gfg, gfs, gup, gupb, gdown, gdownb, gsg, gss, group, grad, in_sem, out_sem) = refs
    parts = [(group_in, group, group_out, i) for i in range(group.shape[0] // LEN)]
    parts += [(grad_in, grad, grad_out, i) for i in range(grad.shape[0] // LEN)]
    ins, outs = [], []
    for k, (src, via, dst, i) in enumerate(parts):
        rows = pl.ds(LEN * i, LEN)
        ins.append(pltpu.make_async_copy(src.at[rows, :], via.at[rows, :], in_sem.at[k]))
        outs.append(pltpu.make_async_copy(via.at[rows, :], dst.at[rows, :], out_sem.at[k]))
        ins[-1].start(priority=k % 2)
    odd = lax.rem(lax.axis_index("narrow"), 2) == 1
    for one, two in zip(ins, outs):
        one.wait()
        two.start(priority=1)
    for i, ref in enumerate((gqb, gvb, gob, gfg, gfs, gdownb, gsg, gss)):
        ref[...] = total[i : i + 1, :BLOCK]
    gupb[...] = total[8:11, :]
    loss[...] = (total[11:12, :] + total[12:13, :])[:, :packs_all]
    for t in range(6):
        gup[:, 128 * t : 128 * (t + 1)] = total[UP + BLOCK * t : UP + BLOCK * (t + 1), :]
    for ref, main, rest in (
        (gq, MAIN, REST), (gk, MAIN + BLOCK, REST + BLOCK // 2), (gv, MAIN + 2 * BLOCK, REST + BLOCK), (go, OUT, OUT + BLOCK),
    ):
        block = unpack_block(total[main : main + BLOCK, :], total[rest : rest + BLOCK // 2, :], odd)
        ref[...] = block[:, :192]
    for t in range(3):
        gdown[:, 128 * t : 128 * (t + 1)] = total[DOWN + SIDE * t : DOWN + SIDE * (t + 1), :]
    for copy in outs:
        copy.wait()


def collect_step(total, group, grad_inputs, dp, narrow):
    packs_all = group.shape[0] // LEN
    vmem = pl.BlockSpec(memory_space=pltpu.VMEM)
    anywhere = pl.BlockSpec(memory_space=pl.ANY)
    full = lambda *shape: jax.ShapeDtypeStruct(shape, jnp.float32)
    square, vector = full(D // dp, D // narrow), full(1, D // dp)
    count = (group.shape[0] + grad_inputs.shape[0]) // LEN
    out = pl.pallas_call(
        functools.partial(collect_kernel, packs_all),
        name="collect",
        out_shape=(
            jax.ShapeDtypeStruct(group.shape, group.dtype), full(1, packs_all), full(*grad_inputs.shape),
            square, vector, square, square, vector, square, vector, vector, vector,
            full(D // dp, FF // narrow), full(FF // dp // 128, 128), full(D // narrow, FF // dp), vector, vector, vector,
        ),
        in_specs=[vmem, anywhere, anywhere],
        out_specs=(anywhere, vmem, anywhere) + (vmem,) * 15,
        scratch_shapes=[
            pltpu.VMEM(group.shape, group.dtype), pltpu.VMEM(grad_inputs.shape, jnp.float32),
            pltpu.SemaphoreType.DMA((count,)), pltpu.SemaphoreType.DMA((count,)),
        ],
        compiler_params=pltpu.CompilerParams(vmem_limit_bytes=VMEM_LIMIT),
    )(total, group, grad_inputs)
    out = [item.reshape(-1) if item.shape[0] in (1, 3) else item for item in out]
    out[14] = out[14].T
    return tuple(out)


def per_device(
    inputs,
    segments,
    row_kind,
    query_weight,
    query_bias,
    key_weight,
    value_weight,
    value_bias,
    output_weight,
    output_bias,
    first_gain,
    first_shift,
    up_weight,
    up_bias,
    down_weight,
    down_bias,
    second_gain,
    second_shift,
    out_cotangent,
    loss_cotangent,
):
    row_count = inputs.shape[0]
    matrices = (query_weight, key_weight, value_weight, output_weight, up_weight, down_weight)
    vectors = (
        query_bias,
        value_bias,
        output_bias,
        first_gain,
        first_shift,
        down_bias,
        second_gain,
        second_shift,
        up_bias,
    )
    dp, narrow = lax.axis_size("dp"), lax.axis_size("narrow")
    direct = (dp, narrow, row_count) == (*GRID, 4 * LEN)
    if direct:
        weights = (*matrices[:5], down_weight.T, *[item.reshape(1, -1) for item in vectors[:8]], up_bias.reshape(-1, 128))
    else:
        weights = fetch_weights(matrices, vectors)
    (square, up, down, vecs, qkv, prob, turned, norm_first, recip_first, active, slope, output_low, norm_second,
     recip_second) = forward_step(direct, weights, inputs, segments, dp, narrow)
    group_out = lax.all_gather(output_low, "narrow", axis=0, tiled=True)
    partial_value, d_second, d_branch, branch_turned, sums_second = transport_step(
        output_low, segments, row_kind, loss_cotangent, out_cotangent, norm_second, recip_second, vecs
    )
    grad_inputs, *grads = backward_step(
        direct,
        (active, slope, d_branch, branch_turned, d_second, sums_second, turned.reshape(3 * D, row_count), norm_first, recip_first, qkv, prob, square,
         up.reshape(D, FF), down, vecs, partial_value),
        dp,
        narrow,
    )
    if direct:
        return collect_step(grads[0], group_out, grad_inputs, dp, narrow)
    transport_loss = lax.all_gather(partial_value[:, 0], "narrow", axis=0, tiled=True)
    squares, g_up, g_down, small, tiles = grads
    mats, vecs = reduce_grads([*squares.reshape(4, D, D), g_up, g_down.T], [*small[:8, :D], tiles[:24].reshape(FF)])
    return (
        group_out,
        transport_loss,
        grad_inputs,
        mats[0],
        vecs[0],
        mats[1],
        mats[2],
        vecs[1],
        mats[3],
        vecs[2],
        vecs[3],
        vecs[4],
        mats[4],
        vecs[8],
        mats[5],
        vecs[5],
        vecs[6],
        vecs[7],
    )


def solution(mesh):
    return jax.shard_map(
        per_device,
        mesh=mesh,
        in_specs=(
            P(("dp", "narrow"), None),
            P("dp", None),
            P("dp", None),
            P("dp", "narrow"),
            P("dp"),
            P("dp", "narrow"),
            P("dp", "narrow"),
            P("dp"),
            P("dp", "narrow"),
            P("dp"),
            P("dp"),
            P("dp"),
            P("dp", "narrow"),
            P("dp"),
            P("dp", "narrow"),
            P("dp"),
            P("dp"),
            P("dp"),
            P(("dp", "narrow"), None),
            P("dp"),
        ),
        out_specs=(
            P("dp", None),
            P("dp"),
            P(("dp", "narrow"), None),
            P("dp", "narrow"),
            P("dp"),
            P("dp", "narrow"),
            P("dp", "narrow"),
            P("dp"),
            P("dp", "narrow"),
            P("dp"),
            P("dp"),
            P("dp"),
            P("dp", "narrow"),
            P("dp"),
            P("dp", "narrow"),
            P("dp"),
            P("dp"),
            P("dp"),
        ),
        check_vma=False,
    )
```

```python
import functools

import jax
import jax.numpy as jnp
from jax import lax
from jax.experimental import pallas as pl
from jax.experimental.pallas import tpu as pltpu
from jax.sharding import PartitionSpec as P

D = 768
HEADS = 12
HEAD_DIM = 64
LEN = 256
ITERS = 20
ROWS = 32
VMEM_LIMIT = 62 * 1024 * 1024

EPS_NORM = 1e-06
BETA = 0.5
MASKED = -1e30


def product(left, right):
    return jnp.dot(left, right, preferred_element_type=jnp.float32)


def product_left(left, right):
    return lax.dot_general(
        left, right, (((0,), (0,)), ((), ())), preferred_element_type=jnp.float32
    )


def product_right(left, right):
    return lax.dot_general(
        left, right, (((1,), (1,)), ((), ())), preferred_element_type=jnp.float32
    )


def fetch_weights(matrices, vectors):
    wide = [lax.all_gather(item, "narrow", axis=1, tiled=True) for item in matrices]
    query, keys, values, output, up, down = [lax.all_gather(item, "dp", axis=0, tiled=True) for item in wide]
    vecs = [lax.all_gather(item, "dp", axis=0, tiled=True).astype(jnp.float32) for item in vectors]
    up = up.reshape(GRID[0], BLOCK, GRID[1], 6, 128).transpose(0, 2, 3, 1, 4)
    up = up.reshape(GRID[0] // 2, 2, GRID[1] // 2, 2, 6 * BLOCK, 128)
    small = jnp.pad(jnp.stack(vecs[:8]), ((0, 8), (0, 128)))
    tiles = jnp.pad(vecs[8].reshape(24, 128), ((0, 8), (0, 0)))
    return (jnp.concatenate([query, keys, values, output], axis=1), up, down.T, small, tiles)


def reduce_grads(matrices, vectors):
    reduced = [lax.psum_scatter(item, "dp", scatter_dimension=0, tiled=True) for item in matrices]
    sums = [lax.psum_scatter(item, "dp", scatter_dimension=0, tiled=True) for item in vectors]
    return (
        [
            lax.psum_scatter(
                item.astype(jnp.bfloat16), "narrow", scatter_dimension=1, tiled=True
            ).astype(jnp.float32)
            for item in reduced
        ],
        lax.psum(sums, "narrow"),
    )


MESH = pl.DeviceIdType.MESH
FF = 4 * D
VEC, SQUARE, UP, DOWN, TOTAL = 0, 16, 592, 1168, 1744
PART = 144
CHUNK_ROWS = (80, 64) * 3 + (144,) * 9
CHUNKS = len(CHUNK_ROWS) + 1
SINGLES = (0, 1, 2, 3, 4, 5, CHUNKS - 1)
GRID = (8, 4)
BLOCK, SIDE = D // GRID[0], D // GRID[1]


def hops():
    dp, narrow = lax.axis_index("dp"), lax.axis_index("narrow")
    return (dp // 2, lax.rem(dp, 2), narrow // 2, lax.rem(narrow, 2))


def place(me, depth, item):
    s, a, b, c = item
    z, x, y, core = me
    z = z if s == 0 else lax.rem(z + s + depth, depth)
    x = 1 - x if a else x
    y = 1 - y if b else y
    core = 1 - core if c else core
    return (2 * z + x, 2 * y + core)


def greet(me, depth):
    peers = [place(me, depth, (s, 0, 0, 0)) for s in range(1, depth)]
    peers += [place(me, depth, (0, *bits)) for bits in ((1, 0, 0), (0, 1, 0), (0, 0, 1))]
    barrier = pltpu.get_barrier_semaphore()
    for peer in peers:
        pl.semaphore_signal(barrier, inc=1, device_id=peer, device_id_type=MESH)
    pl.semaphore_wait(barrier, len(peers))


def number(item):
    s, a, b, c = item
    return ((s * 2 + a) * 2 + b) * 2 + c


GATHER_AXES = (
    "zxy", "zyx", "zxy", "zyx", "zxy", "zyx", "zxy", "zyx", "zxy", "zyx", "zxy", "zyx", "zxy", "zyx", "zxy", "zxy",
)
FORWARD_ORDER = (
    0, 1, 15, 2, 3, 4, 5, 100, 6, 101, 115, 7, 200, 102, 201, 215, 8, 103, 300, 104, 202, 9, 400, 105, 301, 315, 203,
    401, 415, 500, 204, 106, 302, 10, 205, 11, 303, 402, 107, 403, 501, 304, 12, 404, 108, 206, 305, 405, 13, 502,
    109, 600, 207, 110, 601, 208, 602, 111, 603, 306, 112, 406, 700, 307, 209, 113, 210, 407, 800, 308, 408, 801, 14,
    802, 211, 212, 309, 409, 803, 114, 213, 311, 310, 411, 410, 804, 312, 214, 805, 412, 313, 413, 900, 314, 414,
    1000,
)


def split_order(order, kinds, marks):
    after, mark = {"": []}, ""
    for code in order:
        kind, index = divmod(code, 100)
        if kind < len(kinds):
            after[mark].append((kinds[kind], index))
        else:
            mark = marks[kind - len(kinds)] + str(index)
            after[mark] = []
    return after


def chunk_of(k, axes):
    if k == CHUNKS - 1:
        return (k, VEC, SQUARE - VEC, axes[k])
    return (k, SQUARE + sum(CHUNK_ROWS[:k]), CHUNK_ROWS[k], axes[k])


def arrivals(order, depth):
    have, stages = [(0, 0, 0)], []
    for axis in order:
        if axis == "z":
            new = [(far, a, b) for s, a, b in have for far in range(1, depth)]
        else:
            new = [(s, 1, b) if axis == "x" else (s, a, 1) for s, a, b in have]
        stages.append(new)
        have = have + new
    return stages


class Gather:
    def __init__(self, land, pad, send_sem, recv_sem):
        self.land, self.pad, self.send_sem, self.recv_sem = land, pad, send_sem, recv_sem
        self.me = hops()
        self.depth = land.shape[0]

    def block(self, chunk, z, x, y, core):
        return self.land.at[z, x, y, core, pl.ds(chunk[1], chunk[2]), :]

    def copy(self, chunk, block, hop, mark):
        return pltpu.make_async_remote_copy(
            src_ref=block,
            dst_ref=block,
            send_sem=self.send_sem.at[chunk[0]],
            recv_sem=self.recv_sem.at[chunk[0], mark],
            device_id=place(self.me, self.depth, hop),
            device_id_type=MESH,
        )

    def wait(self, chunk, block, mark):
        self.copy(chunk, block, (0, 0, 0, 1), mark).wait_recv()

    def single(self, chunk, item):
        s, a, b = item
        z, x, y, core = self.me
        source = lax.rem(z - s + self.depth, self.depth) if s else z
        return self.block(chunk, source, 1 - x if a else x, 1 - y if b else y, core)

    def send(self, chunk, item, axes):
        s, a, b = item
        block = self.single(chunk, item)
        for axis in axes:
            if axis == "z":
                for far in range(1, self.depth):
                    self.copy(chunk, block, (far, 0, 0, 0), number((far, a, b, 0))).start()
            elif axis == "x":
                self.copy(chunk, block, (0, 1, 0, 0), number((s, 1, b, 0))).start()
            elif axis == "y":
                self.copy(chunk, block, (0, 0, 1, 0), number((s, a, 1, 0))).start()
            else:
                self.copy(chunk, block, (0, 0, 0, 1), 1).start()

    def do(self, kind, k):
        chunk = chunk_of(k, GATHER_AXES)
        order = chunk[3]
        every = slice(None)
        z, x, y, core = self.me
        hop = {"x": (0, 1, 0, 0), "y": (0, 0, 1, 0), "c": (0, 0, 0, 1)}
        if kind == "c":
            self.wait(chunk, self.block(chunk, every, every, every, 1 - core), 1)
        elif k in SINGLES:
            if kind == "s":
                self.send(chunk, (0, 0, 0), order + "c")
            else:
                for item in arrivals(order, self.depth)[int(kind) - 1]:
                    self.wait(chunk, self.single(chunk, item), number((*item, 0)))
                    self.send(chunk, item, order[int(kind) :] + "c")
        elif order[0] == "z":
            column = self.block(chunk, every, x, y, core)
            if order[1] == "x":
                beside, behind = self.block(chunk, every, 1 - x, y, core), self.block(chunk, every, every, 1 - y, core)
            else:
                beside, behind = self.block(chunk, every, x, 1 - y, core), self.block(chunk, every, 1 - x, every, core)
            if kind == "s":
                for far in range(1, self.depth):
                    self.copy(chunk, self.single(chunk, (0, 0, 0)), (far, 0, 0, 0), 2 + far).start()
            elif kind == "1":
                for far in range(1, self.depth):
                    self.wait(chunk, self.single(chunk, (far, 0, 0)), 2 + far)
                for axis, mark in ((order[1], 6), (order[2], 7), ("c", 1)):
                    self.copy(chunk, column, hop[axis], mark).start()
            elif kind == "2":
                self.wait(chunk, beside, 6)
                for axis, mark in ((order[2], 7), ("c", 1)):
                    self.copy(chunk, beside, hop[axis], mark).start()
            else:
                self.wait(chunk, behind, 7)
                self.copy(chunk, behind, hop["c"], 1).start()
        else:
            own = self.single(chunk, (0, 0, 0))
            beside = self.single(chunk, (0, 1, 0) if order[0] == "x" else (0, 0, 1))
            behind = self.block(chunk, z, every, 1 - y, core) if order[0] == "x" else self.block(chunk, z, 1 - x, every, core)
            if kind == "s":
                for axis, mark in ((order[0], 6), (order[1], 7), ("c", 1)):
                    self.copy(chunk, own, hop[axis], mark).start()
            elif kind == "1":
                self.wait(chunk, beside, 6)
                for axis, mark in ((order[1], 7), ("c", 1)):
                    self.copy(chunk, beside, hop[axis], mark).start()
            elif kind == "2":
                self.wait(chunk, behind, 7)
                for far in range(1, self.depth):
                    self.copy(chunk, self.block(chunk, z, every, every, core), (far, 0, 0, 0), 2 + far).start()
                self.copy(chunk, behind, hop["c"], 1).start()
            else:
                for far in range(1, self.depth):
                    layer = self.block(chunk, lax.rem(z - far + self.depth, self.depth), every, every, core)
                    self.wait(chunk, layer, 2 + far)
                    self.copy(chunk, layer, hop["c"], 1).start()

    def drain(self, k):
        chunk = chunk_of(k, GATHER_AXES)
        size = self.pad.at[pl.ds(0, 16 * (8 * self.depth - 1)), pl.ds(0, 128 * chunk[2] // 16)]
        pltpu.make_async_remote_copy(
            src_ref=size,
            dst_ref=size,
            send_sem=self.send_sem.at[k],
            recv_sem=self.recv_sem.at[k, 0],
            device_id=place(self.me, self.depth, (0, 0, 0, 1)),
            device_id_type=MESH,
        ).wait_send()


def swap(half):
    return pltpu.roll(half, 64, 1)


def left_half(shape):
    return lax.broadcasted_iota(jnp.int32, shape, 1) < 64


def pack_block(wide, odd):
    rows = wide.shape[0]
    turned = pltpu.roll(wide, 192, 1)
    main = jnp.where(odd, turned[:, :128], wide[:, :128])
    rest = jnp.where(left_half((rows, 128)), jnp.where(odd, wide[:, :128], wide[:, 128:]), 0.0)
    top, low = rest[: rows // 2], rest[rows // 2 :]
    return main, jnp.where(odd, swap(top) + low, top + swap(low))


def middle_of(even, odd):
    left = left_half(even.shape)
    return jnp.where(left, even, odd), swap(jnp.where(left, odd, even))


def put_main(land, d, at, rows, ref, row, column):
    for pair in range(GRID[1] // 2):
        even, other = land.at[d // 2, d % 2, pair, 0], land.at[d // 2, d % 2, pair, 1]
        left = column + 384 * pair
        ref[pl.ds(row, rows), left : left + 128] = even[at : at + rows, :]
        ref[pl.ds(row, rows), left + 256 : left + 384] = other[at : at + rows, :]


def put_rest(land, d, at, rows, ref, row, column):
    half = rows // 2
    span = slice(at + rows, at + rows + half)
    for pair in range(GRID[1] // 2):
        even, other = land.at[d // 2, d % 2, pair, 0], land.at[d // 2, d % 2, pair, 1]
        top, low = middle_of(even[span, :].astype(jnp.float32), other[span, :].astype(jnp.float32))
        left = column + 384 * pair + 128
        ref[pl.ds(row, half), left : left + 128] = top.astype(jnp.bfloat16)
        ref[pl.ds(row + half, half), left : left + 128] = low.astype(jnp.bfloat16)


def norm_parts(values):
    centre = values - jnp.mean(values, axis=1, keepdims=True)
    spread = jnp.mean(centre * centre, axis=1, keepdims=True)
    recip = lax.rsqrt(spread + EPS_NORM)
    return centre * recip, recip


def gelu_parts(z):
    base = 1.0 + 0.2316419 * jnp.abs(z)
    t = pl.reciprocal(base, approx=True)
    t = t * (2.0 - base * t)
    density = jnp.exp2(z * z * (-0.5 * 1.4426950408889634))
    scale = 0.3989422804014327
    poly = 1.781477937 * scale + t * (-1.821255978 * scale + t * (1.330274429 * scale))
    tail = density * (t * (0.319381530 * scale + t * (-0.356563782 * scale + t * poly)))
    cdf = jnp.where(z < 0.0, tail, 1.0 - tail)
    return z * cdf, cdf + z * density * scale


def forward_kernel(direct, *refs):
    if direct:
        q_ref, k_ref, v_ref, o_ref, upw_ref, downw_ref = refs[:6]
        small_refs = refs[6:15]
        refs = refs[15:]
    else:
        square_in, up_in, down_in, vec_in, bup_in = refs[:5]
        refs = refs[5:]
    rows_in, seg_ref = refs[:2]
    (square_out, up_out, down_out, vec_ref, qkv_out, prob_out, turned_out, norm1_out, recip1_out,
     act_out, slope_out, mixed_out, norm2_out, recip2_out) = refs[2:16]
    (land, square, down, bup, qkv, qkv_turned, prob, turned, ctx, first, flow, norm, recip, act, slope, mixed, in_ref,
     out_sem, pack_sem, tile_sem) = refs[16:36]
    packs = in_ref.shape[0] // LEN
    fetch = pltpu.make_async_copy(rows_in, in_ref, out_sem.at[11])
    fetch.start()
    base = lax.axis_index("narrow") * packs
    pending = {}

    def save(name, src, dst):
        pending[name] = pltpu.make_async_copy(src, dst, out_sem.at[len(pending)])
        pending[name].start()

    if direct:
        send_sem, recv_sem = refs[36:38]
        dp, narrow = lax.axis_index("dp"), lax.axis_index("narrow")
        odd = lax.rem(narrow, 2) == 1
        own = land.at[dp // 2, lax.rem(dp, 2), narrow // 2, lax.rem(narrow, 2)]
        row = lambda ref: jnp.concatenate(
            [ref[...].astype(jnp.float32), jnp.zeros((1, 128 - BLOCK), jnp.float32)], axis=1
        )
        small = [row(ref) for ref in small_refs[:8]] + [small_refs[8][...].astype(jnp.float32)]
        own[0:16, :] = jnp.concatenate([*small, jnp.zeros((5, 128), jnp.float32)]).astype(jnp.bfloat16)
        for i, ref in enumerate((q_ref, k_ref, v_ref, o_ref)):
            main, rest = pack_block(
                jnp.concatenate([ref[...].astype(jnp.float32), jnp.zeros((BLOCK, 64), jnp.float32)], axis=1), odd
            )
            at = SQUARE + PART * i
            own[at : at + BLOCK, :] = main.astype(jnp.bfloat16)
            own[at + BLOCK : at + PART, :] = rest.astype(jnp.bfloat16)
        g = Gather(land, act, send_sem, recv_sem)
        greet(g.me, g.depth)
        after = split_order(FORWARD_ORDER, "s123c", "QAOWGF")
        early = [piece for piece in after[""] if piece[1] < 7 or piece[1] == CHUNKS - 1]
        early = early[: next(i for i, piece in enumerate(early) if piece[0] != "s")]
        for piece in early:
            g.do(*piece)
        for t in range(6):
            own[UP + BLOCK * t : UP + BLOCK * (t + 1), :] = upw_ref[:, 128 * t : 128 * (t + 1)]
        for t in range(3):
            own[DOWN + SIDE * t : DOWN + SIDE * (t + 1), :] = downw_ref[:, 128 * t : 128 * (t + 1)]
        for piece in after[""]:
            if piece not in early:
                g.do(*piece)
        vec_ref[...] = jnp.zeros_like(vec_ref)
        for d in range(GRID[0]):
            tile = land[d // 2, d % 2, 0, 0, 0:16, :].astype(jnp.float32)
            wide = jnp.concatenate([tile, jnp.zeros((16, 128), jnp.float32)], axis=1)
            at, shift = divmod(BLOCK * d, 128)
            wide = pltpu.roll(wide, shift, 1) if shift else wide
            vec_ref[:, 128 * at : 128 * at + 256] += wide
            bup[3 * d : 3 * d + 3, :] = tile[8:11]

        def unpack(i):
            for d in range(GRID[0]):
                put_main(land, d, SQUARE + PART * i, BLOCK, square, BLOCK * d, D * i)
                put_rest(land, d, SQUARE + PART * i, BLOCK, square, BLOCK * d, D * i)

        def pieces_after(mark):
            for piece in after[mark]:
                g.do(*piece)

        def tick(mark, index):
            for name, pieces in after.items():
                if name[:1] == mark and pieces:

                    @pl.when(index == int(name[1:]))
                    def _():
                        for piece in pieces:
                            g.do(*piece)
    else:
        fills = [
            pltpu.make_async_copy(src, dst, out_sem.at[i])
            for i, (src, dst) in enumerate(
                ((square_in, square), (down_in, down), (up_in, land.at[:, :, :, :, pl.ds(UP, DOWN - UP), :]))
            )
        ]
        for copy in fills:
            copy.start()
        vec_ref[...] = vec_in[...]
        bup[...] = bup_in[...]
        for copy in fills:
            copy.wait()
        tick = lambda mark, index: None
        unpack = pieces_after = lambda mark: None

    fetch.wait()
    for i in range(3):
        unpack(i)
        for j in range(3):
            columns = slice(256 * j, 256 * (j + 1))
            part = product(in_ref[...], square[:, D * i + 256 * j : D * i + 256 * (j + 1)])
            if i != 1:
                part = part + vec_ref[i // 2 : i // 2 + 1, columns]
            part = part.astype(jnp.bfloat16)
            qkv[:, D * i + 256 * j : D * i + 256 * (j + 1)] = part
            qkv_turned[D * i + 256 * j : D * i + 256 * (j + 1), :] = jnp.transpose(part)
        pieces_after(f"Q{i}")
    save("qkv", qkv_turned, qkv_out)

    def prob_copy(p):
        return pltpu.make_async_copy(prob.at[p % 2], prob_out.at[p], pack_sem.at[0, p % 2])

    def turned_copy(p):
        at = pl.ds(pl.multiple_of(p * LEN, LEN), LEN)
        return pltpu.make_async_copy(turned.at[p % 2], turned_out.at[:, :, at], pack_sem.at[1, p % 2])

    def attend(p, carry):
        rows = pl.ds(pl.multiple_of(p * LEN, LEN), LEN)
        k = p % 2

        pl.when(p >= 2)(lambda: prob_copy(p - 2).wait())
        seg_row = seg_ref[pl.ds(base + p, 1), :].astype(jnp.float32)
        seg_col = jnp.transpose(jnp.broadcast_to(seg_row, (128, LEN)))
        same = jnp.concatenate([seg_col, seg_col], axis=1) == seg_row
        left = left_half((LEN, 128))
        for h in range(HEADS // 2):
            columns = slice(128 * h, 128 * (h + 1))
            query = qkv[rows, columns] * jnp.asarray(HEAD_DIM**-0.5, jnp.bfloat16)
            keys = qkv[rows, D + 128 * h : D + 128 * (h + 1)]
            values = qkv[rows, 2 * D + 128 * h : 2 * D + 128 * (h + 1)]
            mixes = []
            for side in range(2):
                mine = left if side == 0 else jnp.logical_not(left)
                scores = product_right(jnp.where(mine, query, jnp.zeros_like(query)), keys)
                scores = jnp.where(same, scores, MASKED)
                shifted = jnp.exp(scores - jnp.max(scores, axis=1, keepdims=True))
                total = jnp.sum(shifted, axis=1, keepdims=True)
                low = (shifted * (1.0 / total)).astype(jnp.bfloat16)
                prob[k, 2 * h + side] = low
                mixes.append(product(low, values))
            ctx[rows, columns] = jnp.where(left, mixes[0], mixes[1]).astype(jnp.bfloat16)
        prob_copy(p).start()
        tick("A", p)
        return carry

    lax.fori_loop(0, packs, attend, 0)
    unpack(3)
    save("square", square, square_out)
    prob_copy(packs - 2).wait()
    prob_copy(packs - 1).wait()

    def project(p, carry):
        rows = pl.ds(pl.multiple_of(p * LEN, LEN), LEN)
        k = p % 2

        @pl.when(p >= 2)
        def _():
            turned_copy(p - 2).wait()

        x = in_ref[rows, :]
        context = ctx[rows, :]
        total = x.astype(jnp.float32) + (product(context, square[:, 3 * D :]) + vec_ref[2:3, :D])
        normed, scale = norm_parts(total)
        value = normed * vec_ref[3:4, :D] + vec_ref[4:5, :D]
        first[rows, :] = value
        low = value.astype(jnp.bfloat16)
        flow[rows, :] = low
        norm[rows, :] = normed
        recip[rows, :] = jnp.broadcast_to(scale, (LEN, 128))
        turned[k, 0] = jnp.transpose(x)
        turned[k, 1] = jnp.transpose(context)
        turned[k, 2] = jnp.transpose(low)
        turned_copy(p).start()
        return carry

    lax.fori_loop(0, packs, project, 0)
    pieces_after("O0")
    save("norm", norm, norm1_out)
    save("recip", recip, recip1_out)
    turned_copy(packs - 2).wait()
    turned_copy(packs - 1).wait()

    def tile_copies(t):
        k = t % 2
        copies = []
        for n in range(GRID[1]):
            columns = pl.ds(pl.multiple_of(D * n + 128 * t, 128), 128)
            first_row = pl.multiple_of(UP + BLOCK * t, 16)
            copies += [
                pltpu.make_async_copy(slope.at[k, n], slope_out.at[:, columns], tile_sem.at[0, k, n]),
                pltpu.make_async_copy(act.at[:, columns], act_out.at[:, columns], tile_sem.at[1, k, n]),
                pltpu.make_async_copy(
                    land.at[:, :, n // 2, n % 2, pl.ds(first_row, BLOCK), :], up_out.at[:, :, :, columns], tile_sem.at[2, k, n]
                ),
            ]
        return copies

    def widen(t, carry):
        k = t % 2

        @pl.when(t >= 2)
        def _():
            for copy in tile_copies(t - 2):
                copy.wait()

        first_row = pl.multiple_of(UP + BLOCK * t, 16)
        for pair in range(2):
            weight = jnp.concatenate(
                [land[:, :, pair, i, pl.ds(first_row, BLOCK), :].reshape(D, 128) for i in range(2)], axis=1
            )
            bias = jnp.concatenate([bup[pl.ds(6 * (2 * pair + i) + t, 1), :] for i in range(2)], axis=1)
            for r in range(packs):
                rows = slice(LEN * r, LEN * (r + 1))
                value, turn = gelu_parts(product(flow[rows, :], weight) + bias)
                value, turn = value.astype(jnp.bfloat16), turn.astype(jnp.bfloat16)
                for i in range(2):
                    n = 2 * pair + i
                    columns = pl.ds(pl.multiple_of(D * n + 128 * t, 128), 128)
                    act[rows, columns] = value[:, 128 * i : 128 * (i + 1)]
                    slope[k, n, rows, :] = turn[:, 128 * i : 128 * (i + 1)]
        for copy in tile_copies(t):
            copy.start()
        tick("W", t)
        return carry

    lax.fori_loop(0, 6, widen, 0)
    def down_part(*tiles):
        if direct:
            for d in range(GRID[0]):
                for n in range(GRID[1]):
                    for t in tiles:
                        at = 384 * d + 128 * t
                        down[SIDE * n : SIDE * (n + 1), at : at + 128] = land[
                            d // 2, d % 2, n // 2, n % 2, DOWN + SIDE * t : DOWN + SIDE * (t + 1), :
                        ]
        spans = [slice(384 * d + 128 * t, 384 * d + 128 * (t + 1)) for d in range(GRID[0]) for t in tiles]
        for j in range(3):
            columns = slice(256 * j, 256 * (j + 1))
            weight = jnp.concatenate([down[columns, span] for span in spans], axis=1)
            for r in range(packs):
                rows = slice(LEN * r, LEN * (r + 1))
                hidden = jnp.concatenate([act[rows, span] for span in spans], axis=1)
                first[rows, columns] = first[rows, columns] + product_right(hidden, weight)

    down_part(0, 1)
    pieces_after("G0")
    down_part(2)
    save("down", down, down_out)
    pending["norm"].wait()
    pending["recip"].wait()

    def finish(p, carry):
        rows = pl.ds(pl.multiple_of(p * LEN, LEN), LEN)
        normed, scale = norm_parts(first[rows, :] + vec_ref[5:6, :D])
        norm[rows, :] = normed
        recip[rows, :] = jnp.broadcast_to(scale, (LEN, 128))
        mixed[rows, :] = (normed * vec_ref[6:7, :D] + vec_ref[7:8, :D]).astype(jnp.bfloat16)
        return carry

    lax.fori_loop(0, packs, finish, 0)
    save("mixed", mixed, mixed_out)
    save("norm2", norm, norm2_out)
    save("recip2", recip, recip2_out)
    for t in (4, 5):
        for copy in tile_copies(t):
            copy.wait()
    if direct:
        for k in range(CHUNKS):
            g.drain(k)
    for name, copy in pending.items():
        if name not in ("norm", "recip"):
            copy.wait()


def forward_step(direct, weights, inputs, segments, dp, narrow):
    rows = inputs.shape[0]
    packs = rows // LEN
    vmem = pl.BlockSpec(memory_space=pltpu.VMEM)
    anywhere = pl.BlockSpec(memory_space=pl.ANY)
    low = lambda *shape: jax.ShapeDtypeStruct(shape, jnp.bfloat16)
    full = lambda *shape: jax.ShapeDtypeStruct(shape, jnp.float32)
    room = lambda *shape: pltpu.VMEM(shape, jnp.bfloat16)
    wide = lambda *shape: pltpu.VMEM(shape, jnp.float32)
    sems = [pltpu.SemaphoreType.DMA((CHUNKS,)), pltpu.SemaphoreType.DMA((CHUNKS, 32))] if direct else []
    return pl.pallas_call(
        functools.partial(forward_kernel, direct),
        name="forward",
        out_shape=(
            low(D, FF), low(GRID[0] // 2, 2, BLOCK, FF), low(D, FF), full(16, 896),
            low(3 * D, rows), low(packs, HEADS, LEN, LEN), low(3, D, rows), full(rows, D), full(rows, 128),
            low(rows, FF), low(rows, FF), low(rows, D), full(rows, D), full(rows, 128),
        ),
        in_specs=([vmem] * 15 if direct else [anywhere] * 3 + [vmem] * 2) + [anywhere, vmem],
        out_specs=(anywhere,) * 3 + (vmem,) + (anywhere,) * 10,
        scratch_shapes=[
            room(GRID[0] // 2, 2, GRID[1] // 2, 2, TOTAL, 128), room(D, FF), room(D, FF), wide(32, 128),
            room(rows, 3 * D), room(3 * D, rows), room(2, HEADS, LEN, LEN), room(2, 3, D, LEN), room(rows, D), wide(rows, D), room(rows, D),
            wide(rows, D), wide(rows, 128), room(rows, FF), room(2, 4, rows, 128), room(rows, D), room(rows, D),
            pltpu.SemaphoreType.DMA((12,)), pltpu.SemaphoreType.DMA((2, 2)), pltpu.SemaphoreType.DMA((3, 2, 4)),
            *sems,
        ],
        compiler_params=pltpu.CompilerParams(
            vmem_limit_bytes=VMEM_LIMIT, **(dict(collective_id=0, has_side_effects=True) if direct else {})
        ),
    )(*weights, inputs, segments)


def transport_kernel(
    mixed_ref, seg_ref, kind_ref, weight_ref, cot_in, normed_in, recip_in, gain_ref,
    value_ref, second_out, branch_out, turned_out, sums_ref,
    kern_ref, prod_ref, flow_ref, acc_ref, left_ref, sigma_ref,
    cot_ref, normed_ref, recip_ref, second_ref, branch_ref, turned_ref, load_sem, save_sem,
):
    loads = [
        pltpu.make_async_copy(src, dst, load_sem.at[i])
        for i, (src, dst) in enumerate(((cot_in, cot_ref), (normed_in, normed_ref), (recip_in, recip_ref)))
    ]
    for copy in loads:
        copy.start()
    packs = mixed_ref.shape[0] // LEN
    base = lax.axis_index("narrow") * packs
    blocks = LEN // ROWS
    lanes = lambda col: jnp.concatenate([col, col], axis=1)
    fold = lambda wide: wide[:, :128] + wide[:, 128:]
    eight = lambda wide: jnp.sum(wide.reshape(ROWS // 8, 8, LEN), axis=0)
    replicate = lambda col: jnp.broadcast_to(col, (ROWS, 128))

    def turned(row):
        return jnp.transpose(jnp.broadcast_to(row, (128, LEN)))

    for p in range(packs):
        rows = pl.ds(p * LEN, LEN)
        feats = mixed_ref[rows, :].astype(jnp.float32)
        recip = lax.rsqrt(jnp.sum(feats * feats, axis=1, keepdims=True) + EPS_NORM)
        unit = (feats * recip).astype(jnp.bfloat16)
        cosine = product_right(unit, unit)
        seg_row = seg_ref[pl.ds(base + p, 1), :].astype(jnp.float32)
        region_row = jnp.where(kind_ref[pl.ds(base + p, 1), :] == 0, 0.0, 1.0)
        seg_col = turned(seg_row)
        word_col = 1.0 - turned(region_row)
        same = jnp.where(lanes(seg_col) == seg_row, 1.0, 0.0)
        word_count = jnp.sum(same * (1.0 - region_row), axis=1, keepdims=True)
        region_count = jnp.sum(same * lanes(1.0 - word_col), axis=0, keepdims=True)
        kern_ref[p] = jnp.exp((cosine - 1.0) * (1.0 / BETA)) * same * lanes(word_col) * region_row
        left_ref[p, 0] = word_col
        left_ref[p, 1] = jnp.broadcast_to(word_count, (LEN, 128))
        left_ref[p, 2] = 1.0 - word_col
        prod_ref[0, p] = jnp.ones((LEN, LEN), jnp.float32)
        sigma_ref[0, p, 0:1] = region_row / region_count
        sigma_ref[0, p, 1:2] = region_row
        sigma_ref[0, p, 2:3] = region_count

    def advance(t, carry):
        for p in range(packs):
            sigma = sigma_ref[t, p, 0:1]
            scale = jnp.where(t == 0, 1.0, sigma)
            region = sigma_ref[0, p, 1:2]
            count = sigma_ref[0, p, 2:3]
            total = jnp.zeros((8, LEN), jnp.float32)
            for b in range(blocks):
                rows = pl.ds(b * ROWS, ROWS)
                weighted = kern_ref[p, rows, :] * (prod_ref[t, p, rows, :] * scale)
                row_sum = jnp.sum(fold(weighted * sigma), axis=1, keepdims=True)
                word = left_ref[p, 0, rows, :]
                base = left_ref[p, 1, rows, :] * replicate(row_sum) + left_ref[p, 2, rows, :]
                delta = pl.reciprocal(base, approx=True)
                delta = word * delta * (2.0 - base * delta)
                scaled = weighted * lanes(delta)
                prod_ref[t + 1, p, rows, :] = scaled
                total = total + eight(scaled)
            col_sum = jnp.sum(total, axis=0, keepdims=True)
            sigma_ref[t + 1, p, 0:1] = region / (count * col_sum + 1.0 - region)
        return carry

    lax.fori_loop(0, ITERS, advance, 0, unroll=2)

    starts = []
    for p in range(packs):
        rows = pl.ds(p * LEN, LEN)
        weight = weight_ref[base + p]
        feats = mixed_ref[rows, :].astype(jnp.float32)
        recip = lax.rsqrt(jnp.sum(feats * feats, axis=1, keepdims=True) + EPS_NORM)
        unit = (feats * recip).astype(jnp.bfloat16)
        cosine = product_right(unit, unit)
        moved = (prod_ref[ITERS, p] * sigma_ref[ITERS, p, 0:1]) * (1.0 - cosine)
        value_ref[p : p + 1, :] = jnp.broadcast_to(jnp.sum(moved), (1, 128))
        moved = moved * weight
        flow_ref[p] = moved
        acc_ref[p] = jnp.zeros((LEN, LEN), jnp.float32)
        starts += [jnp.sum(moved, axis=0, keepdims=True), jnp.zeros((1, LEN), jnp.float32)]

    def retreat(step, carry):
        t = ITERS - 1 - step
        out = []
        for p in range(packs):
            flow_sum, spread = carry[2 * p : 2 * p + 2]
            before = sigma_ref[t, p, 0:1]
            d_col = -sigma_ref[0, p, 2:3] * sigma_ref[t + 1, p, 0:1] * (spread + flow_sum)
            total = jnp.zeros((8, LEN), jnp.float32)
            shift = jnp.zeros((8, LEN), jnp.float32)
            for b in range(blocks):
                rows = pl.ds(b * ROWS, ROWS)
                scaled = prod_ref[t + 1, p, rows, :]
                flow = flow_ref[p, rows, :] + scaled * d_col
                d_row = replicate(jnp.sum(fold(flow), axis=1, keepdims=True))
                d_row = -left_ref[p, 1, rows, :] * d_row
                moved = scaled * lanes(d_row)
                flow = flow + moved * before
                flow_ref[p, rows, :] = flow
                acc_ref[p, rows, :] = acc_ref[p, rows, :] + flow
                total = total + eight(flow)
                shift = shift + eight(moved)
            out += [
                jnp.sum(total, axis=0, keepdims=True),
                before * jnp.sum(shift, axis=0, keepdims=True),
            ]
        return tuple(out)

    lax.fori_loop(0, ITERS, retreat, tuple(starts), unroll=2)

    for copy in loads:
        copy.wait()
    saves = []
    sums = [jnp.zeros((1, D), jnp.float32)] * 3
    for p in range(packs):
        rows = pl.ds(p * LEN, LEN)
        coupling = prod_ref[ITERS, p] * sigma_ref[ITERS, p, 0:1]
        d_cost = weight_ref[base + p] * coupling - acc_ref[p] * (1.0 / BETA)
        d_cosine = (-d_cost).astype(jnp.bfloat16)
        feats = mixed_ref[rows, :].astype(jnp.float32)
        recip = lax.rsqrt(jnp.sum(feats * feats, axis=1, keepdims=True) + EPS_NORM)
        unit = feats * recip
        unit_low = unit.astype(jnp.bfloat16)
        d_unit = product(d_cosine, unit_low) + product_left(d_cosine, unit_low)
        d_mixed = cot_ref[rows, :].astype(jnp.float32) + recip * (
            d_unit - unit * jnp.sum(d_unit * unit, axis=1, keepdims=True)
        )
        normed = normed_ref[rows, :]
        scaled = d_mixed * gain_ref[6:7, :D]
        inner_mean = jnp.mean(scaled, axis=1, keepdims=True)
        cross_mean = jnp.mean(scaled * normed, axis=1, keepdims=True)
        d_second = recip_ref[rows, 0:1] * (scaled - inner_mean - normed * cross_mean)
        d_branch = d_second.astype(jnp.bfloat16)
        second_ref[rows, :] = d_second
        branch_ref[rows, :] = d_branch
        turned_ref[:, rows] = jnp.transpose(d_branch)
        for src, dst in (
            (second_ref.at[rows, :], second_out.at[rows, :]),
            (branch_ref.at[rows, :], branch_out.at[rows, :]),
            (turned_ref.at[:, rows], turned_out.at[:, rows]),
        ):
            copy = pltpu.make_async_copy(src, dst, save_sem.at[len(saves)])
            copy.start()
            saves.append(copy)
        sums[0] = sums[0] + jnp.sum(d_mixed * normed, axis=0, keepdims=True)
        sums[1] = sums[1] + jnp.sum(d_mixed, axis=0, keepdims=True)
        sums[2] = sums[2] + jnp.sum(d_branch.astype(jnp.float32), axis=0, keepdims=True)
    for k in range(3):
        sums_ref[k : k + 1, :] = sums[k]
    for copy in saves:
        copy.wait()


def transport_step(mixed, segments, row_kind, weight, cotangent, normed, recip, gain):
    rows = mixed.shape[0]
    packs = rows // LEN
    vmem = pl.BlockSpec(memory_space=pltpu.VMEM)
    anywhere = pl.BlockSpec(memory_space=pl.ANY)
    square = (packs, LEN, LEN)
    return pl.pallas_call(
        transport_kernel,
        name="transport",
        out_shape=(
            jax.ShapeDtypeStruct((packs, 128), jnp.float32),
            jax.ShapeDtypeStruct((rows, D), jnp.float32),
            jax.ShapeDtypeStruct((rows, D), jnp.bfloat16),
            jax.ShapeDtypeStruct((D, rows), jnp.bfloat16),
            jax.ShapeDtypeStruct((8, D), jnp.float32),
        ),
        in_specs=[vmem, vmem, vmem, pl.BlockSpec(memory_space=pltpu.SMEM), anywhere, anywhere, anywhere, vmem],
        out_specs=(vmem, anywhere, anywhere, anywhere, vmem),
        scratch_shapes=[
            pltpu.VMEM(square, jnp.float32),
            pltpu.VMEM((ITERS + 1, *square), jnp.float32),
            pltpu.VMEM(square, jnp.float32),
            pltpu.VMEM(square, jnp.float32),
            pltpu.VMEM((packs, 3, LEN, 128), jnp.float32),
            pltpu.VMEM((ITERS + 1, packs, 8, LEN), jnp.float32),
            pltpu.VMEM((rows, D), jnp.bfloat16),
            pltpu.VMEM((rows, D), jnp.float32),
            pltpu.VMEM((rows, 128), jnp.float32),
            pltpu.VMEM((rows, D), jnp.float32),
            pltpu.VMEM((rows, D), jnp.bfloat16),
            pltpu.VMEM((D, rows), jnp.bfloat16),
            pltpu.SemaphoreType.DMA((3,)),
            pltpu.SemaphoreType.DMA((3 * packs,)),
        ],
        compiler_params=pltpu.CompilerParams(vmem_limit_bytes=VMEM_LIMIT),
    )(mixed, segments, row_kind, weight, cotangent, normed, recip, gain)


REST, OUT, MAIN = 16, 160, 304
SCATTER_ROWS = (80, 80, 80, 64, 80, 64, 80, 64) + (144,) * 4 + (96,) * 6
SCATTER_AXES = (
    "zyx", "yxz", "xyz", "xyz", "yxz", "xyz", "xyz", "xyz", "zxy", "xyz", "yxz", "xyz", "xyz", "yxz", "yxz", "zyx",
    "xyz", "yxz",
)
BACKWARD_ORDER = (
    500, 12, 13, 501, 14, 15, 502, 16, 17, 112, 113, 600, 114, 601, 115, 116, 602, 117, 603, 700, 701, 8, 702, 9, 212,
    213, 703, 704, 10, 108, 109, 705, 11, 216, 214, 800, 110, 313, 111, 801, 215, 802, 217, 803, 312, 900, 2, 3, 209,
    316, 1000, 102, 314, 1001, 103, 1002, 1003, 208, 210, 315, 1004, 211, 413, 1005, 309, 317, 1006, 412, 1007, 202,
    416, 1100, 4, 5, 6, 7, 311, 414, 1200, 104, 203, 1201, 105, 106, 107, 302, 308, 409, 1202, 310, 417, 1203, 415,
    1300, 0, 1, 204, 205, 303, 402, 411, 1400, 100, 101, 408, 1401, 206, 410, 1402, 305, 403, 207, 1403, 304, 201,
    306, 307, 200, 301, 405, 404, 300, 406, 407, 400, 401,
)


class Scatter:
    def __init__(self, part, lands, send_sem, recv_sem, total):
        self.part, self.lands, self.send_sem, self.recv_sem, self.total = part, lands, send_sem, recv_sem, total
        self.me = hops()
        self.depth = part.shape[0]

    def copies(self, k):
        first, order = sum(SCATTER_ROWS[:k]), SCATTER_AXES[k]
        span = pl.ds(first, SCATTER_ROWS[k])
        every = slice(None)
        z, x, y, core = self.me
        part = lambda *at: self.part.at[*at, span, :]
        land_c, land_q, land_p, land_z = self.lands
        land = lambda ref, *at: ref.at[*at, span, :]
        to_x, to_y = (0, 1, 0, 0), (0, 0, 1, 0)
        stages = {"c": [], "3": [], "2": [], "1": []}
        ahead = lambda far: lax.rem(z + far, self.depth)
        if order[0] == "y":
            stages["c"] = [
                (part(every, every, 1 - y, 1 - core), land(land_c, every, every, 1 - y), None, part(every, every, 1 - y, core)),
                (part(every, every, y, 1 - core), land(land_c, every, every, y), None, part(every, every, y, core)),
            ]
        elif order[0] == "x":
            stages["c"] = [
                (part(every, 1 - x, every, 1 - core), land(land_c, every, 1 - x, every), None, part(every, 1 - x, every, core)),
                (part(every, x, every, 1 - core), land(land_c, every, x, every), None, part(every, x, every, core)),
            ]
        else:
            stages["c"] = [(part(every, every, every, 1 - core), land(land_c, every, every, every), None, part(every, every, every, core))]
        if order == "yxz":
            stages["3"] = [(part(every, every, 1 - y, core), land(land_q, every, every), to_y, part(every, every, y, core))]
            stages["2"] = [(part(every, 1 - x, y, core), land(land_p, every), to_x, part(every, x, y, core))]
        elif order == "xyz":
            stages["3"] = [(part(every, 1 - x, every, core), land(land_q, every, every), to_x, part(every, x, every, core))]
            stages["2"] = [(part(every, x, 1 - y, core), land(land_p, every), to_y, part(every, x, y, core))]
        else:
            for far in range(1, self.depth):
                for i in range(2):
                    slot = 2 * (far - 1) + i
                    where = land(land_q, slot, every) if slot < 4 else land(land_p, slice(2 * slot - 8, 2 * slot - 6))
                    stages["3"].append((part(ahead(far), i, every, core), where, (far, 0, 0, 0), part(z, i, every, core)))
            pair, last = land(land_z, slice(0, 2)), land(land_z, 2)
            if order[1] == "y":
                stages["2"] = [(part(z, every, 1 - y, core), pair, to_y, part(z, every, y, core))]
                stages["1"] = [(part(z, 1 - x, y, core), last, to_x, part(z, x, y, core))]
            else:
                stages["2"] = [(part(z, 1 - x, every, core), pair, to_x, part(z, x, every, core))]
                stages["1"] = [(part(z, x, 1 - y, core), last, to_y, part(z, x, y, core))]
        if order[2] == "z":
            stages["1"] = [
                (part(ahead(far), x, y, core), land(land_z, far - 1), (far, 0, 0, 0), part(z, x, y, core))
                for far in range(1, self.depth)
            ]
        made, mark = {}, 0
        for stage, items in stages.items():
            made[stage] = []
            for src, dst, hop, into in items:
                if stage != "c":
                    copy = functools.partial(self.copy, k, mark, src, dst, hop)
                    made[stage].append((copy, dst, into))
                    mark += 1
                else:
                    made[stage].append((None, dst, into))
        whole = functools.partial(
            self.copy, k, mark, part(every, every, every, 1 - core), land(land_c, every, every, every), (0, 0, 0, 1)
        )
        return whole, made

    def copy(self, k, mark, src, dst, hop):
        return pltpu.make_async_remote_copy(
            src_ref=src,
            dst_ref=dst,
            send_sem=self.send_sem.at[k, mark],
            recv_sem=self.recv_sem.at[k, mark],
            device_id=place(self.me, self.depth, hop),
            device_id_type=MESH,
        )

    def do(self, kind, k):
        whole, made = self.copies(k)
        if kind == "s":
            whole().start()
            return
        if kind == "c":
            whole().wait_recv()
        following = {"c": "3", "3": "2", "2": "1"}.get(kind)
        first, rows = sum(SCATTER_ROWS[:k]), SCATTER_ROWS[k]
        for i, (copy, land, into) in enumerate(made[kind]):
            if kind != "c":
                copy().wait_recv()
            if kind != "1":
                into[...] = into[...] + land[...]
            if kind == "c" and i == 0 and len(made["c"]) == 2:
                made["3"][0][0]().start()
        if kind == "1":
            value = made["1"][0][2][...].astype(jnp.float32)
            for copy, land, into in made["1"]:
                value = value + land[...].astype(jnp.float32)
            self.total[pl.ds(first, rows), :] = value
        elif not (kind == "c" and len(made["c"]) == 2):
            for copy, land, into in made[following]:
                copy().start()

    def drain(self, k):
        whole, made = self.copies(k)
        whole().wait_send()
        for stage in "321":
            for copy, land, into in made[stage]:
                copy().wait_send()


def fold_middle(top, low):
    left = left_half(top.shape)
    return jnp.where(left, top, swap(low)), jnp.where(left, swap(low), top)


def take_main(part, d, pair, at, even, other):
    rows = even.shape[0]
    part[d // 2, d % 2, pair, 0, at : at + rows, :] = even.astype(jnp.bfloat16)
    part[d // 2, d % 2, pair, 1, at : at + rows, :] = other.astype(jnp.bfloat16)


def take_rest(part, d, pair, at, block):
    half = block.shape[0] // 2
    one, two = fold_middle(block[:half], block[half:])
    take_main(part, d, pair, at, one, two)


def unpack_block(main, rest, odd):
    other = swap(rest)
    top, low = jnp.where(odd, other, rest), jnp.where(odd, rest, other)
    piece = jnp.concatenate([top, low], axis=0)
    left = left_half(piece.shape)
    swapped = swap(main)
    first = jnp.where(odd, jnp.where(left, piece, swapped), main)
    second = jnp.where(odd, swapped, piece)
    return jnp.concatenate([first, second], axis=1)


def backward_kernel(direct, *refs):
    (act_in, slope_in, branch_in, branch_turned_in, second_in, sums_in, turned_in, norm_in, recip_in, qkv_in, prob_in,
     square_in, up_in, down_in, vec_ref, value_ref) = refs[:16]
    refs = refs[16:]
    if direct:
        grad_in_out, total = refs[:2]
        refs = refs[2:]
    else:
        grad_in_out, gsquare_ref, gup_ref, gdown_ref, gvec_ref, gbup_ref = refs[:6]
        refs = refs[6:]
    (turned, slope, square, up, flow, norm, recip, branch, branch_turned, prob, sums, bup, load_sem, prob_sem,
     out_sem) = refs[:15]
    rows_all = slope.shape[0]
    packs = rows_all // LEN
    if direct:
        part, land_c, land_q, land_p, land_z, send_sem, recv_sem = refs[15:22]
        g = Scatter(part, (land_c, land_q, land_p, land_z), send_sem, recv_sem, total)
        dp, narrow = lax.axis_index("dp"), lax.axis_index("narrow")
    else:
        (stage,) = refs[15:16]

    loads, waited = {}, set()

    def load(name, *pairs):
        loads[name] = []
        for src, dst in pairs:
            copy = pltpu.make_async_copy(src, dst, load_sem.at[sum(map(len, loads.values()))])
            copy.start()
            loads[name].append(copy)

    def need(*names):
        for name in names:
            if name not in waited:
                waited.add(name)
                for copy in loads[name]:
                    copy.wait()

    blocks = [pl.ds(rows_all * i, rows_all) for i in range(3)]
    load("turned branch", (branch_turned_in, branch_turned))
    load("act", *[(act_in.at[:, span], turned.at[span, :]) for span in blocks])
    if direct:
        greet(g.me, g.depth)
    sums[...] = jnp.zeros_like(sums)
    bup[...] = jnp.zeros_like(bup)
    sums[5:6, :D] = sums_in[2:3, :]
    sums[6:7, :D] = sums_in[0:1, :]
    sums[7:8, :D] = sums_in[1:2, :]

    def put(src, dst):
        copy = pltpu.make_async_copy(src, dst, out_sem.at[0])
        copy.start()
        copy.wait()

    def put_down(t):
        at = pl.ds(pl.multiple_of(DOWN + SIDE * t, 16), SIDE)

        def two(i, carry):
            tiles = []
            for j in range(2):
                tile = 3 * (2 * i + j) + t
                rows = pl.ds(pl.multiple_of(tile // 8 * rows_all, 128), rows_all)
                tiles.append(turned[rows, pl.ds(pl.multiple_of(tile % 8 * 128, 128), 128)])
            grad = product(branch_turned[...], jnp.concatenate(tiles, axis=1))
            for j in range(2):
                block = grad[:, 128 * j : 128 * (j + 1)]
                if direct:
                    for n in range(GRID[1]):
                        part[i, j, n // 2, n % 2, at, :] = block[SIDE * n : SIDE * (n + 1)].astype(jnp.bfloat16)
                else:
                    stage[:, :128] = block
                    columns = pl.ds(pl.multiple_of(384 * (2 * i + j) + 128 * t, 128), 128)
                    put(stage.at[:, pl.ds(0, 128)], gdown_ref.at[:, columns])
            return carry

        lax.fori_loop(0, 4, two, 0)

    def narrow_down(c):
        at = pl.multiple_of(256 * c, 128)
        columns = pl.ds(at, 256)
        weight = square[:, columns]
        column_sum = jnp.zeros((1, 256), jnp.float32)
        for r in range(packs):
            rows = slice(LEN * r, LEN * (r + 1))
            value = product(branch[rows, :], weight) * slope[rows, columns].astype(jnp.float32)
            low = value.astype(jnp.bfloat16)
            slope[rows, columns] = low
            column_sum = column_sum + jnp.sum(low.astype(jnp.float32), axis=0, keepdims=True)
        bup[pl.ds(2 * c, 1), :] = column_sum[:, :128]
        bup[pl.ds(2 * c + 1, 1), :] = column_sum[:, 128:]

    def put_up(t, pair):
        first_row = pl.multiple_of(UP + BLOCK * t, 16)
        at = [pl.multiple_of(D * (2 * pair + j) + 128 * t, 128) for j in range(2)]
        columns = jnp.concatenate([slope[:, pl.ds(at[j], 128)] for j in range(2)], axis=1)
        grad = product(turned[2 * D : 3 * D, :], columns)
        for j in range(2):
            block = grad[:, 128 * j : 128 * (j + 1)]
            if direct:
                part[:, :, pair, j, pl.ds(first_row, BLOCK), :] = block.astype(jnp.bfloat16).reshape(
                    GRID[0] // 2, 2, BLOCK, 128
                )
            else:
                stage[:, :128] = block
                put(stage.at[:, pl.ds(0, 128)], gup_ref.at[:, pl.ds(at[j], 128)])

    def norm_back(r):
        rows = pl.ds(pl.multiple_of(r * LEN, LEN), LEN)
        d_first = flow[rows, :]
        for i in range(3):
            d_first = d_first + product_right(slope[rows, rows_all * i : rows_all * (i + 1)], up[D * i : D * (i + 1), :])
        normed = norm[rows, :]
        scaled = d_first * vec_ref[3:4, :D]
        inner_mean = jnp.mean(scaled, axis=1, keepdims=True)
        cross_mean = jnp.mean(scaled * normed, axis=1, keepdims=True)
        d_sum = recip[rows, 0:1] * (scaled - inner_mean - normed * cross_mean)
        flow[rows, :] = d_sum
        low = d_sum.astype(jnp.bfloat16)
        branch[rows, :] = low
        sums[3:4, :D] += jnp.sum(d_first * normed, axis=0, keepdims=True)
        sums[4:5, :D] += jnp.sum(d_first, axis=0, keepdims=True)
        sums[2:3, :D] += jnp.sum(low.astype(jnp.float32), axis=0, keepdims=True)

    def put_out():
        for pair in range(2):
            grad = product(turned[D : 2 * D, :], branch[:, 384 * pair : 384 * (pair + 1)])
            if direct:
                for d in range(GRID[0]):
                    block = grad[BLOCK * d : BLOCK * (d + 1)]
                    take_main(part, d, pair, OUT, block[:, :128], block[:, 256:])
                    take_rest(part, d, pair, OUT + BLOCK, block[:, 128:256])
            else:
                stage[:, :384] = grad
                put(stage.at[:, pl.ds(0, 384)], gsquare_ref.at[pl.ds(3 * D, D), pl.ds(384 * pair, 384)])

    def context_back():
        for r in range(packs):
            rows = slice(LEN * r, LEN * (r + 1))
            turned[3 * D :, rows] = product_right(square[:, 3 * D :], branch[rows, :]).astype(jnp.bfloat16)
        for r in range(packs):
            rows = slice(LEN * r, LEN * (r + 1))
            branch[rows, :] = product_right(branch[rows, :], square[:, 3 * D :]).astype(jnp.bfloat16)

    def unit_of(j, step):
        i, p = j // (packs // 2), 2 * (j % (packs // 2))
        return (i + (i + 1) // 2 if step == "T" else 3 * i + 1), p

    def prob_copy(j, step):
        h, p = unit_of(j, step)
        return pltpu.make_async_copy(prob_in.at[pl.ds(p, 2), pl.ds(2 * h, 2)], prob.at[j % 3], prob_sem.at[j % 3])

    def attend(j, step, count):
        h, p = unit_of(j, step)
        pl.when(j + 2 < count)(lambda: prob_copy(j + 2, step).start())
        prob_copy(j, step).wait()
        tile = pl.multiple_of(128 * h, 128)
        left = left_half((LEN, 128))
        at = [[pl.ds(pl.multiple_of(D * i + tile + 64 * side, 64), 64) for i in range(4)] for side in range(2)]
        parts = []
        for q in range(2):
            rows = pl.ds(pl.multiple_of((p + q) * LEN, LEN), LEN)
            context = branch[rows, pl.ds(tile, 128)]
            all_values = up[pl.ds(pl.multiple_of(2 * D + tile, 128), 128), rows]
            for side in range(2):
                mine = left if side == 0 else jnp.logical_not(left)
                d_prob = product(jnp.where(mine, context, jnp.zeros_like(context)), all_values)
                low = prob[j % 3, q, side]
                share = low.astype(jnp.float32)
                moved = share * d_prob
                d_scores = (moved - share * jnp.sum(moved, axis=1, keepdims=True)).astype(jnp.bfloat16)
                d_values = product(turned[at[side][3], rows], low)
                d_query = product_right(up[at[side][1], rows], d_scores) * HEAD_DIM**-0.5
                d_keys = product(up[at[side][0], rows], d_scores) * HEAD_DIM**-0.5
                parts.append((side, rows, [item.astype(jnp.bfloat16) for item in (d_query, d_keys, d_values)]))
        for side, rows, items in parts:
            for i in range(3):
                up[at[side][i], rows] = items[i]

    def put_tiles(tiles, at):
        for i in range(3):
            for one, two in tiles:
                right = jnp.concatenate(
                    [up[D * i + 128 * one : D * i + 128 * (one + 1), :], up[D * i + 128 * two : D * i + 128 * (two + 1), :]]
                )
                grad = product_right(turned[0:D, :], right)
                if direct:
                    for d in range(GRID[0]):
                        block = grad[BLOCK * d : BLOCK * (d + 1)]
                        if len(tiles) == 2:
                            take_main(part, d, one // 3, at + BLOCK * i, block[:, :128], block[:, 128:])
                        else:
                            take_rest(part, d, 0, at + BLOCK // 2 * i, block[:, :128])
                            take_rest(part, d, 1, at + BLOCK // 2 * i, block[:, 128:])
                else:
                    for k, tile in enumerate((one, two)):
                        stage[:, :128] = grad[:, 128 * k : 128 * (k + 1)]
                        put(stage.at[:, pl.ds(0, 128)], gsquare_ref.at[pl.ds(D * i, D), pl.ds(128 * tile, 128)])

    def put_vectors():
        ones = jnp.ones((8, rows_all), jnp.bfloat16)
        sums[0:1, :D] = product_right(ones, up[0:D, :])[0:1]
        sums[1:2, :D] = product_right(ones, up[2 * D : 3 * D, :])[0:1]
        if direct:
            lane = lax.broadcasted_iota(jnp.int32, (1, 128), 1)
            value = jnp.zeros((1, 128), jnp.float32)
            for p in range(packs):
                value = jnp.where(lane == narrow * packs + p, value_ref[p : p + 1, :], value)
            high = value.astype(jnp.bfloat16).astype(jnp.float32)
            zeros = jnp.zeros((3, 128), jnp.float32)
            for d in range(GRID[0]):
                at, shift = divmod(BLOCK * d, 128)
                wide = sums[:, 128 * at : 128 * at + 256]
                wide = pltpu.roll(wide, 256 - shift, 1) if shift else wide
                mine = lax.broadcasted_iota(jnp.int32, (8, 128), 1) < BLOCK
                own = jnp.where(dp == d, 1.0, 0.0)
                tile = jnp.concatenate(
                    [jnp.where(mine, wide[:8, :128], 0.0), bup[3 * d : 3 * d + 3, :], high * own, (value - high) * own, zeros]
                )
                for n in range(GRID[1]):
                    part[d // 2, d % 2, n // 2, n % 2, 0:16, :] = tile.astype(jnp.bfloat16)

    def widen_back(r):
        rows = pl.ds(pl.multiple_of(r * LEN, LEN), LEN)
        value = product(square[:, :D], up[:D, rows])
        for i in (1, 2):
            value = value + product(square[:, D * i : D * (i + 1)], up[D * i : D * (i + 1), rows])
        norm[rows, :] = flow[rows, :] + jnp.transpose(value)

    after = split_order(BACKWARD_ORDER, "sc321", "DNUBOTMXRW")

    def tick(mark, index=None):
        if not direct:
            return
        for name, pieces in after.items():
            if name[:1] == mark and pieces:
                if index is None:
                    for piece in pieces:
                        g.do(*piece)
                else:

                    @pl.when(index == int(name[1:]))
                    def _():
                        for piece in pieces:
                            g.do(*piece)

    def repeat(mark, first, last, body):
        def step(i, carry):
            body(i)
            tick(mark, i)
            return carry

        lax.fori_loop(first, last, step, 0)

    def up_pair(t):
        put_up(t, 0)
        put_up(t, 1)

    def down_three(i):
        for j in range(3):
            narrow_down(3 * i + j)

    groups = []
    for name in [name for name in after if name]:
        if groups and groups[-1][0] == name[0]:
            groups[-1][1].append(int(name[1:]))
        else:
            groups.append((name[0], [int(name[1:])]))
    for mark, span in groups:
        first, last = span[0], span[-1] + 1
        if mark == "D":
            need("turned branch", "act")
            load("branch", (branch_in, branch))
            load("down", (down_in, square))
            load("slope", (slope_in, slope))
            load("up", *[(up_in.at[:, pl.ds(rows_all * i, rows_all)], up.at[pl.ds(D * i, D), :]) for i in range(3)])
            load("flow", (second_in, flow))
            load("norm", (norm_in, norm))
            load("recip", (recip_in, recip))
            repeat("D", first, last, put_down)
            load("turned", (turned_in, turned.at[pl.ds(0, 3 * D), :]))
        elif mark == "N":
            need("branch", "down", "slope")
            repeat("N", first, last, down_three)
            load("square", (square_in, square))
        elif mark == "U":
            need("turned")
            repeat("U", first, last, up_pair)
        elif mark == "B":
            need("up", "flow", "norm", "recip")
            repeat("B", first, last, norm_back)
            load("qkv", (qkv_in, up))
            for j in range(2):
                prob_copy(j, "T").start()
        elif mark == "O":
            need("turned", "square")
            put_out()
            context_back()
            tick("O", None)
        elif mark == "T":
            need("qkv")
            repeat("T", first, last, lambda j: attend(j, "T", 2 * packs))
            for j in range(2):
                prob_copy(j, "X").start()
        elif mark == "M":
            put_tiles(((0, 2), (3, 5)), MAIN)
            tick("M")
        elif mark == "X":
            repeat("X", first, last, lambda j: attend(j, "X", packs))
        elif mark == "R":
            put_tiles(((1, 4),), REST)
            put_vectors()
            tick("R")
        elif mark == "W":
            repeat("W", first, last, widen_back)
            result = pltpu.make_async_copy(norm, grad_in_out, out_sem.at[1])
            result.start()
    if direct:
        for k in range(len(SCATTER_ROWS)):
            g.drain(k)
    else:
        gvec_ref[...] = sums[...]
        gbup_ref[...] = bup[...]
    result.wait()


def backward_step(direct, operands, dp, narrow):
    rows = operands[1].shape[0]
    vmem = pl.BlockSpec(memory_space=pltpu.VMEM)
    anywhere = pl.BlockSpec(memory_space=pl.ANY)
    full = lambda *shape: jax.ShapeDtypeStruct(shape, jnp.float32)
    room = lambda *shape: pltpu.VMEM(shape, jnp.bfloat16)
    wide = lambda *shape: pltpu.VMEM(shape, jnp.float32)
    if direct:
        outs, places = [full(TOTAL, 128)], [vmem]
        depth = dp // 2
        count = len(SCATTER_ROWS)
        extra = [
            room(depth, 2, 2, 2, TOTAL, 128), room(depth, 2, 2, TOTAL, 128), room(depth, 2, TOTAL, 128),
            room(depth, TOTAL, 128), room(depth - 1, TOTAL, 128),
            pltpu.SemaphoreType.DMA((count, 12)), pltpu.SemaphoreType.DMA((count, 12)),
        ]
    else:
        outs = [full(FF, D), full(D, FF), full(D, FF), full(16, 896), full(32, 128)]
        places = [anywhere] * 3 + [vmem] * 2
        extra = [wide(D, D)]
    return pl.pallas_call(
        functools.partial(backward_kernel, direct),
        name="backward",
        out_shape=(full(rows, D), *outs),
        in_specs=[anywhere] * 5 + [vmem] + [anywhere] * 8 + [vmem] * 2,
        out_specs=(anywhere, *places),
        scratch_shapes=[
            room(FF, rows), room(rows, FF), room(D, FF), room(3 * D, rows), wide(rows, D), wide(rows, D), wide(rows, 128),
            room(rows, D), room(D, rows), room(3, 2, 2, LEN, LEN), wide(16, 896), wide(32, 128),
            pltpu.SemaphoreType.DMA((20,)), pltpu.SemaphoreType.DMA((3,)), pltpu.SemaphoreType.DMA((2,)),
            *extra,
        ],
        compiler_params=pltpu.CompilerParams(
            vmem_limit_bytes=VMEM_LIMIT, **(dict(collective_id=1, has_side_effects=True) if direct else {})
        ),
    )(*operands)


def collect_kernel(packs_all, total, group_in, grad_in, *refs):
    (group_out, loss, grad_out, gq, gqb, gk, gv, gvb, go, gob, gfg, gfs, gup, gupb, gdown, gdownb, gsg, gss, group, grad, in_sem, out_sem) = refs
    parts = [(group_in, group, group_out, i) for i in range(group.shape[0] // LEN)]
    parts += [(grad_in, grad, grad_out, i) for i in range(grad.shape[0] // LEN)]
    ins, outs = [], []
    for k, (src, via, dst, i) in enumerate(parts):
        rows = pl.ds(LEN * i, LEN)
        ins.append(pltpu.make_async_copy(src.at[rows, :], via.at[rows, :], in_sem.at[k]))
        outs.append(pltpu.make_async_copy(via.at[rows, :], dst.at[rows, :], out_sem.at[k]))
        ins[-1].start(priority=k % 2)
    odd = lax.rem(lax.axis_index("narrow"), 2) == 1
    for one, two in zip(ins, outs):
        one.wait()
        two.start(priority=1)
    for i, ref in enumerate((gqb, gvb, gob, gfg, gfs, gdownb, gsg, gss)):
        ref[...] = total[i : i + 1, :BLOCK]
    gupb[...] = total[8:11, :]
    loss[...] = (total[11:12, :] + total[12:13, :])[:, :packs_all]
    for t in range(6):
        gup[:, 128 * t : 128 * (t + 1)] = total[UP + BLOCK * t : UP + BLOCK * (t + 1), :]
    for ref, main, rest in (
        (gq, MAIN, REST), (gk, MAIN + BLOCK, REST + BLOCK // 2), (gv, MAIN + 2 * BLOCK, REST + BLOCK), (go, OUT, OUT + BLOCK),
    ):
        block = unpack_block(total[main : main + BLOCK, :], total[rest : rest + BLOCK // 2, :], odd)
        ref[...] = block[:, :192]
    for t in range(3):
        gdown[:, 128 * t : 128 * (t + 1)] = total[DOWN + SIDE * t : DOWN + SIDE * (t + 1), :]
    for copy in outs:
        copy.wait()


def collect_step(total, group, grad_inputs, dp, narrow):
    packs_all = group.shape[0] // LEN
    vmem = pl.BlockSpec(memory_space=pltpu.VMEM)
    anywhere = pl.BlockSpec(memory_space=pl.ANY)
    full = lambda *shape: jax.ShapeDtypeStruct(shape, jnp.float32)
    square, vector = full(D // dp, D // narrow), full(1, D // dp)
    count = (group.shape[0] + grad_inputs.shape[0]) // LEN
    out = pl.pallas_call(
        functools.partial(collect_kernel, packs_all),
        name="collect",
        out_shape=(
            jax.ShapeDtypeStruct(group.shape, group.dtype), full(1, packs_all), full(*grad_inputs.shape),
            square, vector, square, square, vector, square, vector, vector, vector,
            full(D // dp, FF // narrow), full(FF // dp // 128, 128), full(D // narrow, FF // dp), vector, vector, vector,
        ),
        in_specs=[vmem, anywhere, anywhere],
        out_specs=(anywhere, vmem, anywhere) + (vmem,) * 15,
        scratch_shapes=[
            pltpu.VMEM(group.shape, group.dtype), pltpu.VMEM(grad_inputs.shape, jnp.float32),
            pltpu.SemaphoreType.DMA((count,)), pltpu.SemaphoreType.DMA((count,)),
        ],
        compiler_params=pltpu.CompilerParams(vmem_limit_bytes=VMEM_LIMIT),
    )(total, group, grad_inputs)
    out = [item.reshape(-1) if item.shape[0] in (1, 3) else item for item in out]
    out[14] = out[14].T
    return tuple(out)


def per_device(
    inputs,
    segments,
    row_kind,
    query_weight,
    query_bias,
    key_weight,
    value_weight,
    value_bias,
    output_weight,
    output_bias,
    first_gain,
    first_shift,
    up_weight,
    up_bias,
    down_weight,
    down_bias,
    second_gain,
    second_shift,
    out_cotangent,
    loss_cotangent,
):
    row_count = inputs.shape[0]
    matrices = (query_weight, key_weight, value_weight, output_weight, up_weight, down_weight)
    vectors = (
        query_bias,
        value_bias,
        output_bias,
        first_gain,
        first_shift,
        down_bias,
        second_gain,
        second_shift,
        up_bias,
    )
    dp, narrow = lax.axis_size("dp"), lax.axis_size("narrow")
    direct = (dp, narrow, row_count) == (*GRID, 4 * LEN)
    if direct:
        weights = (*matrices[:5], down_weight.T, *[item.reshape(1, -1) for item in vectors[:8]], up_bias.reshape(-1, 128))
    else:
        weights = fetch_weights(matrices, vectors)
    (square, up, down, vecs, qkv, prob, turned, norm_first, recip_first, active, slope, output_low, norm_second,
     recip_second) = forward_step(direct, weights, inputs, segments, dp, narrow)
    group_out = lax.all_gather(output_low, "narrow", axis=0, tiled=True)
    partial_value, d_second, d_branch, branch_turned, sums_second = transport_step(
        output_low, segments, row_kind, loss_cotangent, out_cotangent, norm_second, recip_second, vecs
    )
    grad_inputs, *grads = backward_step(
        direct,
        (active, slope, d_branch, branch_turned, d_second, sums_second, turned.reshape(3 * D, row_count), norm_first, recip_first, qkv, prob, square,
         up.reshape(D, FF), down, vecs, partial_value),
        dp,
        narrow,
    )
    if direct:
        return collect_step(grads[0], group_out, grad_inputs, dp, narrow)
    transport_loss = lax.all_gather(partial_value[:, 0], "narrow", axis=0, tiled=True)
    squares, g_up, g_down, small, tiles = grads
    mats, vecs = reduce_grads([*squares.reshape(4, D, D), g_up, g_down.T], [*small[:8, :D], tiles[:24].reshape(FF)])
    return (
        group_out,
        transport_loss,
        grad_inputs,
        mats[0],
        vecs[0],
        mats[1],
        mats[2],
        vecs[1],
        mats[3],
        vecs[2],
        vecs[3],
        vecs[4],
        mats[4],
        vecs[8],
        mats[5],
        vecs[5],
        vecs[6],
        vecs[7],
    )


def solution(mesh):
    return jax.shard_map(
        per_device,
        mesh=mesh,
        in_specs=(
            P(("dp", "narrow"), None),
            P("dp", None),
            P("dp", None),
            P("dp", "narrow"),
            P("dp"),
            P("dp", "narrow"),
            P("dp", "narrow"),
            P("dp"),
            P("dp", "narrow"),
            P("dp"),
            P("dp"),
            P("dp"),
            P("dp", "narrow"),
            P("dp"),
            P("dp", "narrow"),
            P("dp"),
            P("dp"),
            P("dp"),
            P(("dp", "narrow"), None),
            P("dp"),
        ),
        out_specs=(
            P("dp", None),
            P("dp"),
            P(("dp", "narrow"), None),
            P("dp", "narrow"),
            P("dp"),
            P("dp", "narrow"),
            P("dp", "narrow"),
            P("dp"),
            P("dp", "narrow"),
            P("dp"),
            P("dp"),
            P("dp"),
            P("dp", "narrow"),
            P("dp"),
            P("dp", "narrow"),
            P("dp"),
            P("dp"),
            P("dp"),
        ),
        check_vma=False,
    )
```
